32 devices in a mesh: dp: 8 (over y, x, core), fsdp: 4 (over z).
Axes of the slice: x: 2, y: 2, z: 4, core: 2. Of those that a mesh axis runs over, the one named last changes fastest.
Arguments:
- bytes_in: bfloat16 [24, 2048, 768], P('dp', 'fsdp'), may hold values from -6 to 6
- latents_in: bfloat16 [24, 256, 1280], P('dp', 'fsdp'), may hold values from -6 to 6
- cotangent: bfloat16 [24, 256, 1280], P('dp', 'fsdp'), may hold values from -6 to 6
- byte_segments: int32 [24, 2048], P('dp'), may hold values from 0 to 3, as said below
- latent_segments: int32 [24, 256], P('dp', 'fsdp'), may hold values from 0 to 3, as said below
- w_query: bfloat16 [1280, 1280], P(('dp', 'fsdp')), may hold values from -0.15625 to 0.15625
- w_key: bfloat16 [768, 1280], P(('dp', 'fsdp')), may hold values from -0.21875 to 0.21875
- w_value: bfloat16 [768, 1280], P(('dp', 'fsdp')), may hold values from -0.21875 to 0.21875
- w_out: bfloat16 [1280, 1280], P(('dp', 'fsdp')), may hold values from -2.5 to 2.5
- w_mlp_in: bfloat16 [1280, 1280], P(('dp', 'fsdp')), may hold values from -0.15625 to 0.15625
- w_mlp_out: bfloat16 [1280, 1280], P(('dp', 'fsdp')), may hold values from -0.15625 to 0.15625
- gain_latent: bfloat16 [1280], P(('dp', 'fsdp')), may hold values from 0.099609375 to 1.8984375
- gain_byte: bfloat16 [768], P(('dp', 'fsdp')), may hold values from 0.099609375 to 1.8984375
- gain_mlp: bfloat16 [1280], P(('dp', 'fsdp')), may hold values from 0.099609375 to 1.8984375
Outputs:
- new_latents: bfloat16 [24, 256, 1280], P('dp', 'fsdp')
- grad_latents: float32 [24, 256, 1280], P('dp', 'fsdp')
- grad_bytes: float32 [24, 2048, 768], P('dp', 'fsdp')
- grad_w_query: float32 [1280, 1280], P(('dp', 'fsdp'))
- grad_w_key: float32 [768, 1280], P(('dp', 'fsdp'))
- grad_w_value: float32 [768, 1280], P(('dp', 'fsdp'))
- grad_w_out: float32 [1280, 1280], P(('dp', 'fsdp'))
- grad_w_mlp_in: float32 [1280, 1280], P(('dp', 'fsdp'))
- grad_w_mlp_out: float32 [1280, 1280], P(('dp', 'fsdp'))
- grad_gain_latent: float32 [1280], P(('dp', 'fsdp'))
- grad_gain_byte: float32 [768], P(('dp', 'fsdp'))
- grad_gain_mlp: float32 [1280], P(('dp', 'fsdp'))
The draws below stay inside these ranges and needn't reach their ends.
Inputs may be any that keep to these rules, and one draw needn't show every extreme that they name: `byte_segments`: in each row the bytes form 4 documents laid end to end: the ids never fall along a row, and every id 0 to 3 holds one or more bytes. `latent_segments`: in each row exactly 64 latents belong to each document.
All inputs are finite; a program needn't handle non-finite values.
Results may differ from the reference program's by a relative error of at most 0.014.
Values may be sent and summed in bfloat16 or wider, within the bound.
No kernel may reach another device: no remote copies, remote signals or barrier semaphores. Data moves between devices by JAX's collectives and lax.ppermute only.
A program may use at most 256 MiB of HBM per device.

```python
import math
import jax
import jax.numpy as jnp
from jax import lax

D_BYTE = 768
LAT = 256
HEADS = 8
HEAD_DIM = 160
SEQ = 2048
NDOC = 4
D_LAT = 1280
BATCH = 24
N_FSDP = 4


def draw_byte_segments(key, part):
    key = jax.random.fold_in(key, 11)
    row_keys = jax.random.split(key, BATCH)

    def one_row(row_key):
        order = jax.random.permutation(row_key, SEQ - 1)
        cuts = jnp.sort(order[:NDOC - 1]) + 1
        positions = jnp.arange(SEQ)
        return jnp.sum((positions[:, None] >= cuts[None, :]).astype(jnp.int32), axis=1)
    return jax.vmap(one_row)(row_keys).astype(jnp.int32)


def draw_latent_segments(key, part):
    key = jax.random.fold_in(key, 23)
    row_keys = jax.random.split(key, BATCH)

    def one_row(row_key):
        return (jax.random.permutation(row_key, LAT) % NDOC).astype(jnp.int32)
    return jax.vmap(one_row)(row_keys).astype(jnp.int32)


def steps_of(own_key, dims, cuts, least, largest):
    factor_of, own = 1.0, jax.random.fold_in(own_key, 6)
    for dim, shards_of in cuts:
        heights = jnp.exp(jax.random.uniform(jax.random.fold_in(own, dim), (shards_of,), jnp.float32, least / len(cuts), largest / len(cuts)))
        factor_of = factor_of * jnp.repeat(heights, dims[dim] // shards_of).reshape([-1 if axis == dim else 1 for axis in range(len(dims))])
    return factor_of


def noise(own_key, extent, scale, most, cuts=(), dtype=jnp.bfloat16):
    values = jax.random.normal(own_key, extent, jnp.float32) * scale
    if len(cuts) > 0:
        values = steps_of(own_key, extent, cuts, -0.22, 0.18) * values
    return jnp.clip(values, min=-most, max=most).astype(dtype)


def setup_inputs(seed: int = 0) -> dict:
    arg_keys = jax.random.split(jax.random.key(seed), 15)
    bytes_in = noise(arg_keys[0], (BATCH, SEQ, D_BYTE), 1.0, 6.0, ((0, 8), (1, 4)))
    latents_in = noise(arg_keys[1], (BATCH, LAT, D_LAT), 1.0, 6.0, ((0, 8), (1, 4)))
    cotangent = noise(arg_keys[2], (BATCH, LAT, D_LAT), 1.0, 6.0, ((0, 8), (1, 4)))
    byte_segments = draw_byte_segments(jax.random.fold_in(arg_keys[14], 71), 0)
    latent_segments = draw_latent_segments(jax.random.fold_in(arg_keys[14], 71), 0)
    w_query = noise(arg_keys[5], (D_LAT, D_LAT), D_LAT ** -0.5, 0.15625, ((0, 32),))
    w_key = noise(arg_keys[6], (D_BYTE, D_LAT), D_BYTE ** -0.5, 0.21875, ((0, 32),))
    w_value = noise(arg_keys[7], (D_BYTE, D_LAT), D_BYTE ** -0.5, 0.21875, ((0, 32),))
    w_out = noise(arg_keys[8], (D_LAT, D_LAT), (max(D_LAT // 256, 1)) ** -0.5, 2.5, ((0, 32),))
    w_mlp_in = noise(arg_keys[9], (D_LAT, D_LAT), D_LAT ** -0.5, 0.15625, ((0, 32),))
    w_mlp_out = noise(arg_keys[10], (D_LAT, D_LAT), D_LAT ** -0.5, 0.15625, ((0, 32),))
    gain_latent = jnp.clip(1.0 + 0.18 * jax.random.normal(arg_keys[11], (D_LAT,), jnp.float32), 0.099609375, 1.8984375).astype(jnp.bfloat16)
    gain_byte = jnp.clip(1.0 + 0.18 * jax.random.normal(arg_keys[12], (D_BYTE,), jnp.float32), 0.099609375, 1.8984375).astype(jnp.bfloat16)
    gain_mlp = jnp.clip(1.0 + 0.18 * jax.random.normal(arg_keys[13], (D_LAT,), jnp.float32), 0.099609375, 1.8984375).astype(jnp.bfloat16)
    return {"bytes_in": bytes_in, "latents_in": latents_in, "cotangent": cotangent, "byte_segments": byte_segments, "latent_segments": latent_segments, "w_query": w_query, "w_key": w_key, "w_value": w_value, "w_out": w_out, "w_mlp_in": w_mlp_in, "w_mlp_out": w_mlp_out, "gain_latent": gain_latent, "gain_byte": gain_byte, "gain_mlp": gain_mlp}


@jax.custom_vjp
def low(v):
    return lax.optimization_barrier(v.astype(jnp.bfloat16)).astype(jnp.float32)

@jax.custom_vjp
def low_back(v):
    return v

def low_keep(v):
    return (low(v), None)

def low_pass(kept, grad):
    return (grad,)

def back_keep(v):
    return (v, None)

def back_low(kept, grad):
    return (low(grad),)
low.defvjp(low_keep, low_pass)
low_back.defvjp(back_keep, back_low)
EPSILON = 1e-05
NEG_FILL = -1e+30

def normalize(values, gain_vec):
    centered = values - lax.optimization_barrier(jnp.mean(values, axis=-1, keepdims=True))
    return centered * lax.rsqrt(lax.optimization_barrier(jnp.mean(centered * centered, axis=-1, keepdims=True)) + EPSILON) * gain_vec

def exact(formula, factor_one, factor_two):
    return jnp.einsum(formula, factor_one, factor_two, precision=lax.Precision.HIGHEST)

def forward(latent_row, byte_row, latent_ids, byte_ids, weights):
    query_mat, key_mat, value_mat, out_mat, inner_mat, outer_mat, latent_gain, byte_gain, mlp_gain = weights
    latent_normed = low(normalize(latent_row, latent_gain))
    byte_normed = low(normalize(byte_row, byte_gain))
    queries = low_back(low(exact('ld,de->le', latent_normed, query_mat)))
    keys = low(exact('sd,de->se', byte_normed, key_mat))
    values = low(exact('sd,de->se', byte_normed, value_mat))
    head_query = queries.reshape(LAT, HEADS, HEAD_DIM)
    group = LAT // N_FSDP
    pieces = []
    for index in range(N_FSDP):
        group_query = head_query[index * group:(index + 1) * group]
        group_key = low_back(keys).reshape(SEQ, HEADS, HEAD_DIM)
        group_value = low_back(values).reshape(SEQ, HEADS, HEAD_DIM)
        scores = low_back(exact('lhc,shc->hls', group_query, group_key) / math.sqrt(HEAD_DIM))
        group_ids = latent_ids[index * group:(index + 1) * group]
        allowed = (group_ids[:, None] == byte_ids[None, :])[None]
        masked = jnp.where(allowed, scores, NEG_FILL)
        exponent = jnp.exp(masked - lax.optimization_barrier(jnp.max(masked, axis=-1, keepdims=True)))
        attn_probs = exponent / lax.optimization_barrier(jnp.sum(exponent, axis=-1, keepdims=True))
        probs_low = low(attn_probs)
        pieces.append(exact('hls,shc->lhc', probs_low, group_value).reshape(group, D_LAT))
    attended = low_back(low(jnp.concatenate(pieces, axis=0)))
    mixed_sum = latent_row + low_back(exact('le,ef->lf', attended, out_mat))
    mlp_normed = low(normalize(mixed_sum, mlp_gain))
    hidden = low_back(exact('le,ef->lf', mlp_normed, inner_mat))
    activated = low(jax.nn.gelu(hidden))
    return mixed_sum + exact('le,ef->lf', activated, outer_mat)

def reference(bytes_in, latents_in, cotangent, byte_segments, latent_segments, w_query, w_key, w_value, w_out, w_mlp_in, w_mlp_out, gain_latent, gain_byte, gain_mlp):
    weights = (w_query.astype(jnp.float32), w_key.astype(jnp.float32), w_value.astype(jnp.float32), w_out.astype(jnp.float32), w_mlp_in.astype(jnp.float32), w_mlp_out.astype(jnp.float32), gain_latent.astype(jnp.float32), gain_byte.astype(jnp.float32), gain_mlp.astype(jnp.float32))

    def one_row(totals, row_data):
        byte_row, latent_row, cot_row, byte_ids, latent_ids = row_data

        def local_forward(latent_value, byte_value, weight_value):
            return forward(latent_value, byte_value, latent_ids, byte_ids, weight_value)
        result, pullback = jax.vjp(local_forward, latent_row.astype(jnp.float32), byte_row.astype(jnp.float32), weights)
        grad_latent, grad_byte, grad_weights = pullback(cot_row.astype(jnp.float32))
        totals = jax.tree.map(lambda total, extra: total + extra, totals, grad_weights)
        return (totals, (result.astype(jnp.bfloat16), grad_latent, grad_byte))
    zero_totals = jax.tree.map(jnp.zeros_like, weights)
    totals, outputs = lax.scan(one_row, zero_totals, (bytes_in, latents_in, cotangent, byte_segments, latent_segments))
    return (outputs[0], outputs[1], outputs[2], totals[0], totals[1], totals[2], totals[3], totals[4], totals[5], totals[6], totals[7], totals[8])
```

```python
import functools
import math

import jax
import jax.numpy as jnp
from jax import lax
from jax.experimental import pallas as pl
from jax.experimental.pallas import tpu as pltpu
from jax.sharding import PartitionSpec as P

HEADS = 8
HEAD_DIM = 160
EPSILON = 1e-05
NEG_FILL = -1e30
LANES = 128
WINDOW = 256
BF = jnp.bfloat16
F32 = jnp.float32
VMEM_LIMIT = 58 * 1024 * 1024


def head_window(head):
    start = head * HEAD_DIM // LANES * LANES
    return start, head * HEAD_DIM - start


def head_lanes(head):
    _, shift = head_window(head)
    lane = lax.broadcasted_iota(jnp.int32, (1, WINDOW), 1)
    return (lane >= shift) & (lane < shift + HEAD_DIM)


def dot(a, b, dims=((1,), (0,))):
    return lax.dot_general(a, b, (dims, ((), ())), preferred_element_type=F32)


def standardize(values):
    centered = values - jnp.mean(values, axis=-1, keepdims=True)
    scale = lax.rsqrt(jnp.mean(centered * centered, axis=-1, keepdims=True) + EPSILON)
    return centered * scale, scale


def norm_pull(upstream, gain, xhat, scale):
    scaled = upstream * gain
    return scale * (
        scaled
        - jnp.mean(scaled, axis=-1, keepdims=True)
        - xhat * jnp.mean(scaled * xhat, axis=-1, keepdims=True)
    )


def split_three(values):
    first = values.astype(BF).astype(F32)
    rest = values - first
    second = rest.astype(BF).astype(F32)
    return first, second, rest - second


def gelu(values):
    inner = math.sqrt(2 / math.pi) * (values + 0.044715 * values * values * values)
    return 0.5 * values * (1.0 + jnp.tanh(inner))


def gelu_slope(values):
    square = values * values
    tanh = jnp.tanh(math.sqrt(2 / math.pi) * (values + 0.044715 * square * values))
    slope = math.sqrt(2 / math.pi) * (1.0 + 3 * 0.044715 * square)
    return 0.5 * (1.0 + tanh) + 0.5 * values * (1.0 - tanh * tanh) * slope


def piece_copies(pieces, flat_refs, first, rows, target, me, sems, base):
    copies = []
    at = 0
    for distance, parts in pieces:
        owner = jnp.bitwise_xor(me, distance)
        for low, high in parts:
            ref = flat_refs[at]
            at += 1
            start, stop = max(low, first), min(high, first + rows)
            if start < stop:
                place = pl.multiple_of(owner * rows + (start - first), 16)
                copies.append(
                    pltpu.make_async_copy(
                        ref.at[pl.ds(start - low, stop - start), :],
                        target.at[pl.ds(place, stop - start), :],
                        sems.at[base + len(copies)],
                    )
                )
    return copies


def params(grid_rank):
    return pltpu.CompilerParams(
        dimension_semantics=("arbitrary",) * grid_rank, vmem_limit_bytes=VMEM_LIMIT
    )


def whole_spec():
    return pl.BlockSpec(memory_space=pltpu.VMEM)


def any_spec():
    return pl.BlockSpec(memory_space=pl.ANY)


def key_value_call(me, bytes_flat, gain, pieces, flat, key_rows, key_at, value_at, rows):
    tokens, width = bytes_flat.shape
    block = tokens // rows
    lat = flat[0].shape[1]
    count = len(flat)

    def kernel(me_ref, x_ref, gain_ref, *refs):
        piece_refs = refs[:count]
        normed_t_ref, key_ref, value_ref, wk, wv, sems = refs[count:]

        def copies():
            one = piece_copies(pieces, piece_refs, key_at, key_rows, wk, me_ref[0], sems, 0)
            two = piece_copies(
                pieces, piece_refs, value_at, key_rows, wv, me_ref[0], sems, len(one)
            )
            return one + two

        @pl.when(pl.program_id(0) == 0)
        def _():
            for copy in copies():
                copy.start()

        xhat, _ = standardize(x_ref[...].astype(F32))
        normed = (xhat * gain_ref[...]).astype(BF)
        normed_t_ref[...] = jnp.transpose(normed, (1, 0))

        @pl.when(pl.program_id(0) == 0)
        def _():
            for copy in copies():
                copy.wait()

        key_ref[...] = dot(normed, wk[...]).astype(BF)
        value_ref[...] = dot(normed, wv[...]).astype(BF)

    row_block = lambda i, m: (i, 0)
    return pl.pallas_call(
        kernel,
        grid_spec=pltpu.PrefetchScalarGridSpec(
            num_scalar_prefetch=1,
            grid=(rows,),
            in_specs=[
                pl.BlockSpec((block, width), row_block),
                pl.BlockSpec((1, width), lambda i, m: (0, 0)),
            ]
            + [any_spec()] * count,
            out_specs=[
                pl.BlockSpec((width, block), lambda i, m: (0, i)),
                pl.BlockSpec((block, lat), row_block),
                pl.BlockSpec((block, lat), row_block),
            ],
            scratch_shapes=[
                pltpu.VMEM((width, lat), BF),
                pltpu.VMEM((width, lat), BF),
                pltpu.SemaphoreType.DMA((4 * count,)),
            ],
        ),
        out_shape=[
            jax.ShapeDtypeStruct((width, tokens), BF),
            jax.ShapeDtypeStruct((tokens, lat), BF),
            jax.ShapeDtypeStruct((tokens, lat), BF),
        ],
        compiler_params=params(1),
        cost_estimate=pl.CostEstimate(
            flops=4 * tokens * width * lat,
            bytes_accessed=2 * (2 * tokens * width + 2 * tokens * lat + 2 * width * lat),
            transcendentals=0,
        ),
        name="keys_values",
    )(me, bytes_flat, gain, *flat)


def attend_call(
    me, latent_parts, gain, latent_ids, byte_ids, keys, values, pieces, flat, query_rows, query_at, rows
):
    groups = len(latent_parts)
    tokens, lat = keys.shape
    block = tokens // rows
    group = latent_ids.shape[1] // groups
    latents = groups * group
    count = len(flat)
    score_scale = 1.0 / math.sqrt(HEAD_DIM)

    def kernel(me_ref, *refs):
        part_refs = refs[:groups]
        gain_ref, lid_ref, bid_ref, key_ref, value_ref = refs[groups : groups + 5]
        piece_refs = refs[groups + 5 : groups + 5 + count]
        rest = refs[groups + 5 + count :]
        normed_t_ref, query_ref = rest[:2]
        out_refs = rest[2 : 2 + groups]
        wq, acc, sems = rest[2 + groups :]

        def copies():
            return piece_copies(pieces, piece_refs, query_at, query_rows, wq, me_ref[0], sems, 0)

        @pl.when(pl.program_id(0) == 0)
        def _():
            for copy in copies():
                copy.start()

        x = jnp.concatenate([ref[...].astype(F32) for ref in part_refs], axis=0)
        xhat, _ = standardize(x)
        normed = (xhat * gain_ref[...]).astype(BF)
        normed_t_ref[...] = jnp.transpose(normed, (1, 0))

        @pl.when(pl.program_id(0) == 0)
        def _():
            for copy in copies():
                copy.wait()

        query_ref[...] = dot(normed, wq[...]).astype(BF)
        allowed = lid_ref[0] == bid_ref[0]
        lane = lax.broadcasted_iota(jnp.int32, (latents, LANES), 1)
        stats = jnp.zeros((latents, LANES), F32)
        for head in range(HEADS):
            at, _ = head_window(head)
            mask = head_lanes(head)
            window = slice(at, at + WINDOW)
            query = jnp.where(mask, query_ref[:, window], jnp.zeros((), BF))
            scores = dot(query, key_ref[:, window], ((1,), (1,))) * score_scale
            scores = jnp.where(allowed, scores, NEG_FILL)
            top = jnp.max(scores, axis=-1, keepdims=True)
            exponent = jnp.exp(scores - top)
            total = jnp.sum(exponent, axis=-1, keepdims=True)
            found = dot(exponent.astype(BF), value_ref[:, window]) / total
            if head == 0:
                acc[:, window] = found
            else:
                acc[:, window] = jnp.where(mask, found, acc[:, window])
            log_total = jnp.where(top > -1e29, top + jnp.log(total), NEG_FILL)
            for index, term in enumerate(split_three(log_total)):
                stats = jnp.where(lane == index * HEADS + head, term, stats)
        for index, ref in enumerate(out_refs):
            chunk = slice(index * group, (index + 1) * group)
            ref[:, :lat] = acc[chunk, :].astype(BF)
            ref[:, lat:] = stats[chunk, :].astype(BF)

    row_block = lambda i, m: (i, 0)
    return pl.pallas_call(
        kernel,
        grid_spec=pltpu.PrefetchScalarGridSpec(
            num_scalar_prefetch=1,
            grid=(rows,),
            in_specs=[pl.BlockSpec((group, lat), row_block)] * groups
            + [
                pl.BlockSpec((1, lat), lambda i, m: (0, 0)),
                pl.BlockSpec((1, latents, 1), lambda i, m: (i, 0, 0)),
                pl.BlockSpec((1, 1, block), lambda i, m: (i, 0, 0)),
                pl.BlockSpec((block, lat), row_block),
                pl.BlockSpec((block, lat), row_block),
            ]
            + [any_spec()] * count,
            out_specs=[
                pl.BlockSpec((lat, latents), lambda i, m: (0, i)),
                pl.BlockSpec((latents, lat), row_block),
            ]
            + [pl.BlockSpec((group, lat + LANES), row_block)] * groups,
            scratch_shapes=[
                pltpu.VMEM((lat, lat), BF),
                pltpu.VMEM((latents, lat), F32),
                pltpu.SemaphoreType.DMA((2 * count,)),
            ],
        ),
        out_shape=[
            jax.ShapeDtypeStruct((lat, rows * latents), BF),
            jax.ShapeDtypeStruct((rows * latents, lat), BF),
        ]
        + [jax.ShapeDtypeStruct((rows * group, lat + LANES), BF)] * groups,
        compiler_params=params(1),
        cost_estimate=pl.CostEstimate(
            flops=2 * rows * latents * lat * lat
            + 4 * rows * HEADS * latents * block * WINDOW,
            bytes_accessed=2 * (4 * tokens * lat + lat * lat),
            transcendentals=rows * HEADS * latents * block,
        ),
        name="attend",
    )(me, *latent_parts, gain, latent_ids, byte_ids, keys, values, *flat)


def feed_call(me, parts, latents_flat, cot_flat, gain, pieces, flat, n):
    groups = len(parts)
    tokens, lat = latents_flat.shape
    count = len(flat)

    def kernel(me_ref, *refs):
        part_refs = refs[:groups]
        x_ref, cot_ref, gain_ref = refs[groups : groups + 3]
        piece_refs = refs[groups + 3 : groups + 3 + count]
        rest = refs[groups + 3 + count :]
        new_ref, mixed_grad_ref, message_ref, attended_t, branch, normed_t, inner, act_t = rest[:8]
        wo, w1, w2, sems = rest[8:]
        me = me_ref[0]
        loads = []
        base = 0
        for first, target in ((0, wo), (n, w1), (2 * n, w2)):
            found = piece_copies(pieces, piece_refs, first, n, target, me, sems, base)
            base += len(found)
            loads.append(found)
        for found in loads:
            for copy in found:
                copy.start()

        lane = lax.broadcasted_iota(jnp.int32, (LANES, lat), 0)
        column = lax.broadcasted_iota(jnp.int32, (LANES, lat), 1)
        spread = jnp.zeros((LANES, lat), jnp.bool_)
        for head in range(HEADS):
            inside = (column >= head * HEAD_DIM) & (column < (head + 1) * HEAD_DIM)
            own = (lane == head) | (lane == HEADS + head) | (lane == 2 * HEADS + head)
            spread = spread | (inside & own)
        spread = spread.astype(F32).astype(BF)
        logs = [dot(ref[:, lat:], spread) for ref in part_refs]
        top = functools.reduce(jnp.maximum, logs)
        shares = [jnp.exp(log - top) for log in logs]
        total = functools.reduce(jnp.add, shares)
        summed = functools.reduce(
            jnp.add, [s * ref[:, :lat].astype(F32) for s, ref in zip(shares, part_refs)]
        )
        attended = (summed / total).astype(BF)
        log_total = top + jnp.log(total)
        attended_t[...] = jnp.transpose(attended, (1, 0))

        for copy in loads[0]:
            copy.wait()
        mixed = x_ref[...].astype(F32) + dot(attended, wo[...])
        xhat, scale = standardize(mixed)
        gain = gain_ref[...]
        normed = (xhat * gain).astype(BF)
        normed_t[...] = jnp.transpose(normed, (1, 0))
        for copy in loads[1]:
            copy.wait()
        hidden = dot(normed, w1[...])
        activated = gelu(hidden).astype(BF)
        act_t[...] = jnp.transpose(activated, (1, 0))
        for copy in loads[2]:
            copy.wait()
        new_ref[...] = (mixed + dot(activated, w2[...])).astype(BF)
        cot = cot_ref[...]
        grad_hidden = (dot(cot, w2[...], ((1,), (1,))) * gelu_slope(hidden)).astype(BF)
        inner[...] = grad_hidden
        upstream = dot(grad_hidden, w1[...], ((1,), (1,)))
        grad_mixed = cot.astype(F32) + norm_pull(upstream, gain, xhat, scale)
        mixed_grad_ref[...] = grad_mixed
        grad_branch = grad_mixed.astype(BF)
        branch[...] = grad_branch
        grad_attended = dot(grad_branch, wo[...], ((1,), (1,))).astype(BF)
        message_ref[:, :lat] = grad_attended
        product = grad_attended.astype(F32) * attended.astype(F32)
        out_lane = lax.broadcasted_iota(jnp.int32, (tokens, LANES), 1)
        stats = jnp.zeros((tokens, LANES), F32)
        for head in range(HEADS):
            at, shift = head_window(head)
            mask = head_lanes(head)
            inner_sum = jnp.sum(
                jnp.where(mask, product[:, at : at + WINDOW], 0.0), axis=-1, keepdims=True
            )
            first_lane = at + shift
            log_column = log_total[:, first_lane : first_lane + 1]
            terms = split_three(log_column) + split_three(inner_sum)
            for index, term in enumerate(terms):
                stats = jnp.where(out_lane == index * HEADS + head, term, stats)
        message_ref[:, lat:] = stats.astype(BF)

    return pl.pallas_call(
        kernel,
        in_specs=[pl.BlockSpec(memory_space=pltpu.SMEM)]
        + [whole_spec()] * (groups + 3)
        + [any_spec()] * count,
        out_specs=[whole_spec()] * 8,
        out_shape=[
            jax.ShapeDtypeStruct((tokens, lat), BF),
            jax.ShapeDtypeStruct((tokens, lat), F32),
            jax.ShapeDtypeStruct((tokens, lat + LANES), BF),
            jax.ShapeDtypeStruct((lat, tokens), BF),
            jax.ShapeDtypeStruct((tokens, lat), BF),
            jax.ShapeDtypeStruct((lat, tokens), BF),
            jax.ShapeDtypeStruct((tokens, lat), BF),
            jax.ShapeDtypeStruct((lat, tokens), BF),
        ],
        scratch_shapes=[pltpu.VMEM((lat, lat), BF)] * 3
        + [pltpu.SemaphoreType.DMA((6 * count,))],
        compiler_params=params(0),
        cost_estimate=pl.CostEstimate(
            flops=12 * tokens * lat * lat,
            bytes_accessed=6 * lat * lat + 30 * tokens * lat,
            transcendentals=8 * tokens * lat,
        ),
        name="feed",
    )(me, *parts, latents_flat, cot_flat, gain, *flat)


def feed_grads_call(me, lefts, rights, n, far):
    lat, tokens = lefts[0].shape
    width = rights[0].shape[1]
    terms = len(lefts)

    def kernel(me_ref, *refs):
        left_refs, right_refs = refs[:terms], refs[terms : 2 * terms]
        outs = refs[2 * terms :]
        me = me_ref[0]
        for distance in range(far):
            place = pl.multiple_of(jnp.bitwise_xor(me, distance) * n, 16)
            for index in range(terms):
                chunk = left_refs[index][pl.ds(place, n), :]
                outs[distance][index * n : (index + 1) * n, :] = dot(
                    chunk, right_refs[index][...]
                ).astype(BF)

    return pl.pallas_call(
        kernel,
        in_specs=[pl.BlockSpec(memory_space=pltpu.SMEM)] + [whole_spec()] * (2 * terms),
        out_specs=[whole_spec()] * far,
        out_shape=[jax.ShapeDtypeStruct((terms * n, width), BF)] * far,
        compiler_params=params(0),
        cost_estimate=pl.CostEstimate(
            flops=2 * terms * tokens * lat * width,
            bytes_accessed=2 * terms * (lat * width + 2 * tokens * lat),
            transcendentals=0,
        ),
        name="feed_grads",
    )(me, *lefts, *rights)


def attend_back_call(
    me, parts, queries, keys, values, latent_ids, byte_ids, byte_t, latent_t, pieces, flat,
    key_rows, query_rows, query_at, rows, far,
):
    groups = len(parts)
    tokens, lat = keys.shape
    width = byte_t.shape[0]
    block = tokens // rows
    latents = queries.shape[0] // rows
    group = latents // groups
    count = len(flat)
    score_scale = 1.0 / math.sqrt(HEAD_DIM)
    chunk_rows = 2 * key_rows + query_rows

    def kernel(me_ref, *refs):
        part_refs = refs[:groups]
        query_ref, key_ref, value_ref, lid_ref, bid_ref, byte_t_ref, latent_t_ref = refs[
            groups : groups + 7
        ]
        piece_refs = refs[groups + 7 : groups + 7 + count]
        rest = refs[groups + 7 + count :]
        grad_key_ref, grad_value_ref = rest[:2]
        up_refs = rest[2 : 2 + groups]
        out_refs = rest[2 + groups : 2 + groups + far]
        wq, message, acc_q, acc_k, acc_v, all_q, all_k, all_v, sems = rest[2 + groups + far :]
        row = pl.program_id(0)
        me = me_ref[0]

        def copies():
            return piece_copies(pieces, piece_refs, query_at, query_rows, wq, me, sems, 0)

        @pl.when(row == 0)
        def _():
            for copy in copies():
                copy.start()

        for index, ref in enumerate(part_refs):
            message[index * group : (index + 1) * group, :] = ref[...]
        stats = jnp.transpose(message[:, lat:].astype(F32), (1, 0))
        allowed = bid_ref[0] == lid_ref[0]
        for head in range(HEADS):
            at, _ = head_window(head)
            mask = head_lanes(head)
            window = slice(at, at + WINDOW)
            take = lambda k: stats[k * HEADS + head : k * HEADS + head + 1, :]
            log_total = take(0) + take(1) + take(2)
            inner_sum = take(3) + take(4) + take(5)
            query = jnp.where(mask, query_ref[:, window], jnp.zeros((), BF))
            grad = jnp.where(mask, message[:, window], jnp.zeros((), BF))
            key = key_ref[:, window]
            scores = dot(key, query, ((1,), (1,))) * score_scale
            probs = jnp.exp(jnp.where(allowed, scores - log_total, NEG_FILL))
            grad_probs = dot(value_ref[:, window], grad, ((1,), (1,)))
            grad_scores = (probs * (grad_probs - inner_sum)).astype(BF)
            found_k = dot(grad_scores, query)
            found_v = dot(probs.astype(BF), grad)
            found_q = dot(grad_scores, key, ((0,), (0,)))
            if head == 0:
                acc_k[:, window] = found_k
                acc_v[:, window] = found_v
                acc_q[:, window] = found_q
            else:
                acc_k[:, window] = jnp.where(mask, found_k, acc_k[:, window])
                acc_v[:, window] = jnp.where(mask, found_v, acc_v[:, window])
                acc_q[:, window] = jnp.where(mask, found_q, acc_q[:, window])

        byte_place = pl.multiple_of(row * block, 16)
        latent_place = pl.multiple_of(row * latents, 16)
        grad_key = (acc_k[...] * score_scale).astype(BF)
        grad_value = acc_v[...].astype(BF)
        grad_query = (acc_q[...] * score_scale).astype(BF)
        grad_key_ref[...] = grad_key
        grad_value_ref[...] = grad_value
        all_k[pl.ds(byte_place, block), :] = grad_key
        all_v[pl.ds(byte_place, block), :] = grad_value
        all_q[pl.ds(latent_place, latents), :] = grad_query

        @pl.when(row == 0)
        def _():
            for copy in copies():
                copy.wait()

        upstream = dot(grad_query, wq[...], ((1,), (1,))).astype(BF)
        for index, ref in enumerate(up_refs):
            ref[...] = upstream[index * group : (index + 1) * group, :]

        @pl.when(row == rows - 1)
        def _():
            for distance in range(far):
                owner = jnp.bitwise_xor(me, distance)
                place = pl.multiple_of(owner * key_rows, 16)
                chunk = byte_t_ref[pl.ds(place, key_rows), :]
                out = out_refs[distance]
                out[:key_rows, :] = dot(chunk, all_k[...]).astype(BF)
                out[key_rows : 2 * key_rows, :] = dot(chunk, all_v[...]).astype(BF)
                place = pl.multiple_of(owner * query_rows, 16)
                chunk = latent_t_ref[pl.ds(place, query_rows), :]
                out[2 * key_rows :, :] = dot(chunk, all_q[...]).astype(BF)

    row_block = lambda i, m: (i, 0)
    once = pl.Buffered(buffer_count=1)
    return pl.pallas_call(
        kernel,
        grid_spec=pltpu.PrefetchScalarGridSpec(
            num_scalar_prefetch=1,
            grid=(rows,),
            in_specs=[pl.BlockSpec((group, lat + LANES), row_block)] * groups
            + [
                pl.BlockSpec((latents, lat), row_block),
                pl.BlockSpec((block, lat), row_block),
                pl.BlockSpec((block, lat), row_block),
                pl.BlockSpec((1, 1, latents), lambda i, m: (i, 0, 0)),
                pl.BlockSpec((1, block, 1), lambda i, m: (i, 0, 0)),
                pl.BlockSpec((width, tokens), lambda i, m: (0, 0), pipeline_mode=once),
                pl.BlockSpec((lat, rows * latents), lambda i, m: (0, 0), pipeline_mode=once),
            ]
            + [any_spec()] * count,
            out_specs=[pl.BlockSpec((block, lat), row_block)] * 2
            + [pl.BlockSpec((group, lat), row_block)] * groups
            + [
                pl.BlockSpec((chunk_rows, lat), lambda i, m: (0, 0), pipeline_mode=once)
            ]
            * far,
            scratch_shapes=[
                pltpu.VMEM((lat, lat), BF),
                pltpu.VMEM((latents, lat + LANES), BF),
                pltpu.VMEM((latents, lat), F32),
                pltpu.VMEM((block, lat), F32),
                pltpu.VMEM((block, lat), F32),
                pltpu.VMEM((rows * latents, lat), BF),
                pltpu.VMEM((tokens, lat), BF),
                pltpu.VMEM((tokens, lat), BF),
                pltpu.SemaphoreType.DMA((2 * count,)),
            ],
        ),
        out_shape=[jax.ShapeDtypeStruct((tokens, lat), BF)] * 2
        + [jax.ShapeDtypeStruct((rows * group, lat), BF)] * groups
        + [jax.ShapeDtypeStruct((chunk_rows, lat), BF)] * far,
        compiler_params=params(1),
        cost_estimate=pl.CostEstimate(
            flops=10 * rows * HEADS * latents * block * WINDOW
            + 4 * tokens * width * lat
            + 4 * rows * latents * lat * lat,
            bytes_accessed=2 * (8 * tokens * lat + 4 * lat * lat),
            transcendentals=rows * HEADS * latents * block,
        ),
        name="attend_back",
    )(me, *parts, queries, keys, values, latent_ids, byte_ids, byte_t, latent_t, *flat)


def byte_grad_call(me, bytes_flat, gain, grad_keys, grad_values, pieces, flat, key_rows, key_at, value_at, rows):
    tokens, width = bytes_flat.shape
    block = tokens // rows
    lat = grad_keys.shape[1]
    count = len(flat)

    def kernel(me_ref, x_ref, gain_ref, gk_ref, gv_ref, *refs):
        piece_refs = refs[:count]
        out_ref, wk, wv, sems = refs[count:]

        def copies():
            one = piece_copies(pieces, piece_refs, key_at, key_rows, wk, me_ref[0], sems, 0)
            two = piece_copies(
                pieces, piece_refs, value_at, key_rows, wv, me_ref[0], sems, len(one)
            )
            return one + two

        @pl.when(pl.program_id(0) == 0)
        def _():
            for copy in copies():
                copy.start()

        xhat, scale = standardize(x_ref[...].astype(F32))

        @pl.when(pl.program_id(0) == 0)
        def _():
            for copy in copies():
                copy.wait()

        upstream = dot(gk_ref[...], wk[...], ((1,), (1,))) + dot(
            gv_ref[...], wv[...], ((1,), (1,))
        )
        out_ref[...] = norm_pull(upstream, gain_ref[...], xhat, scale)

    row_block = lambda i, m: (i, 0)
    return pl.pallas_call(
        kernel,
        grid_spec=pltpu.PrefetchScalarGridSpec(
            num_scalar_prefetch=1,
            grid=(rows,),
            in_specs=[
                pl.BlockSpec((block, width), row_block),
                pl.BlockSpec((1, width), lambda i, m: (0, 0)),
                pl.BlockSpec((block, lat), row_block),
                pl.BlockSpec((block, lat), row_block),
            ]
            + [any_spec()] * count,
            out_specs=pl.BlockSpec((block, width), row_block),
            scratch_shapes=[
                pltpu.VMEM((width, lat), BF),
                pltpu.VMEM((width, lat), BF),
                pltpu.SemaphoreType.DMA((4 * count,)),
            ],
        ),
        out_shape=jax.ShapeDtypeStruct((tokens, width), F32),
        compiler_params=params(1),
        cost_estimate=pl.CostEstimate(
            flops=4 * tokens * width * lat,
            bytes_accessed=2 * (3 * tokens * width + 2 * tokens * lat + 2 * width * lat),
            transcendentals=0,
        ),
        name="byte_grad",
    )(me, bytes_flat, gain, grad_keys, grad_values, *flat)


def swap(value, axis, size, distance):
    return lax.ppermute(value, axis, [(i, i ^ distance) for i in range(size)])


def gather_shards(message, own, size):
    found = [message] + [swap(message, "fsdp", size, j) for j in range(1, size)]
    return [lax.select_n(jnp.bitwise_xor(own, k), *found) for k in range(size)]


def gather_blocks(block, n_dp, half):
    send = lambda value, distance: swap(value, "dp", n_dp, distance)
    rows = block.shape[0]
    full = [(0, rows)]
    chips = [(0, full, [block])]
    if n_dp == 8:
        one, two = send(block, 2), send(block, 4)
        chips.append((2, full, [one]))
        chips.append((4, full, [two]))
        low, high = send(one[:half], 4), send(two[half:], 2)
        chips.append((6, [(0, half), (half, rows)], [low, high]))
    else:
        for distance in range(2, n_dp, 2):
            chips.append((distance, full, [send(block, distance)]))
    pieces, flat = [], []
    for distance, parts, arrays in chips:
        pieces.append((distance, parts))
        flat.extend(arrays)
        pieces.append((distance + 1, parts))
        flat.extend(send(array, 1) for array in arrays)
    return pieces, flat


def add(*values):
    return functools.reduce(jnp.add, [v.astype(F32) for v in values]).astype(BF)


def scatter_blocks(parts, n_dp, half):
    send = lambda value, distance: swap(value, "dp", n_dp, distance)
    arrived = [send(parts[d + 1], 1) for d in range(0, n_dp, 2)]
    chips = [(parts[d], arrived[d // 2]) for d in range(0, n_dp, 2)]
    if n_dp == 8:
        low = send(add(*[v[:half] for v in chips[3]]), 2)
        high = send(add(*[v[half:] for v in chips[3]]), 4)
        one = jnp.concatenate(
            [add(*[v[:half] for v in chips[1]]), add(*[v[half:] for v in chips[1]], high)], axis=0
        )
        two = jnp.concatenate(
            [add(*[v[:half] for v in chips[2]], low), add(*[v[half:] for v in chips[2]])], axis=0
        )
        return add(*chips[0], send(one, 2), send(two, 4))
    return add(*chips[0], *[send(add(*chips[i]), 2 * i) for i in range(1, len(chips))])


def scatter_shards(block, own, size, rows_of):
    def message(distance):
        index = jnp.bitwise_xor(own, distance)
        found, at = [], 0
        for rows in rows_of:
            part = block[at : at + rows * size].reshape(size, rows, block.shape[1])
            found.append(lax.dynamic_index_in_dim(part, index, 0, keepdims=False))
            at += rows * size
        return found

    total = [part.astype(F32) for part in message(0)]
    for distance in range(1, size):
        arrived = swap(jnp.concatenate(message(distance), axis=0), "fsdp", size, distance)
        at = 0
        for index, rows in enumerate(rows_of):
            total[index] = total[index] + arrived[at : at + rows].astype(F32)
            at += rows
    return total


def up_to(value, step):
    return -(-value // step) * step


def pad_rows(value, rows):
    return jnp.pad(value, ((0, rows - value.shape[0]), (0, 0)))


def local(n_dp, n_f, bytes_in, latents_in, cotangent, byte_segments, latent_segments,
          w_query, w_key, w_value, w_out, w_mlp_in, w_mlp_out,
          gain_latent, gain_byte, gain_mlp):
    rows, byte_local, width = bytes_in.shape
    _, group, lat = latents_in.shape
    latents = group * n_f
    dp, own = lax.axis_index("dp"), lax.axis_index("fsdp")
    me = dp.astype(jnp.int32).reshape(1)
    bytes_flat = bytes_in.reshape(rows * byte_local, width)
    latents_flat = latents_in.reshape(rows * group, lat)
    cot_flat = cotangent.reshape(rows * group, lat)

    kr, qr = w_key.shape[0], w_query.shape[0]
    gains = jnp.concatenate([gain_latent, gain_byte, gain_mlp])
    gains = jnp.pad(gains, (0, lat - gains.shape[0]))[None, :]
    message = jnp.concatenate([w_key, w_value, w_query, gains], axis=0)
    message = pad_rows(message, up_to(2 * kr + qr + 1, 16))
    shards = gather_shards(message, own, n_f)
    block = jnp.concatenate(
        [s[:kr] for s in shards]
        + [s[kr : 2 * kr] for s in shards]
        + [s[2 * kr : 2 * kr + qr] for s in shards]
        + [s[2 * kr + qr : 2 * kr + qr + 1] for s in shards],
        axis=0,
    )
    key_rows, query_rows = n_f * kr, n_f * qr
    gain_at = 2 * key_rows + query_rows
    block = pad_rows(block, up_to(gain_at + n_f, 16))
    pieces, flat = gather_blocks(block, n_dp, 2 * key_rows)

    by_distance = [None] * n_dp
    index = 0
    for distance, parts in pieces:
        by_distance[distance] = flat[index + len(parts) - 1]
        index += len(parts)
    gain_rows = []
    for array in by_distance:
        end = array.shape[0] - (block.shape[0] - gain_at)
        gain_rows.append(array[end : end + n_f, : 2 * qr + kr])
    gain_rows = jnp.stack(gain_rows)
    gain_rows = jnp.take(gain_rows, jnp.bitwise_xor(jnp.arange(n_dp), dp), axis=0)
    gain_rows = gain_rows.astype(F32)
    latent_gain = gain_rows[:, :, :qr].reshape(1, lat)
    byte_gain = gain_rows[:, :, qr : qr + kr].reshape(1, width)
    mlp_gain = gain_rows[:, :, qr + kr :].reshape(1, lat)

    ids = latent_segments.reshape(1, rows * group).astype(BF)
    ids = jnp.pad(ids, ((0, 15), (0, lat - rows * group)))
    latent_message = jnp.concatenate([latents_flat, ids], axis=0)
    latent_parts = [latent_message] + [
        swap(latent_message, "fsdp", n_f, j) for j in range(1, n_f)
    ]
    latent_ids = jnp.stack(
        [p[rows * group, : rows * group].reshape(rows, group) for p in latent_parts], axis=1
    ).reshape(rows, latents)
    latent_ids = latent_ids.astype(F32)
    byte_ids = lax.dynamic_slice_in_dim(byte_segments, own * byte_local, byte_local, axis=1)
    byte_ids = byte_ids.astype(F32)

    message = jnp.concatenate([w_out, w_mlp_in, w_mlp_out], axis=0)
    shards = gather_shards(message, own, n_f)
    block_two = jnp.concatenate(
        [s[i * qr : (i + 1) * qr] for i in range(3) for s in shards], axis=0
    )
    half = up_to(3 * query_rows // 2, 16)
    pieces_two, flat_two = gather_blocks(block_two, n_dp, half)

    byte_t, keys, values = key_value_call(
        me, bytes_flat, byte_gain, pieces, flat, key_rows, 0, key_rows, rows
    )
    latent_t, queries, *found = attend_call(
        me, latent_parts, latent_gain, latent_ids[:, :, None], byte_ids[:, None, :],
        keys, values, pieces, flat, query_rows, 2 * key_rows, rows,
    )
    attended_parts = [found[0]] + [swap(found[j], "fsdp", n_f, j) for j in range(1, n_f)]
    new, grad_mixed, grad_message, attended_t, branch, normed_t, inner, act_t = feed_call(
        me, attended_parts, latents_flat, cot_flat, mlp_gain, pieces_two, flat_two, query_rows
    )
    grad_parts = [grad_message] + [swap(grad_message, "fsdp", n_f, j) for j in range(1, n_f)]
    feed_grads = feed_grads_call(
        me, (attended_t, normed_t, act_t), (branch, inner, cot_flat), query_rows, n_dp
    )
    grad_two = scatter_shards(scatter_blocks(feed_grads, n_dp, half), own, n_f, (qr, qr, qr))

    out = attend_back_call(
        me, grad_parts, queries, keys, values, latent_ids[:, None, :], byte_ids[:, :, None],
        byte_t, latent_t, pieces, flat, key_rows, query_rows, 2 * key_rows, rows, n_dp,
    )
    grad_keys, grad_values = out[:2]
    ups = out[2 : 2 + n_f]
    grad_one = scatter_shards(
        scatter_blocks(out[2 + n_f :], n_dp, 2 * key_rows), own, n_f, (kr, kr, qr)
    )
    up_parts = [ups[0]] + [swap(ups[j], "fsdp", n_f, j) for j in range(1, n_f)]
    grad_bytes = byte_grad_call(
        me, bytes_flat, byte_gain, grad_keys, grad_values, pieces, flat,
        key_rows, 0, key_rows, rows,
    )
    upstream = functools.reduce(jnp.add, [p.astype(F32) for p in up_parts])
    xhat, scale = standardize(latents_flat.astype(F32))
    grad_latents = grad_mixed + norm_pull(upstream, latent_gain, xhat, scale)

    def gain_grad(pairs, gain):
        total = sum(jnp.sum(w.astype(F32) * g, axis=1) for w, g in pairs)
        return total / gain.astype(F32)

    grad_key, grad_value, grad_query = grad_one
    grad_out, grad_inner, grad_outer = grad_two
    return (
        new.reshape(rows, group, lat),
        grad_latents.reshape(rows, group, lat),
        grad_bytes.reshape(rows, byte_local, width),
        grad_query,
        grad_key,
        grad_value,
        grad_out,
        grad_inner,
        grad_outer,
        gain_grad([(w_query, grad_query)], gain_latent),
        gain_grad([(w_key, grad_key), (w_value, grad_value)], gain_byte),
        gain_grad([(w_mlp_in, grad_inner)], gain_mlp),
    )


def solution(mesh):
    rows3 = P("dp", "fsdp", None)
    split2 = P(("dp", "fsdp"), None)
    split1 = P(("dp", "fsdp"))
    in_specs = (rows3,) * 3 + (P("dp", None), P("dp", "fsdp")) + (split2,) * 6 + (split1,) * 3
    out_specs = (rows3,) * 3 + (split2,) * 6 + (split1,) * 3
    body = functools.partial(local, mesh.shape["dp"], mesh.shape["fsdp"])
    return jax.shard_map(
        body, mesh=mesh, in_specs=in_specs, out_specs=out_specs, check_vma=False
    )
```

```python
import functools
import math

import jax
import jax.numpy as jnp
from jax import lax
from jax.experimental import pallas as pl
from jax.experimental.pallas import tpu as pltpu
from jax.sharding import PartitionSpec as P

HEADS = 8
HEAD_DIM = 160
EPSILON = 1e-05
NEG_FILL = -1e30
LANES = 128
WINDOW = 256
BF = jnp.bfloat16
F32 = jnp.float32
GAIN_ROWS = 16
SMALL = pl.CostEstimate(flops=1, bytes_accessed=1, transcendentals=0)


def head_window(head):
    start = head * HEAD_DIM // LANES * LANES
    return start, head * HEAD_DIM - start


def head_lanes(head):
    _, shift = head_window(head)
    lane = lax.broadcasted_iota(jnp.int32, (1, WINDOW), 1)
    return (lane >= shift) & (lane < shift + HEAD_DIM)


def dot(a, b, dims=((1,), (0,))):
    return lax.dot_general(a, b, (dims, ((), ())), preferred_element_type=F32)


def standardize(values):
    centered = values - jnp.mean(values, axis=-1, keepdims=True)
    scale = lax.rsqrt(jnp.mean(centered * centered, axis=-1, keepdims=True) + EPSILON)
    return centered * scale, scale


def norm_pull(upstream, gain, xhat, scale):
    scaled = upstream * gain
    return scale * (
        scaled
        - jnp.mean(scaled, axis=-1, keepdims=True)
        - xhat * jnp.mean(scaled * xhat, axis=-1, keepdims=True)
    )


def split_three(values):
    first = values.astype(BF).astype(F32)
    rest = values - first
    second = rest.astype(BF).astype(F32)
    return first, second, rest - second


def gelu(values):
    inner = math.sqrt(2 / math.pi) * (values + 0.044715 * values * values * values)
    return 0.5 * values * (1.0 + jnp.tanh(inner))


def gelu_slope(values):
    square = values * values
    tanh = jnp.tanh(math.sqrt(2 / math.pi) * (values + 0.044715 * square * values))
    slope = math.sqrt(2 / math.pi) * (1.0 + 3 * 0.044715 * square)
    return 0.5 * (1.0 + tanh) + 0.5 * values * (1.0 - tanh * tanh) * slope


def piece_copies(pieces, flat_refs, first, rows, target, me, sems, base):
    copies = []
    lanes = target.shape[1]
    at = 0
    for distance, parts in pieces:
        owner = jnp.bitwise_xor(me, distance)
        for low, high in parts:
            ref = flat_refs[at]
            at += 1
            start, stop = max(low, first), min(high, first + rows)
            if start < stop:
                place = pl.multiple_of(owner * rows + (start - first), 16)
                copies.append(
                    pltpu.make_async_copy(
                        ref.at[pl.ds(start - low, stop - start), pl.ds(0, lanes)],
                        target.at[pl.ds(place, stop - start), :],
                        sems.at[base + len(copies)],
                    )
                )
    return copies


def group_values(refs, place):
    if len(refs) != 5:
        return [ref[...] for ref in refs]
    own = place[1]
    at_end = (own == 0) | (own == 3)
    values = [ref[...] for ref in refs[:3]]
    return values + [jnp.where(at_end, refs[4][...], refs[3][...])]


def gain_vector(held, size, lane_at, shards):
    per_shard = size // shards
    blocks = held.shape[0] // GAIN_ROWS
    per_block = shards // blocks
    lane = lax.broadcasted_iota(jnp.int32, (LANES, size), 0)
    column = lax.broadcasted_iota(jnp.int32, (LANES, size), 1)
    pick = (lane == lane_at + column % per_shard).astype(F32).astype(BF)
    spread = dot(held[...], pick)
    row = lax.broadcasted_iota(jnp.int32, spread.shape, 0)
    column = lax.broadcasted_iota(jnp.int32, spread.shape, 1) // per_shard
    owner = (row // GAIN_ROWS) * per_block + row % GAIN_ROWS
    right = (owner == column) & (row % GAIN_ROWS < per_block)
    return jnp.sum(jnp.where(right, spread, 0.0), axis=0, keepdims=True)


def params(grid_rank, mebibytes=60):
    return pltpu.CompilerParams(
        dimension_semantics=("arbitrary",) * grid_rank, vmem_limit_bytes=mebibytes << 20
    )


def whole_spec():
    return pl.BlockSpec(memory_space=pltpu.VMEM)


def any_spec():
    return pl.BlockSpec(memory_space=pltpu.HBM)


class Held:
    def __init__(self, pieces, flat, spans):
        self.pieces, self.flat, self.spans = pieces, flat, spans

    def crossed(self):
        at = 0
        for distance, parts in self.pieces:
            if distance == self.blocks - 2:
                return self.flat[at : at + len(parts)]
            at += len(parts)

    def copies(self, names, refs, targets, place, sems):
        found, base = [], 0
        for name, target in zip(names, targets):
            first, rows = self.spans[name]
            some = piece_copies(self.pieces, refs, first, rows, target, place[0], sems, base)
            base += len(some)
            found.append(some)
        return found


def run_all(groups, action):
    for group in groups:
        for copy in group:
            getattr(copy, action)()


def shape(dims, dtype=BF):
    return jax.ShapeDtypeStruct(dims, dtype)


def full_block(dims):
    return pl.BlockSpec(
        dims, lambda i, p: (0,) * len(dims), pipeline_mode=pl.Buffered(buffer_count=1)
    )


def scalar_spec():
    return pl.BlockSpec(memory_space=pltpu.SMEM)


def assemble_call(place, parts, segments, total, size):
    def kernel(place_ref, *refs):
        part_refs, out_ref, acc = refs[: len(parts)], refs[len(parts)], refs[len(parts) + 1]
        values = [v.astype(F32) for v in group_values(part_refs, place_ref)]
        end = max(at + size * rows for _, rows, at in segments)
        if end < total:
            first = end // 8 * 8
            acc[first:, :] = jnp.zeros((total - first, acc.shape[1]), F32)
        for index in range(size):
            want = jnp.bitwise_xor(place_ref[1], index)
            value = values[size - 1]
            for distance in range(size - 2, -1, -1):
                value = jnp.where(want == distance, values[distance], value)
            for first, rows, at in segments:
                acc[at + index * rows : at + (index + 1) * rows, :] = value[first : first + rows]
        out_ref[...] = acc[...].astype(BF)

    lat = parts[0].shape[1]
    return pl.pallas_call(
        kernel,
        in_specs=[scalar_spec()] + [whole_spec()] * len(parts),
        out_specs=whole_spec(),
        out_shape=shape((total, lat)),
        scratch_shapes=[pltpu.VMEM((total, lat), F32)],
        compiler_params=params(0, 24),
        cost_estimate=SMALL,
        name="assemble",
    )(place, *parts)


def key_value_call(place, bytes_flat, held, rows):
    tokens, width = bytes_flat.shape
    block = tokens // rows
    lat = held.flat[0].shape[1]
    count = len(held.flat)
    shards = place_shards(held)

    def kernel(place_ref, x_ref, *refs):
        piece_refs = refs[:count]
        normed_t_ref, key_ref, value_ref, wk, wv, gains, gain, sems = refs[count:]
        first = pl.program_id(0) == 0

        def loads():
            return held.copies(
                ("gains", "key", "value"), piece_refs, (gains, wk, wv), place_ref, sems
            )

        @pl.when(first)
        def _():
            run_all(loads(), "start")

        xhat, _ = standardize(x_ref[...].astype(F32))

        @pl.when(first)
        def _():
            run_all(loads(), "wait")
            gain[...] = gain_vector(gains, width, held.lanes["byte"], shards)

        normed = (xhat * gain[...]).astype(BF)
        key_ref[...] = dot(normed, wk[...]).astype(BF)
        value_ref[...] = dot(normed, wv[...]).astype(BF)
        normed_t_ref[...] = jnp.transpose(normed, (1, 0))

    row_block = lambda i, p: (i, 0)
    return pl.pallas_call(
        kernel,
        grid_spec=pltpu.PrefetchScalarGridSpec(
            num_scalar_prefetch=1,
            grid=(rows,),
            in_specs=[pl.BlockSpec((block, width), row_block)] + [any_spec()] * count,
            out_specs=[
                pl.BlockSpec((width, block), lambda i, p: (0, i)),
                pl.BlockSpec((block, lat), row_block),
                pl.BlockSpec((block, lat), row_block),
            ],
            scratch_shapes=[
                pltpu.VMEM((width, lat), BF),
                pltpu.VMEM((width, lat), BF),
                pltpu.VMEM((held.blocks * GAIN_ROWS, LANES), BF),
                pltpu.VMEM((1, width), F32),
                pltpu.SemaphoreType.DMA((6 * count,)),
            ],
        ),
        out_shape=[shape((width, tokens)), shape((tokens, lat)), shape((tokens, lat))],
        compiler_params=params(1),
        cost_estimate=SMALL,
        name="keys_values",
    )(place, bytes_flat, *held.flat)


def place_shards(held):
    return held.blocks * held.size


def attend_call(place, latent_parts, byte_ids, keys, values, held, groups, group, first, rows):
    parts = len(latent_parts)
    lat = keys.shape[1]
    block = byte_ids.shape[2]
    latents = groups * group
    count = len(held.flat)
    shards = place_shards(held)
    score_scale = 1.0 / math.sqrt(HEAD_DIM)

    def kernel(place_ref, *refs):
        part_refs = refs[:parts]
        bid_ref, key_ref, value_ref = refs[parts : parts + 3]
        piece_refs = refs[parts + 3 : parts + 3 + count]
        rest = refs[parts + 3 + count :]
        normed_t_ref, query_ref = rest[:2]
        out_refs = rest[2 : 2 + groups]
        wq, gains, gain, acc, sems = rest[2 + groups :]
        start = pl.program_id(0) == 0

        def loads():
            return held.copies(("gains", "query"), piece_refs, (gains, wq), place_ref, sems)

        @pl.when(start)
        def _():
            run_all(loads(), "start")

        message = jnp.concatenate(group_values(part_refs, place_ref), axis=0)
        ids = message[:, lat : lat + 1].astype(F32)
        xhat, _ = standardize(message[:, :lat].astype(F32))

        @pl.when(start)
        def _():
            run_all(loads(), "wait")
            gain[...] = gain_vector(gains, lat, held.lanes["latent"], shards)

        normed = (xhat * gain[...]).astype(BF)
        query_ref[...] = dot(normed, wq[...]).astype(BF)
        normed_t_ref[...] = jnp.transpose(normed, (1, 0))
        allowed = ids == bid_ref[0]
        lane = lax.broadcasted_iota(jnp.int32, (latents, LANES), 1)
        stats = jnp.zeros((latents, LANES), F32)
        for head in range(HEADS):
            at, _ = head_window(head)
            mask = head_lanes(head)
            window = slice(at, at + WINDOW)
            query = jnp.where(mask, query_ref[:, window], jnp.zeros((), BF))
            scores = dot(query, key_ref[:, window], ((1,), (1,))) * score_scale
            scores = jnp.where(allowed, scores, NEG_FILL)
            top = jnp.max(scores, axis=-1, keepdims=True)
            exponent = jnp.exp(scores - top)
            total = jnp.sum(exponent, axis=-1, keepdims=True)
            found = dot(exponent.astype(BF), value_ref[:, window]) / total
            if head == 0:
                acc[:, window] = found
            else:
                acc[:, window] = jnp.where(mask, found, acc[:, window])
            log_total = jnp.where(top > -1e29, top + jnp.log(total), NEG_FILL)
            for index, term in enumerate(split_three(log_total)):
                stats = jnp.where(lane == index * HEADS + head, term, stats)
        for index, ref in enumerate(out_refs):
            chunk = slice(index * group, (index + 1) * group)
            ref[:, :lat] = acc[chunk, :].astype(BF)
            ref[:, lat:] = stats[chunk, :].astype(BF)

    row_block = lambda i, p: (first + i, 0)
    own_block = lambda i, p: (i, 0)
    return pl.pallas_call(
        kernel,
        grid_spec=pltpu.PrefetchScalarGridSpec(
            num_scalar_prefetch=1,
            grid=(rows,),
            in_specs=[pl.BlockSpec((group, lat + LANES), row_block)] * parts
            + [
                pl.BlockSpec((1, 1, block), lambda i, p: (first + i, 0, 0)),
                pl.BlockSpec((block, lat), row_block),
                pl.BlockSpec((block, lat), row_block),
            ]
            + [any_spec()] * count,
            out_specs=[
                pl.BlockSpec((lat, latents), lambda i, p: (0, i)),
                pl.BlockSpec((latents, lat), own_block),
            ]
            + [pl.BlockSpec((group, lat + LANES), own_block)] * groups,
            scratch_shapes=[
                pltpu.VMEM((lat, lat), BF),
                pltpu.VMEM((held.blocks * GAIN_ROWS, LANES), BF),
                pltpu.VMEM((1, lat), F32),
                pltpu.VMEM((latents, lat), F32),
                pltpu.SemaphoreType.DMA((4 * count,)),
            ],
        ),
        out_shape=[shape((lat, rows * latents)), shape((rows * latents, lat))]
        + [shape((rows * group, lat + LANES))] * groups,
        compiler_params=params(1),
        cost_estimate=SMALL,
        name="attend",
    )(place, *latent_parts, byte_ids, keys, values, *held.flat)


def feed_call(place, parts, latent_message, cot_flat, held_gain, held, cuts):
    groups, pieces_of = len(parts), len(parts[0])
    tokens, lat = cot_flat.shape
    count, gain_count = len(held.flat), len(held_gain.flat)
    shards = place_shards(held_gain)

    def kernel(place_ref, *refs):
        refs = list(refs)
        take = lambda n: [refs.pop(0) for _ in range(n)]
        part_refs = [take(pieces_of) for _ in range(groups)]
        x_ref, cot_ref = take(2)
        gain_refs, piece_refs = take(gain_count), take(count)
        new_ref, mixed_grad_ref = take(2)
        message_refs = take(len(cuts))
        attended_t, branch, normed_t, inner, act_t = take(5)
        wo, w1, w2, gains, sems, gain_sems = refs
        gain_loads = held_gain.copies(("gains",), gain_refs, (gains,), place_ref, gain_sems)
        loads = held.copies(("out", "inner", "outer"), piece_refs, (wo, w1, w2), place_ref, sems)
        run_all(gain_loads, "start")
        run_all(loads, "start")

        lane = lax.broadcasted_iota(jnp.int32, (LANES, lat), 0)
        column = lax.broadcasted_iota(jnp.int32, (LANES, lat), 1)
        spread = jnp.zeros((LANES, lat), jnp.bool_)
        for head in range(HEADS):
            inside = (column >= head * HEAD_DIM) & (column < (head + 1) * HEAD_DIM)
            own = (lane == head) | (lane == HEADS + head) | (lane == 2 * HEADS + head)
            spread = spread | (inside & own)
        spread = spread.astype(F32).astype(BF)
        found = [jnp.concatenate([ref[...] for ref in some], axis=0) for some in part_refs]
        logs = [dot(value[:, lat:], spread) for value in found]
        top = functools.reduce(jnp.maximum, logs)
        shares = [jnp.exp(log - top) for log in logs]
        total = functools.reduce(jnp.add, shares)
        summed = functools.reduce(
            jnp.add, [s * value[:, :lat].astype(F32) for s, value in zip(shares, found)]
        )
        attended = (summed / total).astype(BF)
        log_total = top + jnp.log(total)
        attended_t[...] = jnp.transpose(attended, (1, 0))

        run_all(gain_loads, "wait")
        gain = gain_vector(gains, lat, held_gain.lanes["mlp"], shards)
        run_all(loads[:1], "wait")
        mixed = x_ref[:, :lat].astype(F32) + dot(attended, wo[...])
        xhat, scale = standardize(mixed)
        normed = (xhat * gain).astype(BF)
        normed_t[...] = jnp.transpose(normed, (1, 0))
        run_all(loads[1:2], "wait")
        hidden = dot(normed, w1[...])
        activated = gelu(hidden).astype(BF)
        act_t[...] = jnp.transpose(activated, (1, 0))
        run_all(loads[2:], "wait")
        new_ref[...] = (mixed + dot(activated, w2[...])).astype(BF)
        cot = cot_ref[...]
        grad_hidden = (dot(cot, w2[...], ((1,), (1,))) * gelu_slope(hidden)).astype(BF)
        inner[...] = grad_hidden
        upstream = dot(grad_hidden, w1[...], ((1,), (1,)))
        grad_mixed = cot.astype(F32) + norm_pull(upstream, gain, xhat, scale)
        mixed_grad_ref[...] = grad_mixed
        grad_branch = grad_mixed.astype(BF)
        branch[...] = grad_branch
        grad_attended = dot(grad_branch, wo[...], ((1,), (1,))).astype(BF)
        product = grad_attended.astype(F32) * attended.astype(F32)
        out_lane = lax.broadcasted_iota(jnp.int32, (tokens, LANES), 1)
        ids = x_ref[:, lat : lat + 1].astype(F32)
        stats = jnp.where(out_lane == 6 * HEADS, ids, 0.0)
        for head in range(HEADS):
            at, shift = head_window(head)
            mask = head_lanes(head)
            inner_sum = jnp.sum(
                jnp.where(mask, product[:, at : at + WINDOW], 0.0), axis=-1, keepdims=True
            )
            first_lane = at + shift
            log_column = log_total[:, first_lane : first_lane + 1]
            terms = split_three(log_column) + split_three(inner_sum)
            for index, term in enumerate(terms):
                stats = jnp.where(out_lane == index * HEADS + head, term, stats)
        stats = stats.astype(BF)
        for (first, some), ref in zip(cuts, message_refs):
            ref[:, :lat] = grad_attended[first : first + some]
            ref[:, lat:] = stats[first : first + some]

    flat_parts = [array for some in parts for array in some]
    return pl.pallas_call(
        kernel,
        in_specs=[scalar_spec()]
        + [whole_spec()] * (len(flat_parts) + 2)
        + [any_spec()] * (gain_count + count),
        out_specs=[whole_spec()] * (7 + len(cuts)),
        out_shape=[shape((tokens, lat)), shape((tokens, lat), F32)]
        + [shape((some, lat + LANES)) for _, some in cuts]
        + [
            shape((lat, tokens)),
            shape((tokens, lat)),
            shape((lat, tokens)),
            shape((tokens, lat)),
            shape((lat, tokens)),
        ],
        scratch_shapes=[pltpu.VMEM((lat, lat), BF)] * 3
        + [
            pltpu.VMEM((held_gain.blocks * GAIN_ROWS, LANES), BF),
            pltpu.SemaphoreType.DMA((6 * count,)),
            pltpu.SemaphoreType.DMA((2 * gain_count,)),
        ],
        compiler_params=params(0),
        cost_estimate=SMALL,
        name="feed",
    )(place, *flat_parts, latent_message, cot_flat, *held_gain.flat, *held.flat)


def feed_grads_call(place, lefts, rights, n, far):
    lat, tokens = lefts[0].shape
    width = rights[0].shape[1]
    terms = len(lefts)

    def kernel(place_ref, *refs):
        left_refs, right_refs = refs[:terms], refs[terms : 2 * terms]
        outs = refs[2 * terms :]
        for distance in range(far):
            at = pl.multiple_of(jnp.bitwise_xor(place_ref[0], distance) * n, 16)
            for index in range(terms):
                chunk = left_refs[index][pl.ds(at, n), :]
                outs[distance][index * n : (index + 1) * n, :] = dot(
                    chunk, right_refs[index][...]
                ).astype(BF)

    return pl.pallas_call(
        kernel,
        in_specs=[scalar_spec()] + [whole_spec()] * (2 * terms),
        out_specs=[whole_spec()] * far,
        out_shape=[shape((terms * n, width))] * far,
        compiler_params=params(0),
        cost_estimate=SMALL,
        name="feed_grads",
    )(place, *lefts, *rights)


def attend_back_call(
    place, parts, queries, keys, values, byte_ids, held, groups, group, first, rows
):
    count_parts = len(parts)
    lat = keys.shape[1]
    block = byte_ids.shape[1]
    latents = groups * group
    count = len(held.flat)
    score_scale = 1.0 / math.sqrt(HEAD_DIM)

    def kernel(place_ref, *refs):
        refs = list(refs)
        take = lambda n: [refs.pop(0) for _ in range(n)]
        part_refs = take(count_parts)
        query_ref, key_ref, value_ref, bid_ref = take(4)
        piece_refs = take(count)
        grad_key_ref, grad_value_ref, grad_query_ref = take(3)
        up_refs = take(groups)
        wq, acc_q, acc_k, acc_v, sems = refs
        row = pl.program_id(0)

        def loads():
            return held.copies(("query",), piece_refs, (wq,), place_ref, sems)

        @pl.when(row == 0)
        def _():
            run_all(loads(), "start")

        message = jnp.concatenate(group_values(part_refs, place_ref), axis=0)
        stats = jnp.transpose(message[:, lat:].astype(F32), (1, 0))
        allowed = bid_ref[0] == stats[6 * HEADS : 6 * HEADS + 1, :]
        for head in range(HEADS):
            at, _ = head_window(head)
            mask = head_lanes(head)
            window = slice(at, at + WINDOW)
            stat = lambda k: stats[k * HEADS + head : k * HEADS + head + 1, :]
            log_total = stat(0) + stat(1) + stat(2)
            inner_sum = stat(3) + stat(4) + stat(5)
            query = jnp.where(mask, query_ref[:, window], jnp.zeros((), BF))
            grad = jnp.where(mask, message[:, window], jnp.zeros((), BF))
            key = key_ref[:, window]
            scores = dot(key, query, ((1,), (1,))) * score_scale
            probs = jnp.exp(jnp.where(allowed, scores - log_total, NEG_FILL))
            grad_probs = dot(value_ref[:, window], grad, ((1,), (1,)))
            grad_scores = (probs * (grad_probs - inner_sum)).astype(BF)
            found_k = dot(grad_scores, query)
            found_v = dot(probs.astype(BF), grad)
            found_q = dot(grad_scores, key, ((0,), (0,)))
            if head == 0:
                acc_k[:, window] = found_k
                acc_v[:, window] = found_v
                acc_q[:, window] = found_q
            else:
                acc_k[:, window] = jnp.where(mask, found_k, acc_k[:, window])
                acc_v[:, window] = jnp.where(mask, found_v, acc_v[:, window])
                acc_q[:, window] = jnp.where(mask, found_q, acc_q[:, window])

        grad_query = (acc_q[...] * score_scale).astype(BF)
        grad_key_ref[...] = (acc_k[...] * score_scale).astype(BF)
        grad_value_ref[...] = acc_v[...].astype(BF)
        grad_query_ref[...] = grad_query

        @pl.when(row == 0)
        def _():
            run_all(loads(), "wait")

        upstream = dot(grad_query, wq[...], ((1,), (1,))).astype(BF)
        for index, ref in enumerate(up_refs):
            ref[...] = upstream[index * group : (index + 1) * group, :]

    row_block = lambda i, p: (first + i, 0)
    own_block = lambda i, p: (i, 0)
    return pl.pallas_call(
        kernel,
        grid_spec=pltpu.PrefetchScalarGridSpec(
            num_scalar_prefetch=1,
            grid=(rows,),
            in_specs=[pl.BlockSpec((group, lat + LANES), own_block)] * count_parts
            + [
                pl.BlockSpec((latents, lat), own_block),
                pl.BlockSpec((block, lat), row_block),
                pl.BlockSpec((block, lat), row_block),
                pl.BlockSpec((1, block, 1), lambda i, p: (first + i, 0, 0)),
            ]
            + [any_spec()] * count,
            out_specs=[
                pl.BlockSpec((block, lat), own_block),
                pl.BlockSpec((block, lat), own_block),
                pl.BlockSpec((latents, lat), own_block),
            ]
            + [pl.BlockSpec((group, lat), own_block)] * groups,
            scratch_shapes=[
                pltpu.VMEM((lat, lat), BF),
                pltpu.VMEM((latents, lat), F32),
                pltpu.VMEM((block, lat), F32),
                pltpu.VMEM((block, lat), F32),
                pltpu.SemaphoreType.DMA((2 * count,)),
            ],
        ),
        out_shape=[shape((rows * block, lat))] * 2
        + [shape((rows * latents, lat))]
        + [shape((rows * group, lat))] * groups,
        compiler_params=params(1),
        cost_estimate=SMALL,
        name="attend_back",
    )(place, *parts, queries, keys, values, byte_ids, *held.flat)


def weight_grads_call(place, lefts, rights, some_rows, far):
    lat = rights[0][0].shape[1]
    chunk = sum(some_rows)
    left_counts, counts = [len(parts) for parts in lefts], [len(parts) for parts in rights]

    def kernel(place_ref, *refs):
        refs = list(refs)
        take = lambda n: [refs.pop(0) for _ in range(n)]
        left_refs = [take(n) for n in left_counts]
        right_refs = [take(n) for n in counts]
        outs = take(far)
        at = 0
        for index, (left, held) in enumerate(zip((0, 0, 1), refs)):
            factors, column, found = left_refs[left], 0, 0.0
            for part, right in enumerate(right_refs[index]):
                some = right.shape[0]
                if len(factors) > 1:
                    factor = factors[part][...]
                else:
                    factor = factors[0][:, column : column + some]
                found = found + dot(factor, right[...])
                column += some
            held[...] = found.astype(BF)
            some = some_rows[index]
            for distance in range(far):
                owner = jnp.bitwise_xor(place_ref[0], distance)
                outs[distance][at : at + some, :] = held[
                    pl.ds(pl.multiple_of(owner * some, 16), some), :
                ]
            at += some

    tile = lambda i, p: (0, i)
    flat_lefts = [left for parts in lefts for left in parts]
    flat_rights = [right for parts in rights for right in parts]
    return pl.pallas_call(
        kernel,
        grid_spec=pltpu.PrefetchScalarGridSpec(
            num_scalar_prefetch=1,
            grid=(lat // WINDOW,),
            in_specs=[full_block(left.shape) for left in flat_lefts]
            + [pl.BlockSpec((right.shape[0], WINDOW), tile) for right in flat_rights],
            out_specs=[pl.BlockSpec((chunk, WINDOW), tile)] * far,
            scratch_shapes=[pltpu.VMEM((lefts[i][0].shape[0], WINDOW), BF) for i in (0, 0, 1)],
        ),
        out_shape=[shape((chunk, lat))] * far,
        compiler_params=params(1),
        cost_estimate=SMALL,
        name="weight_grads",
    )(place, *flat_lefts, *flat_rights)


def byte_grad_call(place, bytes_flat, grads, held, rows, cuts):
    tokens, width = bytes_flat.shape
    block = tokens // rows
    lat = grads[0][0].shape[1]
    count = len(held.flat)
    shards = place_shards(held)

    def kernel(place_ref, x_ref, *refs):
        grad_refs = refs[: 2 * len(cuts)]
        piece_refs = refs[2 * len(cuts) : 2 * len(cuts) + count]
        out_ref, wk, wv, gains, gain, sems = refs[2 * len(cuts) + count :]
        row = pl.program_id(0)

        def loads():
            return held.copies(
                ("gains", "key", "value"), piece_refs, (gains, wk, wv), place_ref, sems
            )

        @pl.when(row == 0)
        def _():
            run_all(loads(), "start")

        xhat, scale = standardize(x_ref[...].astype(F32))

        @pl.when(row == 0)
        def _():
            run_all(loads(), "wait")
            gain[...] = gain_vector(gains, width, held.lanes["byte"], shards)

        for index, (first, some) in enumerate(cuts):

            @pl.when((row >= first) & (row < first + some))
            def _():
                upstream = dot(grad_refs[2 * index][...], wk[...], ((1,), (1,))) + dot(
                    grad_refs[2 * index + 1][...], wv[...], ((1,), (1,))
                )
                out_ref[...] = norm_pull(upstream, gain[...], xhat, scale)

    row_block = lambda i, p: (i, 0)

    def cut_block(first, some):
        return lambda i, p: (jnp.clip(i - first, 0, some - 1), 0)

    return pl.pallas_call(
        kernel,
        grid_spec=pltpu.PrefetchScalarGridSpec(
            num_scalar_prefetch=1,
            grid=(rows,),
            in_specs=[pl.BlockSpec((block, width), row_block)]
            + [pl.BlockSpec((block, lat), cut_block(*cut)) for cut in cuts for _ in range(2)]
            + [any_spec()] * count,
            out_specs=pl.BlockSpec((block, width), row_block),
            scratch_shapes=[
                pltpu.VMEM((width, lat), BF),
                pltpu.VMEM((width, lat), BF),
                pltpu.VMEM((held.blocks * GAIN_ROWS, LANES), BF),
                pltpu.VMEM((1, width), F32),
                pltpu.SemaphoreType.DMA((6 * count,)),
            ],
        ),
        out_shape=shape((tokens, width), F32),
        compiler_params=params(1),
        cost_estimate=SMALL,
        name="byte_grad",
    )(place, bytes_flat, *[g for some in grads for g in some], *held.flat)


def latent_grad_call(place, latent_message, grad_mixed, ups, held):
    tokens, lat = grad_mixed.shape
    cuts, groups = len(ups), len(ups[0])
    count = len(held.flat)
    shards = place_shards(held)

    def kernel(place_ref, x_ref, mixed_ref, *refs):
        up_refs = [refs[i * groups : (i + 1) * groups] for i in range(cuts)]
        piece_refs = refs[cuts * groups : cuts * groups + count]
        out_ref, gains, sems = refs[cuts * groups + count :]
        loads = held.copies(("gains",), piece_refs, (gains,), place_ref, sems)
        run_all(loads, "start")
        xhat, scale = standardize(x_ref[:, :lat].astype(F32))
        upstream = jnp.concatenate(
            [
                functools.reduce(jnp.add, [ref[...].astype(F32) for ref in some])
                for some in up_refs
            ],
            axis=0,
        )
        run_all(loads, "wait")
        gain = gain_vector(gains, lat, held.lanes["latent"], shards)
        out_ref[...] = mixed_ref[...] + norm_pull(upstream, gain, xhat, scale)

    return pl.pallas_call(
        kernel,
        in_specs=[scalar_spec()]
        + [whole_spec()] * (2 + cuts * groups)
        + [any_spec()] * count,
        out_specs=whole_spec(),
        out_shape=shape((tokens, lat), F32),
        scratch_shapes=[
            pltpu.VMEM((held.blocks * GAIN_ROWS, LANES), BF),
            pltpu.SemaphoreType.DMA((2 * count,)),
        ],
        compiler_params=params(0, 24),
        cost_estimate=SMALL,
        name="latent_grad",
    )(place, latent_message, grad_mixed, *[u for some in ups for u in some], *held.flat)


def swap(value, axis, size, distance):
    return lax.ppermute(value, axis, [(i, i ^ distance) for i in range(size)])


def tie(value, *earlier):
    return lax.optimization_barrier((value, *earlier))[0]


def swap_all(parts, size):
    return [swap(parts[j], "fsdp", size, j) for j in range(1, size)]


def by_index(parts, own, size):
    if len(parts) == 5:
        parts = parts[:3] + [jnp.where((own == 0) | (own == 3), parts[4], parts[3])]
    return [lax.select_n(jnp.bitwise_xor(own, k), *parts) for k in range(size)]


def build_block(place, own, parts, sizes, size):
    segments, first, at = [], 0, 0
    for rows in sizes:
        segments.append((first, rows, at))
        first += rows
        at += rows * size
    total = up_to(at, 16)
    if all(first % 8 == 0 for first, _, _ in segments):
        return assemble_call(place, parts, segments, total, size)
    shards = by_index(parts, own, size)
    found = [s[first : first + rows] for first, rows, _ in segments for s in shards]
    return pad_rows(jnp.concatenate(found, axis=0), total)


def add(*values):
    return functools.reduce(jnp.add, [v.astype(F32) for v in values]).astype(BF)


def meet_call(first, high, second, low, half):
    rows, lat = first[0].shape

    def kernel(a, b, h, c, d, l, one, two):
        one[:half, :] = (a[:half, :].astype(F32) + b[:half, :].astype(F32)).astype(BF)
        one[half:, :] = (
            a[half:, :].astype(F32) + b[half:, :].astype(F32) + h[...].astype(F32)
        ).astype(BF)
        two[:half, :] = (
            c[:half, :].astype(F32) + d[:half, :].astype(F32) + l[...].astype(F32)
        ).astype(BF)
        two[half:, :] = (c[half:, :].astype(F32) + d[half:, :].astype(F32)).astype(BF)

    return pl.pallas_call(
        kernel,
        in_specs=[whole_spec()] * 6,
        out_specs=[whole_spec()] * 2,
        out_shape=[shape((rows, lat))] * 2,
        compiler_params=params(0, 24),
        cost_estimate=SMALL,
        name="meet",
    )(*first, high, *second, low)


def cut_call(place, terms, sizes, size):
    lat = terms[0].shape[1]
    rows = sum(sizes)

    def kernel(place_ref, *refs):
        term_refs, outs, acc = refs[: len(terms)], refs[len(terms) : -1], refs[-1]
        acc[...] = functools.reduce(jnp.add, [ref[...].astype(F32) for ref in term_refs])
        for distance, out in enumerate(outs):
            owner = jnp.bitwise_xor(place_ref[1], distance)
            found, at = [], 0
            for some in sizes:
                found.append(acc[pl.ds(pl.multiple_of(at + owner * some, 8), some), :])
                at += some * size
            out[...] = jnp.concatenate(found, axis=0).astype(out.dtype)

    return pl.pallas_call(
        kernel,
        in_specs=[scalar_spec()] + [whole_spec()] * len(terms),
        out_specs=[whole_spec()] * size,
        out_shape=[shape((rows, lat), F32)] + [shape((rows, lat))] * (size - 1),
        scratch_shapes=[pltpu.VMEM(terms[0].shape, F32)],
        compiler_params=params(0, 24),
        cost_estimate=SMALL,
        name="cut",
    )(place, *terms)


def cut_terms(place, own, terms, sizes, size):
    if all(some % 8 == 0 for some in sizes):
        return cut_call(place, terms, sizes, size)
    block = functools.reduce(jnp.add, [v.astype(F32) for v in terms])
    outs = []
    for distance in range(size):
        index = jnp.bitwise_xor(own, distance)
        found, at = [], 0
        for some in sizes:
            part = block[at : at + some * size].reshape(size, some, block.shape[1])
            found.append(lax.dynamic_index_in_dim(part, index, 0, keepdims=False))
            at += some * size
        value = jnp.concatenate(found, axis=0)
        outs.append(value if distance == 0 else value.astype(BF))
    return outs


def total(own, arrived):
    return functools.reduce(jnp.add, [v.astype(F32) for v in [own, *arrived]])


def split_rows(value, sizes):
    found, at = [], 0
    for some in sizes:
        found.append(value[at : at + some])
        at += some
    return found


def up_to(value, step):
    return -(-value // step) * step


def pad_rows(value, rows):
    return jnp.pad(value, ((0, rows - value.shape[0]), (0, 0)))


class Plan:
    def __init__(self, n_dp, n_f):
        self.n_dp, self.n_f = n_dp, n_f
        self.gate = ()

    def send(self, value, distance):
        return swap(tie(value, *self.gate), "dp", self.n_dp, distance)

    def pass_on(self, value, distance):
        return swap(tie(value, *self.gate), "fsdp", self.n_f, distance)

    def relay(self, own, two):
        middle = lax.ppermute(tie(own, *self.gate), "fsdp", [(1, 2), (2, 1)])
        return middle, lax.ppermute(tie(two, *self.gate), "fsdp", [(2, 3), (1, 0)])

    def spread(self, value):
        value = tie(value, *self.gate)
        middle = lax.ppermute(value, "fsdp", [(1, 2), (2, 1)])
        return middle, lax.ppermute(value, "fsdp", [(3, 2), (0, 1)])

    def tied(self, values):
        return [tie(values[0], *self.gate), *values[1:]]


def square_pieces(block, chips, half):
    rows = block.shape[0]
    full, halves = [(0, rows)], [(0, half), (half, rows)]
    pieces, flat = [], []
    for distance, parts, pairs in (
        (0, full, chips[:1]),
        (2, full, chips[1:2]),
        (4, full, chips[2:3]),
        (6, halves, chips[3:]),
    ):
        for core in range(2):
            pieces.append((distance + core, parts))
            flat.extend(pair[core] for pair in pairs)
    return pieces, flat


def local(n_dp, n_f, bytes_in, latents_in, cotangent, byte_segments, latent_segments,
          w_query, w_key, w_value, w_out, w_mlp_in, w_mlp_out,
          gain_latent, gain_byte, gain_mlp):
    rows, byte_local, width = bytes_in.shape
    _, group, lat = latents_in.shape
    dp, own = lax.axis_index("dp"), lax.axis_index("fsdp")
    place = jnp.stack([dp, own]).astype(jnp.int32)
    bytes_flat = bytes_in.reshape(rows * byte_local, width)
    latents_flat = latents_in.reshape(rows * group, lat)
    cot_flat = cotangent.reshape(rows * group, lat)
    kr, qr = w_key.shape[0], w_query.shape[0]
    key_rows, query_rows = n_f * kr, n_f * qr
    cuts = [(0, 1), (1, rows - 1)]
    cut_rows = [(first * group, some * group) for first, some in cuts]

    gains = jnp.concatenate([gain_latent, gain_byte, gain_mlp])
    gains = jnp.pad(gains, (0, lat - gains.shape[0]))[None, :]
    message_one = jnp.concatenate([w_key, w_value, w_query, gains], axis=0)
    message_one = pad_rows(message_one, up_to(2 * kr + qr + 1, 16))
    message_two = jnp.concatenate([w_out, w_mlp_in, w_mlp_out], axis=0)
    ids = latent_segments.reshape(rows * group, 1).astype(BF)
    ids = jnp.pad(ids, ((0, 0), (0, LANES - 1)))
    latent_message = jnp.concatenate([latents_flat, ids], axis=1)
    byte_ids = lax.dynamic_slice_in_dim(byte_segments, own * byte_local, byte_local, axis=1)
    byte_ids = byte_ids.astype(F32)
    byte_row, byte_column = byte_ids[:, None, :], byte_ids[:, :, None]
    sizes_one, sizes_two = (kr, kr, qr), (qr, qr, qr)
    half_one, half_two = 2 * key_rows, up_to(3 * query_rows // 2, 16)
    spans_one = {
        "key": (0, key_rows),
        "value": (key_rows, key_rows),
        "query": (2 * key_rows, query_rows),
        "gains": (2 * key_rows + query_rows, GAIN_ROWS),
    }
    spans_two = {name: (i * query_rows, query_rows) for i, name in enumerate(("out", "inner", "outer"))}

    def held_one(pieces, flat):
        held = Held(pieces, flat, spans_one)
        held.blocks, held.size = n_dp, n_f
        held.lanes = {"latent": 0, "byte": qr, "mlp": qr + kr}
        return held

    def key_value(one, bytes_flat):
        return key_value_call(place, bytes_flat, one, rows)

    def attend(index, one, parts, keys, values):
        found = attend_call(
            place, parts, byte_row, keys, values, one, n_f, group, *cuts[index]
        )
        return found[0], found[1], found[2:]

    def feed(one, two, attended):
        return feed_call(place, attended, latent_message, cot_flat, one, two, cut_rows)

    def feed_grads(lefts, rights):
        return feed_grads_call(place, lefts, rights, query_rows, n_dp)

    def attend_back(index, one, parts, saved):
        return attend_back_call(
            place, parts, *saved, byte_column, one, n_f, group, *cuts[index]
        )

    def weight_grads(lefts, first, last):
        return weight_grads_call(
            place, lefts, list(zip(first, last)), (key_rows, key_rows, query_rows), n_dp
        )

    def byte_grad(one, grads):
        return byte_grad_call(place, bytes_flat, grads, one, rows, cuts)

    run = square if (n_dp, n_f) == (8, 4) else plain
    new, grad_latents, grad_bytes, grad_one, grad_two = run(**locals())

    def gain_grad(pairs, gain):
        found = sum(jnp.sum(w.astype(F32) * g, axis=1) for w, g in pairs)
        return found / gain.astype(F32)

    grad_key, grad_value, grad_query = split_rows(grad_one, sizes_one)
    grad_out, grad_inner, grad_outer = split_rows(grad_two, sizes_two)
    return (
        new.reshape(rows, group, lat),
        grad_latents.reshape(rows, group, lat),
        grad_bytes.reshape(rows, byte_local, width),
        grad_query,
        grad_key,
        grad_value,
        grad_out,
        grad_inner,
        grad_outer,
        gain_grad([(w_query, grad_query)], gain_latent),
        gain_grad([(w_key, grad_key), (w_value, grad_value)], gain_byte),
        gain_grad([(w_mlp_in, grad_inner)], gain_mlp),
    )


def plain(*, n_dp, n_f, place, own, bytes_flat, message_one, message_two, latent_message,
          sizes_one, sizes_two, spans_two, cot_flat, held_one, key_value, attend, feed,
          feed_grads, attend_back, weight_grads, byte_grad, **_):
    def gather(message, sizes):
        parts = [message, *swap_all([message] * n_f, n_f)]
        block = build_block(place, own, parts, sizes, n_f)
        flat = [block] + [swap(block, "dp", n_dp, d) for d in range(1, n_dp)]
        return [(d, [(0, block.shape[0])]) for d in range(n_dp)], flat

    def scatter(parts, sizes):
        terms = [parts[0]] + [swap(parts[d], "dp", n_dp, d) for d in range(1, n_dp)]
        cut = cut_terms(place, own, terms, sizes, n_f)
        return total(cut[0], swap_all(cut, n_f))

    one = held_one(*gather(message_one, (*sizes_one, 1)))
    two = Held(*gather(message_two, sizes_two), spans_two)
    byte_t, keys, values = key_value(one, bytes_flat)
    latent_parts = [latent_message, *swap_all([latent_message] * n_f, n_f)]
    latent_t, queries, found = zip(*[attend(i, one, latent_parts, keys, values) for i in range(2)])
    attended = list(zip(*[[f[0], *swap_all(f, n_f)] for f in found]))
    new, grad_mixed, *messages, attended_t, branch, normed_t, inner, act_t = feed(
        one, two, attended
    )
    grad_two = scatter(feed_grads((attended_t, normed_t, act_t), (branch, inner, cot_flat)), sizes_two)
    parts = [[m, *swap_all([m] * n_f, n_f)] for m in messages]
    first, last = [attend_back(i, one, parts[i], (queries[i], keys, values)) for i in range(2)]
    grad_bytes = byte_grad(one, (first[:2], last[:2]))
    grad_one = scatter(weight_grads(((byte_t,), latent_t), first[:3], last[:3]), sizes_one)
    ups = [[ups[0], *swap_all(ups, n_f)] for ups in (first[3:], last[3:])]
    grad_latents = latent_grad_call(place, latent_message, grad_mixed, ups, one)
    return new, grad_latents, grad_bytes, grad_one, grad_two


def square(*, n_dp, n_f, place, own, bytes_flat, message_one, message_two, latent_message,
           sizes_one, sizes_two, spans_two, half_one, half_two, cot_flat, held_one, key_value,
           attend, feed, feed_grads, attend_back, weight_grads, byte_grad, **_):
    plan = Plan(n_dp, n_f)
    send, pass_on = plan.send, plan.pass_on

    near = [pass_on(message_one, 2), pass_on(message_one, 1)]
    plan.gate = near
    parts = [message_one, near[1], near[0], *plan.relay(message_one, near[0])]
    block = build_block(place, own, parts, (*sizes_one, 1), n_f)
    plan.gate = [block]
    x, y, other = send(block, 2), send(block, 4), send(block, 1)
    latent_two, latent_one = pass_on(latent_message, 2), pass_on(latent_message, 1)
    plan.gate = [x, y, other, latent_two, latent_one]
    low, high = send(x[:half_one], 4), send(y[half_one:], 2)
    latent_parts = [
        latent_message, latent_one, latent_two, *plan.relay(latent_message, latent_two)
    ]
    x_other = send(x, 1)
    y_other = send(tie(y, x_other), 1)
    plan.gate = [low, high, y_other, *latent_parts[3:]]
    low_other, high_other = send(low, 1), send(high, 1)
    pairs = [(block, other), (x, x_other), (y, y_other), (low, low_other), (high, high_other)]
    one = held_one(*square_pieces(block, pairs, half_one))
    two_two, two_one = pass_on(message_two, 2), pass_on(message_two, 1)
    plan.gate = [low_other, high_other]
    byte_t, keys, values = key_value(one, tie(bytes_flat, *plan.gate))
    plan.gate = [two_two, two_one, keys]
    parts = [message_two, two_one, two_two, *plan.relay(message_two, two_two)]
    latent_t_first, queries_first, found = attend(0, one, plan.tied(latent_parts), keys, values)
    plan.gate = [queries_first, *parts[3:]]
    block = build_block(place, own, plan.tied(parts), sizes_two, n_f)
    x, y = send(block, 2), send(block, 4)
    attended_first = [found[0], *[pass_on(found[j], j) for j in range(1, n_f)]]
    plan.gate = [block]
    latent_t_last, queries_last, found = attend(1, one, plan.tied(latent_parts), keys, values)
    plan.gate = attended_first[1:]
    attended_last = [found[0], *[pass_on(found[j], j) for j in range(1, n_f)]]
    plan.gate = [x, y, queries_last, *attended_first[1:]]
    low, high = send(x[:half_two], 4), send(y[half_two:], 2)
    plan.gate = [low, high, *attended_last[1:]]
    pairs = [(v, send(v, 1)) for v in (block, x, y, low, high)]
    two = Held(*square_pieces(block, pairs, half_two), spans_two)
    new, grad_mixed, first, last, attended_t, branch, normed_t, inner, act_t = feed(
        one, two, list(zip(attended_first, attended_last))
    )
    plan.gate = []
    near = [pass_on(first, 2), pass_on(first, 1)]
    grads = feed_grads((attended_t, normed_t, act_t), (branch, inner, cot_flat))
    plan.gate = near
    first_parts = [first, near[1], near[0], *plan.relay(first, near[0])]
    arrived = {d: send(grads[d + 1], 1) for d in (6, 4, 2)}
    plan.gate = [*arrived.values(), *first_parts[3:]]
    low = add(tie(grads[6][:half_two], *plan.gate), arrived[6][:half_two])
    high = add(tie(grads[6][half_two:], *plan.gate), arrived[6][half_two:])
    low, high = send(low, 2), send(high, 4)
    near = [pass_on(last, 2), pass_on(last, 1)]
    arrived[0] = send(grads[1], 1)
    back_first = attend_back(0, one, plan.tied(first_parts), (queries_first, keys, values))
    plan.gate = [low, high, arrived[0], *near, back_first[0]]
    last_parts = [last, near[1], near[0], *plan.relay(last, near[0])]
    x, y = meet_call(
        (grads[2], arrived[2]), tie(high, *plan.gate), (grads[4], arrived[4]), low, half_two
    )
    plan.gate = [x, y]
    terms_two = [grads[0], arrived[0], send(x, 2), send(y, 4)]
    plan.gate = [x, y, *last_parts[3:]]
    ups_first = back_first[3:]
    ups_first = [ups_first[0], *[pass_on(ups_first[j], j) for j in range(1, n_f)]]
    back_last = attend_back(1, one, plan.tied(last_parts), (queries_last, keys, values))
    plan.gate = [back_last[0], *ups_first[1:], *terms_two[2:]]
    cut_two = cut_terms(place, own, plan.tied(terms_two), sizes_two, n_f)
    ups = back_last[3:]
    plan.gate = [cut_two[0]]
    near = [pass_on(ups[1], 1), *plan.spread(ups[3])]
    arrived_two = [pass_on(cut_two[1], 1), pass_on(cut_two[3], 3)]
    grads = weight_grads(
        ((byte_t,), (latent_t_first, latent_t_last)),
        back_first[:3],
        [tie(back_last[0], *plan.gate), *back_last[1:3]],
    )
    plan.gate = [*near, grads[0]]
    arrived = {d: send(grads[d + 1], 1) for d in (6, 4, 2)}
    low = add(grads[6][:half_one], arrived[6][:half_one])
    high = add(grads[6][half_one:], arrived[6][half_one:])
    merged = add(tie(ups[2], *plan.gate), near[2])
    plan.gate = [low, high, merged, *arrived.values()]
    low, high = send(low, 2), send(high, 4)
    ups_last = [ups[0], *near[:2], pass_on(merged, 2)]
    plan.gate = [low, high, *arrived_two]
    x, y = meet_call(
        (grads[2], arrived[2]), tie(high, *plan.gate), (grads[4], arrived[4]), low, half_one
    )
    plan.gate = [x, y]
    arrived[0] = send(grads[1], 1)
    terms_one = [grads[0], arrived[0], send(x, 2), send(y, 4)]
    arrived_two.append(pass_on(cut_two[2], 2))
    grad_bytes = byte_grad(one, (plan.tied(back_first[:2]), back_last[:2]))
    plan.gate = [*terms_one[2:], grad_bytes, arrived_two[-1], ups_last[-1]]
    cut_one = cut_terms(place, own, plan.tied(terms_one), sizes_one, n_f)
    plan.gate = [cut_one[0]]
    grad_one = total(cut_one[0], [pass_on(cut_one[j], j) for j in range(1, n_f)])
    grad_two = total(cut_two[0], arrived_two)
    grad_latents = latent_grad_call(
        place, latent_message, tie(grad_mixed, *plan.gate), [ups_first, ups_last], one
    )
    return new, grad_latents, grad_bytes, grad_one, grad_two


def solution(mesh):
    rows3 = P("dp", "fsdp", None)
    split2 = P(("dp", "fsdp"), None)
    split1 = P(("dp", "fsdp"))
    in_specs = (rows3,) * 3 + (P("dp", None), P("dp", "fsdp")) + (split2,) * 6 + (split1,) * 3
    out_specs = (rows3,) * 3 + (split2,) * 6 + (split1,) * 3
    body = functools.partial(local, mesh.shape["dp"], mesh.shape["fsdp"])
    return jax.shard_map(
        body, mesh=mesh, in_specs=in_specs, out_specs=out_specs, check_vma=False
    )
```

```python
import functools
import math

import jax
import jax.numpy as jnp
from jax import lax
from jax.experimental import pallas as pl
from jax.experimental.pallas import tpu as pltpu
from jax.sharding import PartitionSpec as P

HEADS = 8
HEAD_DIM = 160
EPSILON = 1e-05
NEG_FILL = -1e30
LANES = 128
WINDOW = 256
BF = jnp.bfloat16
F32 = jnp.float32
GAIN_ROWS = 16
SMALL = pl.CostEstimate(flops=1, bytes_accessed=1, transcendentals=0)


def head_window(head):
    start = head * HEAD_DIM // LANES * LANES
    return start, head * HEAD_DIM - start


def head_lanes(head):
    _, shift = head_window(head)
    lane = lax.broadcasted_iota(jnp.int32, (1, WINDOW), 1)
    return (lane >= shift) & (lane < shift + HEAD_DIM)


def dot(a, b, dims=((1,), (0,))):
    return lax.dot_general(a, b, (dims, ((), ())), preferred_element_type=F32)


def standardize(values):
    centered = values - jnp.mean(values, axis=-1, keepdims=True)
    scale = lax.rsqrt(jnp.mean(centered * centered, axis=-1, keepdims=True) + EPSILON)
    return centered * scale, scale


def norm_pull(upstream, gain, xhat, scale):
    scaled = upstream * gain
    return scale * (
        scaled
        - jnp.mean(scaled, axis=-1, keepdims=True)
        - xhat * jnp.mean(scaled * xhat, axis=-1, keepdims=True)
    )


def split_three(values):
    first = values.astype(BF).astype(F32)
    rest = values - first
    second = rest.astype(BF).astype(F32)
    return first, second, rest - second


def gelu(values):
    inner = math.sqrt(2 / math.pi) * (values + 0.044715 * values * values * values)
    return 0.5 * values * (1.0 + jnp.tanh(inner))


def gelu_slope(values):
    square = values * values
    tanh = jnp.tanh(math.sqrt(2 / math.pi) * (values + 0.044715 * square * values))
    slope = math.sqrt(2 / math.pi) * (1.0 + 3 * 0.044715 * square)
    return 0.5 * (1.0 + tanh) + 0.5 * values * (1.0 - tanh * tanh) * slope


def piece_copies(pieces, flat_refs, first, rows, target, me, sems, base):
    copies = []
    lanes = target.shape[1]
    at = 0
    for distance, parts in pieces:
        owner = jnp.bitwise_xor(me, distance)
        for low, high in parts:
            ref = flat_refs[at]
            at += 1
            start, stop = max(low, first), min(high, first + rows)
            if start < stop:
                place = pl.multiple_of(owner * rows + (start - first), 16)
                copies.append(
                    pltpu.make_async_copy(
                        ref.at[pl.ds(start - low, stop - start), pl.ds(0, lanes)],
                        target.at[pl.ds(place, stop - start), :],
                        sems.at[base + len(copies)],
                    )
                )
    return copies


def group_values(refs, place):
    if len(refs) != 5:
        return [ref[...] for ref in refs]
    own = place[1]
    at_end = (own == 0) | (own == 3)
    values = [ref[...] for ref in refs[:3]]
    return values + [jnp.where(at_end, refs[4][...], refs[3][...])]


def gain_vector(held, size, lane_at, shards):
    per_shard = size // shards
    blocks = held.shape[0] // GAIN_ROWS
    per_block = shards // blocks
    lane = lax.broadcasted_iota(jnp.int32, (LANES, size), 0)
    column = lax.broadcasted_iota(jnp.int32, (LANES, size), 1)
    pick = (lane == lane_at + column % per_shard).astype(F32).astype(BF)
    spread = dot(held[...], pick)
    row = lax.broadcasted_iota(jnp.int32, spread.shape, 0)
    column = lax.broadcasted_iota(jnp.int32, spread.shape, 1) // per_shard
    owner = (row // GAIN_ROWS) * per_block + row % GAIN_ROWS
    right = (owner == column) & (row % GAIN_ROWS < per_block)
    return jnp.sum(jnp.where(right, spread, 0.0), axis=0, keepdims=True)


def params(grid_rank, mebibytes=60):
    return pltpu.CompilerParams(
        dimension_semantics=("arbitrary",) * grid_rank, vmem_limit_bytes=mebibytes << 20
    )


def whole_spec():
    return pl.BlockSpec(memory_space=pltpu.VMEM)


def any_spec():
    return pl.BlockSpec(memory_space=pltpu.HBM)


class Held:
    def __init__(self, pieces, flat, spans):
        self.pieces, self.flat, self.spans = pieces, flat, spans

    def crossed(self):
        at = 0
        for distance, parts in self.pieces:
            if distance == self.blocks - 2:
                return self.flat[at : at + len(parts)]
            at += len(parts)

    def copies(self, names, refs, targets, place, sems):
        found, base = [], 0
        for name, target in zip(names, targets):
            first, rows = self.spans[name]
            some = piece_copies(self.pieces, refs, first, rows, target, place[0], sems, base)
            base += len(some)
            found.append(some)
        return found


def run_all(groups, action):
    for group in groups:
        for copy in group:
            getattr(copy, action)()


def shape(dims, dtype=BF):
    return jax.ShapeDtypeStruct(dims, dtype)


def full_block(dims):
    return pl.BlockSpec(
        dims, lambda i, p: (0,) * len(dims), pipeline_mode=pl.Buffered(buffer_count=1)
    )


def scalar_spec():
    return pl.BlockSpec(memory_space=pltpu.SMEM)


def assemble_call(place, parts, segments, total, size):
    def kernel(place_ref, *refs):
        part_refs, out_ref, acc = refs[: len(parts)], refs[len(parts)], refs[len(parts) + 1]
        values = [v.astype(F32) for v in group_values(part_refs, place_ref)]
        end = max(at + size * rows for _, rows, at in segments)
        if end < total:
            first = end // 8 * 8
            acc[first:, :] = jnp.zeros((total - first, acc.shape[1]), F32)
        for index in range(size):
            want = jnp.bitwise_xor(place_ref[1], index)
            value = values[size - 1]
            for distance in range(size - 2, -1, -1):
                value = jnp.where(want == distance, values[distance], value)
            for first, rows, at in segments:
                acc[at + index * rows : at + (index + 1) * rows, :] = value[first : first + rows]
        out_ref[...] = acc[...].astype(BF)

    lat = parts[0].shape[1]
    return pl.pallas_call(
        kernel,
        in_specs=[scalar_spec()] + [whole_spec()] * len(parts),
        out_specs=whole_spec(),
        out_shape=shape((total, lat)),
        scratch_shapes=[pltpu.VMEM((total, lat), F32)],
        compiler_params=params(0, 24),
        cost_estimate=SMALL,
        name="assemble",
    )(place, *parts)


def key_value_call(place, bytes_flat, held, rows):
    tokens, width = bytes_flat.shape
    block = tokens // rows
    lat = held.flat[0].shape[1]
    count = len(held.flat)
    shards = place_shards(held)

    def kernel(place_ref, x_ref, *refs):
        piece_refs = refs[:count]
        normed_t_ref, key_ref, value_ref, wk, wv, gains, gain, sems = refs[count:]
        first = pl.program_id(0) == 0

        def loads():
            return held.copies(
                ("gains", "key", "value"), piece_refs, (gains, wk, wv), place_ref, sems
            )

        @pl.when(first)
        def _():
            run_all(loads(), "start")

        xhat, _ = standardize(x_ref[...].astype(F32))

        @pl.when(first)
        def _():
            run_all(loads(), "wait")
            gain[...] = gain_vector(gains, width, held.lanes["byte"], shards)

        normed = (xhat * gain[...]).astype(BF)
        key_ref[...] = dot(normed, wk[...]).astype(BF)
        value_ref[...] = dot(normed, wv[...]).astype(BF)
        normed_t_ref[...] = jnp.transpose(normed, (1, 0))

    row_block = lambda i, p: (i, 0)
    return pl.pallas_call(
        kernel,
        grid_spec=pltpu.PrefetchScalarGridSpec(
            num_scalar_prefetch=1,
            grid=(rows,),
            in_specs=[pl.BlockSpec((block, width), row_block)] + [any_spec()] * count,
            out_specs=[
                pl.BlockSpec((width, block), lambda i, p: (0, i)),
                pl.BlockSpec((block, lat), row_block),
                pl.BlockSpec((block, lat), row_block),
            ],
            scratch_shapes=[
                pltpu.VMEM((width, lat), BF),
                pltpu.VMEM((width, lat), BF),
                pltpu.VMEM((held.blocks * GAIN_ROWS, LANES), BF),
                pltpu.VMEM((1, width), F32),
                pltpu.SemaphoreType.DMA((6 * count,)),
            ],
        ),
        out_shape=[shape((width, tokens)), shape((tokens, lat)), shape((tokens, lat))],
        compiler_params=params(1),
        cost_estimate=SMALL,
        name="keys_values",
    )(place, bytes_flat, *held.flat)


def place_shards(held):
    return held.blocks * held.size


def attend_call(place, latent_parts, byte_ids, keys, values, held, groups, group, first, rows):
    parts = len(latent_parts)
    lat = keys.shape[1]
    block = byte_ids.shape[2]
    latents = groups * group
    count = len(held.flat)
    shards = place_shards(held)
    score_scale = 1.0 / math.sqrt(HEAD_DIM)

    def kernel(place_ref, *refs):
        part_refs = refs[:parts]
        bid_ref, key_ref, value_ref = refs[parts : parts + 3]
        piece_refs = refs[parts + 3 : parts + 3 + count]
        rest = refs[parts + 3 + count :]
        normed_t_ref, query_ref = rest[:2]
        out_refs = rest[2 : 2 + groups]
        wq, gains, gain, acc, sems = rest[2 + groups :]
        start = pl.program_id(0) == 0

        def loads():
            return held.copies(("gains", "query"), piece_refs, (gains, wq), place_ref, sems)

        @pl.when(start)
        def _():
            run_all(loads(), "start")

        message = jnp.concatenate(group_values(part_refs, place_ref), axis=0)
        ids = message[:, lat : lat + 1].astype(F32)
        xhat, _ = standardize(message[:, :lat].astype(F32))

        @pl.when(start)
        def _():
            run_all(loads(), "wait")
            gain[...] = gain_vector(gains, lat, held.lanes["latent"], shards)

        normed = (xhat * gain[...]).astype(BF)
        query_ref[...] = dot(normed, wq[...]).astype(BF)
        normed_t_ref[...] = jnp.transpose(normed, (1, 0))
        allowed = ids == bid_ref[0]
        lane = lax.broadcasted_iota(jnp.int32, (latents, LANES), 1)
        stats = jnp.zeros((latents, LANES), F32)
        for head in range(HEADS):
            at, _ = head_window(head)
            mask = head_lanes(head)
            window = slice(at, at + WINDOW)
            query = jnp.where(mask, query_ref[:, window], jnp.zeros((), BF))
            scores = dot(query, key_ref[:, window], ((1,), (1,))) * score_scale
            scores = jnp.where(allowed, scores, NEG_FILL)
            top = jnp.max(scores, axis=-1, keepdims=True)
            exponent = jnp.exp(scores - top)
            total = jnp.sum(exponent, axis=-1, keepdims=True)
            found = dot(exponent.astype(BF), value_ref[:, window]) / total
            if head == 0:
                acc[:, window] = found
            else:
                acc[:, window] = jnp.where(mask, found, acc[:, window])
            log_total = jnp.where(top > -1e29, top + jnp.log(total), NEG_FILL)
            for index, term in enumerate(split_three(log_total)):
                stats = jnp.where(lane == index * HEADS + head, term, stats)
        for index, ref in enumerate(out_refs):
            chunk = slice(index * group, (index + 1) * group)
            ref[:, :lat] = acc[chunk, :].astype(BF)
            ref[:, lat:] = stats[chunk, :].astype(BF)

    row_block = lambda i, p: (first + i, 0)
    own_block = lambda i, p: (i, 0)
    return pl.pallas_call(
        kernel,
        grid_spec=pltpu.PrefetchScalarGridSpec(
            num_scalar_prefetch=1,
            grid=(rows,),
            in_specs=[pl.BlockSpec((group, lat + LANES), row_block)] * parts
            + [
                pl.BlockSpec((1, 1, block), lambda i, p: (first + i, 0, 0)),
                pl.BlockSpec((block, lat), row_block),
                pl.BlockSpec((block, lat), row_block),
            ]
            + [any_spec()] * count,
            out_specs=[
                pl.BlockSpec((lat, latents), lambda i, p: (0, i)),
                pl.BlockSpec((latents, lat), own_block),
            ]
            + [pl.BlockSpec((group, lat + LANES), own_block)] * groups,
            scratch_shapes=[
                pltpu.VMEM((lat, lat), BF),
                pltpu.VMEM((held.blocks * GAIN_ROWS, LANES), BF),
                pltpu.VMEM((1, lat), F32),
                pltpu.VMEM((latents, lat), F32),
                pltpu.SemaphoreType.DMA((4 * count,)),
            ],
        ),
        out_shape=[shape((lat, rows * latents)), shape((rows * latents, lat))]
        + [shape((rows * group, lat + LANES))] * groups,
        compiler_params=params(1),
        cost_estimate=SMALL,
        name="attend",
    )(place, *latent_parts, byte_ids, keys, values, *held.flat)


def feed_call(place, parts, latent_message, cot_flat, held_gain, held, cuts):
    groups, pieces_of = len(parts), len(parts[0])
    tokens, lat = cot_flat.shape
    count, gain_count = len(held.flat), len(held_gain.flat)
    shards = place_shards(held_gain)

    def kernel(place_ref, *refs):
        refs = list(refs)
        take = lambda n: [refs.pop(0) for _ in range(n)]
        part_refs = [take(pieces_of) for _ in range(groups)]
        x_ref, cot_ref = take(2)
        gain_refs, piece_refs = take(gain_count), take(count)
        new_ref, mixed_grad_ref = take(2)
        message_refs = take(len(cuts))
        attended_t, branch, normed_t, inner, act_t = take(5)
        wo, w1, w2, gains, sems, gain_sems = refs
        gain_loads = held_gain.copies(("gains",), gain_refs, (gains,), place_ref, gain_sems)
        loads = held.copies(("out", "inner", "outer"), piece_refs, (wo, w1, w2), place_ref, sems)
        run_all(gain_loads, "start")
        run_all(loads, "start")

        lane = lax.broadcasted_iota(jnp.int32, (LANES, lat), 0)
        column = lax.broadcasted_iota(jnp.int32, (LANES, lat), 1)
        spread = jnp.zeros((LANES, lat), jnp.bool_)
        for head in range(HEADS):
            inside = (column >= head * HEAD_DIM) & (column < (head + 1) * HEAD_DIM)
            own = (lane == head) | (lane == HEADS + head) | (lane == 2 * HEADS + head)
            spread = spread | (inside & own)
        spread = spread.astype(F32).astype(BF)
        found = [jnp.concatenate([ref[...] for ref in some], axis=0) for some in part_refs]
        logs = [dot(value[:, lat:], spread) for value in found]
        top = functools.reduce(jnp.maximum, logs)
        shares = [jnp.exp(log - top) for log in logs]
        total = functools.reduce(jnp.add, shares)
        summed = functools.reduce(
            jnp.add, [s * value[:, :lat].astype(F32) for s, value in zip(shares, found)]
        )
        attended = (summed / total).astype(BF)
        log_total = top + jnp.log(total)
        attended_t[...] = jnp.transpose(attended, (1, 0))

        run_all(gain_loads, "wait")
        gain = gain_vector(gains, lat, held_gain.lanes["mlp"], shards)
        run_all(loads[:1], "wait")
        mixed = x_ref[:, :lat].astype(F32) + dot(attended, wo[...])
        xhat, scale = standardize(mixed)
        normed = (xhat * gain).astype(BF)
        normed_t[...] = jnp.transpose(normed, (1, 0))
        run_all(loads[1:2], "wait")
        hidden = dot(normed, w1[...])
        activated = gelu(hidden).astype(BF)
        act_t[...] = jnp.transpose(activated, (1, 0))
        run_all(loads[2:], "wait")
        new_ref[...] = (mixed + dot(activated, w2[...])).astype(BF)
        cot = cot_ref[...]
        grad_hidden = (dot(cot, w2[...], ((1,), (1,))) * gelu_slope(hidden)).astype(BF)
        inner[...] = grad_hidden
        upstream = dot(grad_hidden, w1[...], ((1,), (1,)))
        grad_mixed = cot.astype(F32) + norm_pull(upstream, gain, xhat, scale)
        mixed_grad_ref[...] = grad_mixed
        grad_branch = grad_mixed.astype(BF)
        branch[...] = grad_branch
        grad_attended = dot(grad_branch, wo[...], ((1,), (1,))).astype(BF)
        product = grad_attended.astype(F32) * attended.astype(F32)
        out_lane = lax.broadcasted_iota(jnp.int32, (tokens, LANES), 1)
        ids = x_ref[:, lat : lat + 1].astype(F32)
        stats = jnp.where(out_lane == 6 * HEADS, ids, 0.0)
        for head in range(HEADS):
            at, shift = head_window(head)
            mask = head_lanes(head)
            inner_sum = jnp.sum(
                jnp.where(mask, product[:, at : at + WINDOW], 0.0), axis=-1, keepdims=True
            )
            first_lane = at + shift
            log_column = log_total[:, first_lane : first_lane + 1]
            terms = split_three(log_column) + split_three(inner_sum)
            for index, term in enumerate(terms):
                stats = jnp.where(out_lane == index * HEADS + head, term, stats)
        stats = stats.astype(BF)
        for (first, some), ref in zip(cuts, message_refs):
            ref[:, :lat] = grad_attended[first : first + some]
            ref[:, lat:] = stats[first : first + some]

    flat_parts = [array for some in parts for array in some]
    return pl.pallas_call(
        kernel,
        in_specs=[scalar_spec()]
        + [whole_spec()] * (len(flat_parts) + 2)
        + [any_spec()] * (gain_count + count),
        out_specs=[whole_spec()] * (7 + len(cuts)),
        out_shape=[shape((tokens, lat)), shape((tokens, lat), F32)]
        + [shape((some, lat + LANES)) for _, some in cuts]
        + [
            shape((lat, tokens)),
            shape((tokens, lat)),
            shape((lat, tokens)),
            shape((tokens, lat)),
            shape((lat, tokens)),
        ],
        scratch_shapes=[pltpu.VMEM((lat, lat), BF)] * 3
        + [
            pltpu.VMEM((held_gain.blocks * GAIN_ROWS, LANES), BF),
            pltpu.SemaphoreType.DMA((6 * count,)),
            pltpu.SemaphoreType.DMA((2 * gain_count,)),
        ],
        compiler_params=params(0),
        cost_estimate=SMALL,
        name="feed",
    )(place, *flat_parts, latent_message, cot_flat, *held_gain.flat, *held.flat)


def feed_grads_call(place, lefts, rights, n, far):
    lat, tokens = lefts[0].shape
    width = rights[0].shape[1]
    terms = len(lefts)

    def kernel(place_ref, *refs):
        left_refs, right_refs = refs[:terms], refs[terms : 2 * terms]
        outs = refs[2 * terms :]
        for distance in range(far):
            at = pl.multiple_of(jnp.bitwise_xor(place_ref[0], distance) * n, 16)
            for index in range(terms):
                chunk = left_refs[index][pl.ds(at, n), :]
                outs[distance][index * n : (index + 1) * n, :] = dot(
                    chunk, right_refs[index][...]
                ).astype(BF)

    return pl.pallas_call(
        kernel,
        in_specs=[scalar_spec()] + [whole_spec()] * (2 * terms),
        out_specs=[whole_spec()] * far,
        out_shape=[shape((terms * n, width))] * far,
        compiler_params=params(0),
        cost_estimate=SMALL,
        name="feed_grads",
    )(place, *lefts, *rights)


def attend_back_call(
    place, parts, queries, keys, values, byte_ids, held, groups, group, first, rows
):
    count_parts = len(parts)
    lat = keys.shape[1]
    block = byte_ids.shape[2]
    latents = groups * group
    count = len(held.flat)
    score_scale = 1.0 / math.sqrt(HEAD_DIM)

    def kernel(place_ref, *refs):
        refs = list(refs)
        take = lambda n: [refs.pop(0) for _ in range(n)]
        part_refs = take(count_parts)
        query_ref, key_ref, value_ref, bid_ref = take(4)
        piece_refs = take(count)
        grad_key_ref, grad_value_ref, grad_query_ref = take(3)
        up_refs = take(groups)
        wq, acc_q, acc_k, acc_v, sems = refs
        row = pl.program_id(0)

        def loads():
            return held.copies(("query",), piece_refs, (wq,), place_ref, sems)

        @pl.when(row == 0)
        def _():
            run_all(loads(), "start")

        message = jnp.concatenate(group_values(part_refs, place_ref), axis=0)
        stats = jnp.transpose(message[:, lat:].astype(F32), (1, 0))
        byte_ids = jnp.transpose(jnp.broadcast_to(bid_ref[0], (LANES, block)), (1, 0))[:, :1]
        allowed = byte_ids == stats[6 * HEADS : 6 * HEADS + 1, :]
        for head in range(HEADS):
            at, _ = head_window(head)
            mask = head_lanes(head)
            window = slice(at, at + WINDOW)
            stat = lambda k: stats[k * HEADS + head : k * HEADS + head + 1, :]
            log_total = stat(0) + stat(1) + stat(2)
            inner_sum = stat(3) + stat(4) + stat(5)
            query = jnp.where(mask, query_ref[:, window], jnp.zeros((), BF))
            grad = jnp.where(mask, message[:, window], jnp.zeros((), BF))
            key = key_ref[:, window]
            scores = dot(key, query, ((1,), (1,))) * score_scale
            probs = jnp.exp(jnp.where(allowed, scores - log_total, NEG_FILL))
            grad_probs = dot(value_ref[:, window], grad, ((1,), (1,)))
            grad_scores = (probs * (grad_probs - inner_sum)).astype(BF)
            found_k = dot(grad_scores, query)
            found_v = dot(probs.astype(BF), grad)
            found_q = dot(grad_scores, key, ((0,), (0,)))
            if head == 0:
                acc_k[:, window] = found_k
                acc_v[:, window] = found_v
                acc_q[:, window] = found_q
            else:
                acc_k[:, window] = jnp.where(mask, found_k, acc_k[:, window])
                acc_v[:, window] = jnp.where(mask, found_v, acc_v[:, window])
                acc_q[:, window] = jnp.where(mask, found_q, acc_q[:, window])

        grad_query = (acc_q[...] * score_scale).astype(BF)
        grad_key_ref[...] = (acc_k[...] * score_scale).astype(BF)
        grad_value_ref[...] = acc_v[...].astype(BF)
        grad_query_ref[...] = grad_query

        @pl.when(row == 0)
        def _():
            run_all(loads(), "wait")

        upstream = dot(grad_query, wq[...], ((1,), (1,))).astype(BF)
        for index, ref in enumerate(up_refs):
            ref[...] = upstream[index * group : (index + 1) * group, :]

    row_block = lambda i, p: (first + i, 0)
    own_block = lambda i, p: (i, 0)
    return pl.pallas_call(
        kernel,
        grid_spec=pltpu.PrefetchScalarGridSpec(
            num_scalar_prefetch=1,
            grid=(rows,),
            in_specs=[pl.BlockSpec((group, lat + LANES), own_block)] * count_parts
            + [
                pl.BlockSpec((latents, lat), own_block),
                pl.BlockSpec((block, lat), row_block),
                pl.BlockSpec((block, lat), row_block),
                pl.BlockSpec((1, 1, block), lambda i, p: (first + i, 0, 0)),
            ]
            + [any_spec()] * count,
            out_specs=[
                pl.BlockSpec((block, lat), own_block),
                pl.BlockSpec((block, lat), own_block),
                pl.BlockSpec((latents, lat), own_block),
            ]
            + [pl.BlockSpec((group, lat), own_block)] * groups,
            scratch_shapes=[
                pltpu.VMEM((lat, lat), BF),
                pltpu.VMEM((latents, lat), F32),
                pltpu.VMEM((block, lat), F32),
                pltpu.VMEM((block, lat), F32),
                pltpu.SemaphoreType.DMA((2 * count,)),
            ],
        ),
        out_shape=[shape((rows * block, lat))] * 2
        + [shape((rows * latents, lat))]
        + [shape((rows * group, lat))] * groups,
        compiler_params=params(1),
        cost_estimate=SMALL,
        name="attend_back",
    )(place, *parts, queries, keys, values, byte_ids, *held.flat)


def weight_grads_call(place, lefts, rights, some_rows, far):
    lat = rights[0][0].shape[1]
    chunk = sum(some_rows)
    left_counts, counts = [len(parts) for parts in lefts], [len(parts) for parts in rights]

    def kernel(place_ref, *refs):
        refs = list(refs)
        take = lambda n: [refs.pop(0) for _ in range(n)]
        left_refs = [take(n) for n in left_counts]
        right_refs = [take(n) for n in counts]
        outs = take(far)
        at = 0
        for index, (left, held) in enumerate(zip((0, 0, 1), refs)):
            factors, column, found = left_refs[left], 0, 0.0
            for part, right in enumerate(right_refs[index]):
                some = right.shape[0]
                if len(factors) > 1:
                    factor = factors[part][...]
                else:
                    factor = factors[0][:, column : column + some]
                found = found + dot(factor, right[...])
                column += some
            held[...] = found.astype(BF)
            some = some_rows[index]
            for distance in range(far):
                owner = jnp.bitwise_xor(place_ref[0], distance)
                outs[distance][at : at + some, :] = held[
                    pl.ds(pl.multiple_of(owner * some, 16), some), :
                ]
            at += some

    tile = lambda i, p: (0, i)
    flat_lefts = [left for parts in lefts for left in parts]
    flat_rights = [right for parts in rights for right in parts]
    return pl.pallas_call(
        kernel,
        grid_spec=pltpu.PrefetchScalarGridSpec(
            num_scalar_prefetch=1,
            grid=(lat // WINDOW,),
            in_specs=[full_block(left.shape) for left in flat_lefts]
            + [pl.BlockSpec((right.shape[0], WINDOW), tile) for right in flat_rights],
            out_specs=[pl.BlockSpec((chunk, WINDOW), tile)] * far,
            scratch_shapes=[pltpu.VMEM((lefts[i][0].shape[0], WINDOW), BF) for i in (0, 0, 1)],
        ),
        out_shape=[shape((chunk, lat))] * far,
        compiler_params=params(1),
        cost_estimate=SMALL,
        name="weight_grads",
    )(place, *flat_lefts, *flat_rights)


def byte_grad_call(place, bytes_flat, grads, held, rows, cuts):
    tokens, width = bytes_flat.shape
    block = tokens // rows
    lat = grads[0][0].shape[1]
    count = len(held.flat)
    shards = place_shards(held)

    def kernel(place_ref, x_ref, *refs):
        grad_refs = refs[: 2 * len(cuts)]
        piece_refs = refs[2 * len(cuts) : 2 * len(cuts) + count]
        out_ref, wk, wv, gains, gain, sems = refs[2 * len(cuts) + count :]
        row = pl.program_id(0)

        def loads():
            return held.copies(
                ("gains", "key", "value"), piece_refs, (gains, wk, wv), place_ref, sems
            )

        @pl.when(row == 0)
        def _():
            run_all(loads(), "start")

        xhat, scale = standardize(x_ref[...].astype(F32))

        @pl.when(row == 0)
        def _():
            run_all(loads(), "wait")
            gain[...] = gain_vector(gains, width, held.lanes["byte"], shards)

        for index, (first, some) in enumerate(cuts):

            @pl.when((row >= first) & (row < first + some))
            def _():
                upstream = dot(grad_refs[2 * index][...], wk[...], ((1,), (1,))) + dot(
                    grad_refs[2 * index + 1][...], wv[...], ((1,), (1,))
                )
                out_ref[...] = norm_pull(upstream, gain[...], xhat, scale)

    row_block = lambda i, p: (i, 0)

    def cut_block(first, some):
        return lambda i, p: (jnp.clip(i - first, 0, some - 1), 0)

    return pl.pallas_call(
        kernel,
        grid_spec=pltpu.PrefetchScalarGridSpec(
            num_scalar_prefetch=1,
            grid=(rows,),
            in_specs=[pl.BlockSpec((block, width), row_block)]
            + [pl.BlockSpec((block, lat), cut_block(*cut)) for cut in cuts for _ in range(2)]
            + [any_spec()] * count,
            out_specs=pl.BlockSpec((block, width), row_block),
            scratch_shapes=[
                pltpu.VMEM((width, lat), BF),
                pltpu.VMEM((width, lat), BF),
                pltpu.VMEM((held.blocks * GAIN_ROWS, LANES), BF),
                pltpu.VMEM((1, width), F32),
                pltpu.SemaphoreType.DMA((6 * count,)),
            ],
        ),
        out_shape=shape((tokens, width), F32),
        compiler_params=params(1),
        cost_estimate=SMALL,
        name="byte_grad",
    )(place, bytes_flat, *[g for some in grads for g in some], *held.flat)


def latent_grad_call(place, latent_message, grad_mixed, ups, held):
    tokens, lat = grad_mixed.shape
    cuts, groups = len(ups), len(ups[0])
    count = len(held.flat)
    shards = place_shards(held)

    def kernel(place_ref, x_ref, mixed_ref, *refs):
        up_refs = [refs[i * groups : (i + 1) * groups] for i in range(cuts)]
        piece_refs = refs[cuts * groups : cuts * groups + count]
        out_ref, gains, sems = refs[cuts * groups + count :]
        loads = held.copies(("gains",), piece_refs, (gains,), place_ref, sems)
        run_all(loads, "start")
        xhat, scale = standardize(x_ref[:, :lat].astype(F32))
        upstream = jnp.concatenate(
            [
                functools.reduce(jnp.add, [ref[...].astype(F32) for ref in some])
                for some in up_refs
            ],
            axis=0,
        )
        run_all(loads, "wait")
        gain = gain_vector(gains, lat, held.lanes["latent"], shards)
        out_ref[...] = mixed_ref[...] + norm_pull(upstream, gain, xhat, scale)

    return pl.pallas_call(
        kernel,
        in_specs=[scalar_spec()]
        + [whole_spec()] * (2 + cuts * groups)
        + [any_spec()] * count,
        out_specs=whole_spec(),
        out_shape=shape((tokens, lat), F32),
        scratch_shapes=[
            pltpu.VMEM((held.blocks * GAIN_ROWS, LANES), BF),
            pltpu.SemaphoreType.DMA((2 * count,)),
        ],
        compiler_params=params(0, 24),
        cost_estimate=SMALL,
        name="latent_grad",
    )(place, latent_message, grad_mixed, *[u for some in ups for u in some], *held.flat)


def swap(value, axis, size, distance):
    return lax.ppermute(value, axis, [(i, i ^ distance) for i in range(size)])


def tie(value, *earlier):
    return lax.optimization_barrier((value, *earlier))[0]


def passed(value, *earlier, cost):
    def kernel(in_ref, out_ref):
        pass

    return pl.pallas_call(
        kernel,
        in_specs=[any_spec()],
        out_specs=any_spec(),
        out_shape=shape(value.shape, value.dtype),
        input_output_aliases={0: 0},
        cost_estimate=pl.CostEstimate(
            flops=int(cost * 1.1e9), bytes_accessed=1, transcendentals=0
        ),
        name="passed",
    )(tie(value, *earlier))


def swap_all(parts, size):
    return [swap(parts[j], "fsdp", size, j) for j in range(1, size)]


def by_index(parts, own, size):
    if len(parts) == 5:
        parts = parts[:3] + [jnp.where((own == 0) | (own == 3), parts[4], parts[3])]
    return [lax.select_n(jnp.bitwise_xor(own, k), *parts) for k in range(size)]


def build_block(place, own, parts, sizes, size):
    segments, first, at = [], 0, 0
    for rows in sizes:
        segments.append((first, rows, at))
        first += rows
        at += rows * size
    total = up_to(at, 16)
    if all(first % 8 == 0 for first, _, _ in segments):
        return assemble_call(place, parts, segments, total, size)
    shards = by_index(parts, own, size)
    found = [s[first : first + rows] for first, rows, _ in segments for s in shards]
    return pad_rows(jnp.concatenate(found, axis=0), total)


def add(*values):
    return functools.reduce(jnp.add, [v.astype(F32) for v in values]).astype(BF)


def meet_call(first, high, second, low, half):
    rows, lat = first[0].shape

    def kernel(a, b, h, c, d, l, one, two):
        one[:half, :] = (a[:half, :].astype(F32) + b[:half, :].astype(F32)).astype(BF)
        one[half:, :] = (
            a[half:, :].astype(F32) + b[half:, :].astype(F32) + h[...].astype(F32)
        ).astype(BF)
        two[:half, :] = (
            c[:half, :].astype(F32) + d[:half, :].astype(F32) + l[...].astype(F32)
        ).astype(BF)
        two[half:, :] = (c[half:, :].astype(F32) + d[half:, :].astype(F32)).astype(BF)

    return pl.pallas_call(
        kernel,
        in_specs=[whole_spec()] * 6,
        out_specs=[whole_spec()] * 2,
        out_shape=[shape((rows, lat))] * 2,
        compiler_params=params(0, 24),
        cost_estimate=SMALL,
        name="meet",
    )(*first, high, *second, low)


def cut_call(place, terms, sizes, size):
    lat = terms[0].shape[1]
    rows = sum(sizes)

    def kernel(place_ref, *refs):
        term_refs, outs, acc = refs[: len(terms)], refs[len(terms) : -1], refs[-1]
        acc[...] = functools.reduce(jnp.add, [ref[...].astype(F32) for ref in term_refs])
        for distance, out in enumerate(outs):
            owner = jnp.bitwise_xor(place_ref[1], distance)
            found, at = [], 0
            for some in sizes:
                found.append(acc[pl.ds(pl.multiple_of(at + owner * some, 8), some), :])
                at += some * size
            out[...] = jnp.concatenate(found, axis=0).astype(out.dtype)

    return pl.pallas_call(
        kernel,
        in_specs=[scalar_spec()] + [whole_spec()] * len(terms),
        out_specs=[whole_spec()] * size,
        out_shape=[shape((rows, lat), F32)] + [shape((rows, lat))] * (size - 1),
        scratch_shapes=[pltpu.VMEM(terms[0].shape, F32)],
        compiler_params=params(0, 24),
        cost_estimate=SMALL,
        name="cut",
    )(place, *terms)


def cut_terms(place, own, terms, sizes, size):
    if all(some % 8 == 0 for some in sizes):
        return cut_call(place, terms, sizes, size)
    block = functools.reduce(jnp.add, [v.astype(F32) for v in terms])
    outs = []
    for distance in range(size):
        index = jnp.bitwise_xor(own, distance)
        found, at = [], 0
        for some in sizes:
            part = block[at : at + some * size].reshape(size, some, block.shape[1])
            found.append(lax.dynamic_index_in_dim(part, index, 0, keepdims=False))
            at += some * size
        value = jnp.concatenate(found, axis=0)
        outs.append(value if distance == 0 else value.astype(BF))
    return outs


def total(own, arrived):
    return functools.reduce(jnp.add, [v.astype(F32) for v in [own, *arrived]])


def split_rows(value, sizes):
    found, at = [], 0
    for some in sizes:
        found.append(value[at : at + some])
        at += some
    return found


def up_to(value, step):
    return -(-value // step) * step


def pad_rows(value, rows):
    return jnp.pad(value, ((0, rows - value.shape[0]), (0, 0)))


class Plan:
    def __init__(self, n_dp, n_f):
        self.n_dp, self.n_f = n_dp, n_f
        self.gate = ()

    def send(self, value, distance):
        return swap(tie(value, *self.gate), "dp", self.n_dp, distance)

    def pass_on(self, value, distance):
        return swap(tie(value, *self.gate), "fsdp", self.n_f, distance)

    def relay(self, own, two):
        middle = lax.ppermute(tie(own, *self.gate), "fsdp", [(1, 2), (2, 1)])
        return middle, lax.ppermute(tie(two, *self.gate), "fsdp", [(2, 3), (1, 0)])

    def spread(self, value):
        value = tie(value, *self.gate)
        middle = lax.ppermute(value, "fsdp", [(1, 2), (2, 1)])
        return middle, lax.ppermute(value, "fsdp", [(3, 2), (0, 1)])

    def tied(self, values):
        return [tie(values[0], *self.gate), *values[1:]]


def square_pieces(block, chips, half):
    rows = block.shape[0]
    full, halves = [(0, rows)], [(0, half), (half, rows)]
    pieces, flat = [], []
    for distance, parts, pairs in (
        (0, full, chips[:1]),
        (2, full, chips[1:2]),
        (4, full, chips[2:3]),
        (6, halves, chips[3:]),
    ):
        for core in range(2):
            pieces.append((distance + core, parts))
            flat.extend(pair[core] for pair in pairs)
    return pieces, flat


def local(n_dp, n_f, bytes_in, latents_in, cotangent, byte_segments, latent_segments,
          w_query, w_key, w_value, w_out, w_mlp_in, w_mlp_out,
          gain_latent, gain_byte, gain_mlp):
    rows, byte_local, width = bytes_in.shape
    _, group, lat = latents_in.shape
    dp, own = lax.axis_index("dp"), lax.axis_index("fsdp")
    place = jnp.stack([dp, own]).astype(jnp.int32)
    bytes_flat = bytes_in.reshape(rows * byte_local, width)
    latents_flat = latents_in.reshape(rows * group, lat)
    cot_flat = cotangent.reshape(rows * group, lat)
    kr, qr = w_key.shape[0], w_query.shape[0]
    key_rows, query_rows = n_f * kr, n_f * qr
    cuts = [(0, 1), (1, rows - 1)]
    cut_rows = [(first * group, some * group) for first, some in cuts]

    gains = jnp.concatenate([gain_latent, gain_byte, gain_mlp])
    gains = jnp.pad(gains, (0, lat - gains.shape[0]))[None, :]
    message_one = jnp.concatenate([w_key, w_value, w_query, gains], axis=0)
    message_one = pad_rows(message_one, up_to(2 * kr + qr + 1, 16))
    message_two = jnp.concatenate([w_out, w_mlp_in, w_mlp_out], axis=0)
    ids = latent_segments.reshape(rows * group, 1).astype(BF)
    ids = jnp.pad(ids, ((0, 0), (0, LANES - 1)))
    latent_message = jnp.concatenate([latents_flat, ids], axis=1)
    byte_ids = lax.dynamic_slice_in_dim(byte_segments, own * byte_local, byte_local, axis=1)
    byte_ids = byte_ids.astype(F32)
    byte_row = byte_ids[:, None, :]
    sizes_one, sizes_two = (kr, kr, qr), (qr, qr, qr)
    half_one, half_two = 2 * key_rows, up_to(3 * query_rows // 2, 16)
    spans_one = {
        "key": (0, key_rows),
        "value": (key_rows, key_rows),
        "query": (2 * key_rows, query_rows),
        "gains": (2 * key_rows + query_rows, GAIN_ROWS),
    }
    spans_two = {name: (i * query_rows, query_rows) for i, name in enumerate(("out", "inner", "outer"))}

    def held_one(pieces, flat):
        held = Held(pieces, flat, spans_one)
        held.blocks, held.size = n_dp, n_f
        held.lanes = {"latent": 0, "byte": qr, "mlp": qr + kr}
        return held

    def key_value(one, bytes_flat):
        return key_value_call(place, bytes_flat, one, rows)

    def attend(index, one, parts, keys, values):
        found = attend_call(
            place, parts, byte_row, keys, values, one, n_f, group, *cuts[index]
        )
        return found[0], found[1], found[2:]

    def feed(one, two, attended):
        return feed_call(place, attended, latent_message, cot_flat, one, two, cut_rows)

    def feed_grads(lefts, rights):
        return feed_grads_call(place, lefts, rights, query_rows, n_dp)

    def attend_back(index, one, parts, saved):
        return attend_back_call(
            place, parts, *saved, byte_row, one, n_f, group, *cuts[index]
        )

    def weight_grads(lefts, first, last):
        return weight_grads_call(
            place, lefts, list(zip(first, last)), (key_rows, key_rows, query_rows), n_dp
        )

    def byte_grad(one, grads):
        return byte_grad_call(place, bytes_flat, grads, one, rows, cuts)

    run = square if (n_dp, n_f) == (8, 4) else plain
    new, grad_latents, grad_bytes, grad_one, grad_two = run(**locals())

    def gain_grad(pairs, gain):
        found = sum(jnp.sum(w.astype(F32) * g, axis=1) for w, g in pairs)
        return found / gain.astype(F32)

    grad_key, grad_value, grad_query = split_rows(grad_one, sizes_one)
    grad_out, grad_inner, grad_outer = split_rows(grad_two, sizes_two)
    return (
        new.reshape(rows, group, lat),
        grad_latents.reshape(rows, group, lat),
        grad_bytes.reshape(rows, byte_local, width),
        grad_query,
        grad_key,
        grad_value,
        grad_out,
        grad_inner,
        grad_outer,
        gain_grad([(w_query, grad_query)], gain_latent),
        gain_grad([(w_key, grad_key), (w_value, grad_value)], gain_byte),
        gain_grad([(w_mlp_in, grad_inner)], gain_mlp),
    )


def plain(*, n_dp, n_f, place, own, bytes_flat, message_one, message_two, latent_message,
          sizes_one, sizes_two, spans_two, cot_flat, held_one, key_value, attend, feed,
          feed_grads, attend_back, weight_grads, byte_grad, **_):
    def gather(message, sizes):
        parts = [message, *swap_all([message] * n_f, n_f)]
        block = build_block(place, own, parts, sizes, n_f)
        flat = [block] + [swap(block, "dp", n_dp, d) for d in range(1, n_dp)]
        return [(d, [(0, block.shape[0])]) for d in range(n_dp)], flat

    def scatter(parts, sizes):
        terms = [parts[0]] + [swap(parts[d], "dp", n_dp, d) for d in range(1, n_dp)]
        cut = cut_terms(place, own, terms, sizes, n_f)
        return total(cut[0], swap_all(cut, n_f))

    one = held_one(*gather(message_one, (*sizes_one, 1)))
    two = Held(*gather(message_two, sizes_two), spans_two)
    byte_t, keys, values = key_value(one, bytes_flat)
    latent_parts = [latent_message, *swap_all([latent_message] * n_f, n_f)]
    latent_t, queries, found = zip(*[attend(i, one, latent_parts, keys, values) for i in range(2)])
    attended = list(zip(*[[f[0], *swap_all(f, n_f)] for f in found]))
    new, grad_mixed, *messages, attended_t, branch, normed_t, inner, act_t = feed(
        one, two, attended
    )
    grad_two = scatter(feed_grads((attended_t, normed_t, act_t), (branch, inner, cot_flat)), sizes_two)
    parts = [[m, *swap_all([m] * n_f, n_f)] for m in messages]
    first, last = [attend_back(i, one, parts[i], (queries[i], keys, values)) for i in range(2)]
    grad_bytes = byte_grad(one, (first[:2], last[:2]))
    grad_one = scatter(weight_grads(((byte_t,), latent_t), first[:3], last[:3]), sizes_one)
    ups = [[ups[0], *swap_all(ups, n_f)] for ups in (first[3:], last[3:])]
    grad_latents = latent_grad_call(place, latent_message, grad_mixed, ups, one)
    return new, grad_latents, grad_bytes, grad_one, grad_two


def square(*, n_dp, n_f, place, own, bytes_flat, message_one, message_two, latent_message,
           sizes_one, sizes_two, spans_two, half_one, half_two, cot_flat, held_one, key_value,
           attend, feed, feed_grads, attend_back, weight_grads, byte_grad, **_):
    plan = Plan(n_dp, n_f)
    send, pass_on = plan.send, plan.pass_on

    near = [pass_on(message_one, 2), pass_on(message_one, 1)]
    plan.gate = near
    parts = [message_one, near[1], near[0], *plan.relay(message_one, near[0])]
    block = build_block(place, own, parts, (*sizes_one, 1), n_f)
    plan.gate = [block]
    x, y, other = send(block, 2), send(block, 4), send(block, 1)
    latent_two, latent_one = pass_on(latent_message, 2), pass_on(latent_message, 1)
    plan.gate = [x, y, other, latent_two, latent_one]
    low, high = send(x[:half_one], 4), send(y[half_one:], 2)
    latent_parts = [
        latent_message, latent_one, latent_two, *plan.relay(latent_message, latent_two)
    ]
    x_other = send(x, 1)
    y_other = send(tie(y, x_other), 1)
    plan.gate = [low, high, y_other, *latent_parts[3:]]
    low_other, high_other = send(low, 1), send(high, 1)
    pairs = [(block, other), (x, x_other), (y, y_other), (low, low_other), (high, high_other)]
    one = held_one(*square_pieces(block, pairs, half_one))
    two_two, two_one = pass_on(message_two, 2), pass_on(message_two, 1)
    plan.gate = [low_other, high_other]
    byte_t, keys, values = key_value(one, tie(bytes_flat, *plan.gate))
    plan.gate = [two_two, two_one, keys]
    parts = [message_two, two_one, two_two, *plan.relay(message_two, two_two)]
    latent_t_first, queries_first, found = attend(0, one, plan.tied(latent_parts), keys, values)
    plan.gate = [queries_first, *parts[3:]]
    block = build_block(place, own, plan.tied(parts), sizes_two, n_f)
    x, y = send(block, 2), send(block, 4)
    attended_first = [found[0], *[pass_on(found[j], j) for j in range(1, n_f)]]
    plan.gate = [block]
    latent_t_last, queries_last, found = attend(1, one, plan.tied(latent_parts), keys, values)
    plan.gate = attended_first[1:]
    attended_last = [found[0], *[pass_on(found[j], j) for j in range(1, n_f)]]
    plan.gate = [x, y, queries_last, *attended_first[1:]]
    low, high = send(x[:half_two], 4), send(y[half_two:], 2)
    attended_last[1] = passed(attended_last[1], *attended_last[2:], cost=4)
    plan.gate = [low, high, *attended_last[1:]]
    pairs = [(v, send(v, 1)) for v in (block, x, y, low, high)]
    two = Held(*square_pieces(block, pairs, half_two), spans_two)
    new, grad_mixed, first, last, attended_t, branch, normed_t, inner, act_t = feed(
        one, two, list(zip(attended_first, attended_last))
    )
    plan.gate = []
    near = [pass_on(first, 2), pass_on(first, 1)]
    grads = feed_grads((attended_t, normed_t, act_t), (branch, inner, cot_flat))
    plan.gate = near
    first_parts = [first, near[1], near[0], *plan.relay(first, near[0])]
    near = [pass_on(last, 2), pass_on(last, 1)]
    arrived = {d: send(grads[d + 1], 1) for d in (6, 4)}
    low = add(grads[6][:half_two], arrived[6][:half_two])
    high = add(grads[6][half_two:], arrived[6][half_two:])
    plan.gate = [*arrived.values(), *first_parts[3:]]
    low, high = send(low, 2), send(high, 4)
    arrived[2] = send(grads[3], 1)
    back_first = attend_back(0, one, plan.tied(first_parts), (queries_first, keys, values))
    plan.gate = [low, high, arrived[2], *near, back_first[0]]
    last_parts = [last, near[1], near[0], *plan.relay(last, near[0])]
    arrived[0] = send(grads[1], 1)
    x, y = meet_call(
        (grads[2], arrived[2]), tie(high, *plan.gate), (grads[4], arrived[4]), low, half_two
    )
    plan.gate = [x, y, arrived[0], *last_parts[3:]]
    terms_two = [grads[0], arrived[0], send(x, 2), send(y, 4)]
    ups_first = back_first[3:]
    ups_first = [ups_first[0], *[pass_on(ups_first[j], j) for j in range(1, n_f)]]
    back_last = attend_back(1, one, plan.tied(last_parts), (queries_last, keys, values))
    plan.gate = [back_last[0], *ups_first[1:]]
    ups = back_last[3:]
    near = [pass_on(ups[1], 1), *plan.spread(ups[3])]
    grads = weight_grads(
        ((byte_t,), (latent_t_first, latent_t_last)),
        back_first[:3],
        [tie(back_last[0], *plan.gate), *back_last[1:3]],
    )
    plan.gate = [*near, grads[0], *terms_two[2:]]
    arrived = {d: send(grads[d + 1], 1) for d in (6, 4, 2)}
    low = add(grads[6][:half_one], arrived[6][:half_one])
    high = add(grads[6][half_one:], arrived[6][half_one:])
    merged = add(tie(ups[2], *plan.gate), near[2])
    plan.gate = [low, high, merged, *arrived.values()]
    low, high = send(low, 2), send(high, 4)
    ups_last = [ups[0], *near[:2], pass_on(merged, 2)]
    cut_two = cut_terms(place, own, plan.tied(terms_two), sizes_two, n_f)
    plan.gate = [low, high, cut_two[0]]
    x, y = meet_call(
        (grads[2], arrived[2]), tie(high, *plan.gate), (grads[4], arrived[4]), low, half_one
    )
    arrived_two = [pass_on(cut_two[j], j) for j in range(1, n_f)]
    plan.gate = [x, y]
    terms_one = [grads[0], None, send(x, 2), send(y, 4)]
    grad_bytes = byte_grad(one, (plan.tied(back_first[:2]), back_last[:2]))
    plan.gate = [x, y, ups_last[-1]]
    terms_one[1] = send(grads[1], 1)
    plan.gate = [*terms_one[1:], grad_bytes]
    cut_one = cut_terms(place, own, plan.tied(terms_one), sizes_one, n_f)
    plan.gate = [cut_one[0]]
    grad_one = total(cut_one[0], [pass_on(cut_one[j], j) for j in range(1, n_f)])
    grad_two = total(cut_two[0], arrived_two)
    grad_latents = latent_grad_call(
        place, latent_message, tie(grad_mixed, *plan.gate), [ups_first, ups_last], one
    )
    return new, grad_latents, grad_bytes, grad_one, grad_two


def solution(mesh):
    rows3 = P("dp", "fsdp", None)
    split2 = P(("dp", "fsdp"), None)
    split1 = P(("dp", "fsdp"))
    in_specs = (rows3,) * 3 + (P("dp", None), P("dp", "fsdp")) + (split2,) * 6 + (split1,) * 3
    out_specs = (rows3,) * 3 + (split2,) * 6 + (split1,) * 3
    body = functools.partial(local, mesh.shape["dp"], mesh.shape["fsdp"])
    return jax.shard_map(
        body, mesh=mesh, in_specs=in_specs, out_specs=out_specs, check_vma=False
    )
```

```python
import functools
import math

import jax
import jax.numpy as jnp
from jax import lax
from jax.experimental import pallas as pl
from jax.experimental.pallas import tpu as pltpu
from jax.sharding import PartitionSpec as P

HEADS = 8
HEAD_DIM = 160
EPSILON = 1e-05
NEG_FILL = -1e30
LANES = 128
WINDOW = 256
BF = jnp.bfloat16
F32 = jnp.float32
GAIN_ROWS = 16
SMALL = pl.CostEstimate(flops=1, bytes_accessed=1, transcendentals=0)


def head_window(head):
    start = head * HEAD_DIM // LANES * LANES
    return start, head * HEAD_DIM - start


def head_lanes(head):
    _, shift = head_window(head)
    lane = lax.broadcasted_iota(jnp.int32, (1, WINDOW), 1)
    return (lane >= shift) & (lane < shift + HEAD_DIM)


def dot(a, b, dims=((1,), (0,))):
    return lax.dot_general(a, b, (dims, ((), ())), preferred_element_type=F32)


def standardize(values):
    centered = values - jnp.mean(values, axis=-1, keepdims=True)
    scale = lax.rsqrt(jnp.mean(centered * centered, axis=-1, keepdims=True) + EPSILON)
    return centered * scale, scale


def norm_pull(upstream, gain, xhat, scale):
    scaled = upstream * gain
    return scale * (
        scaled
        - jnp.mean(scaled, axis=-1, keepdims=True)
        - xhat * jnp.mean(scaled * xhat, axis=-1, keepdims=True)
    )


def split_three(values):
    first = values.astype(BF).astype(F32)
    rest = values - first
    second = rest.astype(BF).astype(F32)
    return first, second, rest - second


def gelu(values):
    inner = math.sqrt(2 / math.pi) * (values + 0.044715 * values * values * values)
    return 0.5 * values * (1.0 + jnp.tanh(inner))


def gelu_slope(values):
    square = values * values
    tanh = jnp.tanh(math.sqrt(2 / math.pi) * (values + 0.044715 * square * values))
    slope = math.sqrt(2 / math.pi) * (1.0 + 3 * 0.044715 * square)
    return 0.5 * (1.0 + tanh) + 0.5 * values * (1.0 - tanh * tanh) * slope


def piece_copies(pieces, flat_refs, first, rows, target, me, sems, base):
    copies = []
    lanes = target.shape[1]
    at = 0
    for distance, parts in pieces:
        owner = jnp.bitwise_xor(me, distance)
        for low, high in parts:
            ref = flat_refs[at]
            at += 1
            start, stop = max(low, first), min(high, first + rows)
            if start < stop:
                place = pl.multiple_of(owner * rows + (start - first), 16)
                copies.append(
                    pltpu.make_async_copy(
                        ref.at[pl.ds(start - low, stop - start), pl.ds(0, lanes)],
                        target.at[pl.ds(place, stop - start), :],
                        sems.at[base + len(copies)],
                    )
                )
    return copies


def group_values(refs, place):
    if len(refs) != 5:
        return [ref[...] for ref in refs]
    own = place[1]
    at_end = (own == 0) | (own == 3)
    values = [ref[...] for ref in refs[:3]]
    return values + [jnp.where(at_end, refs[4][...], refs[3][...])]


def gain_vector(held, size, lane_at, shards):
    per_shard = size // shards
    blocks = held.shape[0] // GAIN_ROWS
    per_block = shards // blocks
    lane = lax.broadcasted_iota(jnp.int32, (LANES, size), 0)
    column = lax.broadcasted_iota(jnp.int32, (LANES, size), 1)
    pick = (lane == lane_at + column % per_shard).astype(F32).astype(BF)
    spread = dot(held[...], pick)
    row = lax.broadcasted_iota(jnp.int32, spread.shape, 0)
    column = lax.broadcasted_iota(jnp.int32, spread.shape, 1) // per_shard
    owner = (row // GAIN_ROWS) * per_block + row % GAIN_ROWS
    right = (owner == column) & (row % GAIN_ROWS < per_block)
    return jnp.sum(jnp.where(right, spread, 0.0), axis=0, keepdims=True)


def params(grid_rank, mebibytes=60):
    return pltpu.CompilerParams(
        dimension_semantics=("arbitrary",) * grid_rank, vmem_limit_bytes=mebibytes << 20
    )


def whole_spec():
    return pl.BlockSpec(memory_space=pltpu.VMEM)


def any_spec():
    return pl.BlockSpec(memory_space=pltpu.HBM)


class Held:
    def __init__(self, pieces, flat, spans):
        self.pieces, self.flat, self.spans = pieces, flat, spans

    def crossed(self):
        at = 0
        for distance, parts in self.pieces:
            if distance == self.blocks - 2:
                return self.flat[at : at + len(parts)]
            at += len(parts)

    def copies(self, names, refs, targets, place, sems):
        found, base = [], 0
        for name, target in zip(names, targets):
            first, rows = self.spans[name]
            some = piece_copies(self.pieces, refs, first, rows, target, place[0], sems, base)
            base += len(some)
            found.append(some)
        return found


def run_all(groups, action):
    for group in groups:
        for copy in group:
            getattr(copy, action)()


def shape(dims, dtype=BF):
    return jax.ShapeDtypeStruct(dims, dtype)


def full_block(dims):
    return pl.BlockSpec(
        dims, lambda i, p: (0,) * len(dims), pipeline_mode=pl.Buffered(buffer_count=1)
    )


def scalar_spec():
    return pl.BlockSpec(memory_space=pltpu.SMEM)


def assemble_call(place, parts, segments, total, size):
    def kernel(place_ref, *refs):
        part_refs, out_ref, acc = refs[: len(parts)], refs[len(parts)], refs[len(parts) + 1]
        values = [v.astype(F32) for v in group_values(part_refs, place_ref)]
        end = max(at + size * rows for _, rows, at in segments)
        if end < total:
            first = end // 8 * 8
            acc[first:, :] = jnp.zeros((total - first, acc.shape[1]), F32)
        for index in range(size):
            want = jnp.bitwise_xor(place_ref[1], index)
            value = values[size - 1]
            for distance in range(size - 2, -1, -1):
                value = jnp.where(want == distance, values[distance], value)
            for first, rows, at in segments:
                acc[at + index * rows : at + (index + 1) * rows, :] = value[first : first + rows]
        out_ref[...] = acc[...].astype(BF)

    lat = parts[0].shape[1]
    return pl.pallas_call(
        kernel,
        in_specs=[scalar_spec()] + [whole_spec()] * len(parts),
        out_specs=whole_spec(),
        out_shape=shape((total, lat)),
        scratch_shapes=[pltpu.VMEM((total, lat), F32)],
        compiler_params=params(0, 24),
        cost_estimate=SMALL,
        name="assemble",
    )(place, *parts)


def key_value_call(place, bytes_flat, held, rows):
    tokens, width = bytes_flat.shape
    block = tokens // rows
    lat = held.flat[0].shape[1]
    count = len(held.flat)
    shards = place_shards(held)

    def kernel(place_ref, x_ref, *refs):
        piece_refs = refs[:count]
        normed_t_ref, key_ref, value_ref, wk, wv, gains, gain, sems = refs[count:]
        first = pl.program_id(0) == 0

        def loads():
            return held.copies(
                ("gains", "key", "value"), piece_refs, (gains, wk, wv), place_ref, sems
            )

        @pl.when(first)
        def _():
            run_all(loads(), "start")

        xhat, _ = standardize(x_ref[...].astype(F32))

        @pl.when(first)
        def _():
            run_all(loads(), "wait")
            gain[...] = gain_vector(gains, width, held.lanes["byte"], shards)

        normed = (xhat * gain[...]).astype(BF)
        key_ref[...] = dot(normed, wk[...]).astype(BF)
        value_ref[...] = dot(normed, wv[...]).astype(BF)
        normed_t_ref[...] = jnp.transpose(normed, (1, 0))

    row_block = lambda i, p: (i, 0)
    return pl.pallas_call(
        kernel,
        grid_spec=pltpu.PrefetchScalarGridSpec(
            num_scalar_prefetch=1,
            grid=(rows,),
            in_specs=[pl.BlockSpec((block, width), row_block)] + [any_spec()] * count,
            out_specs=[
                pl.BlockSpec((width, block), lambda i, p: (0, i)),
                pl.BlockSpec((block, lat), row_block),
                pl.BlockSpec((block, lat), row_block),
            ],
            scratch_shapes=[
                pltpu.VMEM((width, lat), BF),
                pltpu.VMEM((width, lat), BF),
                pltpu.VMEM((held.blocks * GAIN_ROWS, LANES), BF),
                pltpu.VMEM((1, width), F32),
                pltpu.SemaphoreType.DMA((6 * count,)),
            ],
        ),
        out_shape=[shape((width, tokens)), shape((tokens, lat)), shape((tokens, lat))],
        compiler_params=params(1),
        cost_estimate=SMALL,
        name="keys_values",
    )(place, bytes_flat, *held.flat)


def place_shards(held):
    return held.blocks * held.size


def attend_call(place, latent_parts, byte_ids, keys, values, held, groups, group, first, rows):
    parts = len(latent_parts)
    lat = keys.shape[1]
    block = byte_ids.shape[2]
    latents = groups * group
    count = len(held.flat)
    shards = place_shards(held)
    score_scale = 1.0 / math.sqrt(HEAD_DIM)

    def kernel(place_ref, *refs):
        part_refs = refs[:parts]
        bid_ref, key_ref, value_ref = refs[parts : parts + 3]
        piece_refs = refs[parts + 3 : parts + 3 + count]
        rest = refs[parts + 3 + count :]
        normed_t_ref, query_ref = rest[:2]
        out_refs = rest[2 : 2 + groups]
        wq, gains, gain, acc, sems = rest[2 + groups :]
        start = pl.program_id(0) == 0

        def loads():
            return held.copies(("gains", "query"), piece_refs, (gains, wq), place_ref, sems)

        @pl.when(start)
        def _():
            run_all(loads(), "start")

        message = jnp.concatenate(group_values(part_refs, place_ref), axis=0)
        ids = message[:, lat : lat + 1].astype(F32)
        xhat, _ = standardize(message[:, :lat].astype(F32))

        @pl.when(start)
        def _():
            run_all(loads(), "wait")
            gain[...] = gain_vector(gains, lat, held.lanes["latent"], shards)

        normed = (xhat * gain[...]).astype(BF)
        query_ref[...] = dot(normed, wq[...]).astype(BF)
        normed_t_ref[...] = jnp.transpose(normed, (1, 0))
        allowed = ids == bid_ref[0]
        lane = lax.broadcasted_iota(jnp.int32, (latents, LANES), 1)
        stats = jnp.zeros((latents, LANES), F32)
        for head in range(HEADS):
            at, _ = head_window(head)
            mask = head_lanes(head)
            window = slice(at, at + WINDOW)
            query = jnp.where(mask, query_ref[:, window], jnp.zeros((), BF))
            scores = dot(query, key_ref[:, window], ((1,), (1,))) * score_scale
            scores = jnp.where(allowed, scores, NEG_FILL)
            top = jnp.max(scores, axis=-1, keepdims=True)
            exponent = jnp.exp(scores - top)
            total = jnp.sum(exponent, axis=-1, keepdims=True)
            found = dot(exponent.astype(BF), value_ref[:, window]) / total
            if head == 0:
                acc[:, window] = found
            else:
                acc[:, window] = jnp.where(mask, found, acc[:, window])
            log_total = jnp.where(top > -1e29, top + jnp.log(total), NEG_FILL)
            for index, term in enumerate(split_three(log_total)):
                stats = jnp.where(lane == index * HEADS + head, term, stats)
        for index, ref in enumerate(out_refs):
            chunk = slice(index * group, (index + 1) * group)
            ref[:, :lat] = acc[chunk, :].astype(BF)
            ref[:, lat:] = stats[chunk, :].astype(BF)

    row_block = lambda i, p: (first + i, 0)
    own_block = lambda i, p: (i, 0)
    return pl.pallas_call(
        kernel,
        grid_spec=pltpu.PrefetchScalarGridSpec(
            num_scalar_prefetch=1,
            grid=(rows,),
            in_specs=[pl.BlockSpec((group, lat + LANES), row_block)] * parts
            + [
                pl.BlockSpec((1, 1, block), lambda i, p: (first + i, 0, 0)),
                pl.BlockSpec((block, lat), row_block),
                pl.BlockSpec((block, lat), row_block),
            ]
            + [any_spec()] * count,
            out_specs=[
                pl.BlockSpec((lat, latents), lambda i, p: (0, i)),
                pl.BlockSpec((latents, lat), own_block),
            ]
            + [pl.BlockSpec((group, lat + LANES), own_block)] * groups,
            scratch_shapes=[
                pltpu.VMEM((lat, lat), BF),
                pltpu.VMEM((held.blocks * GAIN_ROWS, LANES), BF),
                pltpu.VMEM((1, lat), F32),
                pltpu.VMEM((latents, lat), F32),
                pltpu.SemaphoreType.DMA((4 * count,)),
            ],
        ),
        out_shape=[shape((lat, rows * latents)), shape((rows * latents, lat))]
        + [shape((rows * group, lat + LANES))] * groups,
        compiler_params=params(1),
        cost_estimate=SMALL,
        name="attend",
    )(place, *latent_parts, byte_ids, keys, values, *held.flat)


def feed_call(place, parts, latent_message, cot_flat, held_gain, held, cuts):
    groups, pieces_of = len(parts), len(parts[0])
    tokens, lat = cot_flat.shape
    count, gain_count = len(held.flat), len(held_gain.flat)
    shards = place_shards(held_gain)

    def kernel(place_ref, *refs):
        refs = list(refs)
        take = lambda n: [refs.pop(0) for _ in range(n)]
        part_refs = [take(pieces_of) for _ in range(groups)]
        x_ref, cot_ref = take(2)
        gain_refs, piece_refs = take(gain_count), take(count)
        new_ref, mixed_grad_ref = take(2)
        message_refs = take(len(cuts))
        attended_t, branch, normed_t, inner, act_t = take(5)
        wo, w1, w2, gains, sems, gain_sems = refs
        gain_loads = held_gain.copies(("gains",), gain_refs, (gains,), place_ref, gain_sems)
        loads = held.copies(("out", "inner", "outer"), piece_refs, (wo, w1, w2), place_ref, sems)
        run_all(gain_loads, "start")
        run_all(loads, "start")

        lane = lax.broadcasted_iota(jnp.int32, (LANES, lat), 0)
        column = lax.broadcasted_iota(jnp.int32, (LANES, lat), 1)
        spread = jnp.zeros((LANES, lat), jnp.bool_)
        for head in range(HEADS):
            inside = (column >= head * HEAD_DIM) & (column < (head + 1) * HEAD_DIM)
            own = (lane == head) | (lane == HEADS + head) | (lane == 2 * HEADS + head)
            spread = spread | (inside & own)
        spread = spread.astype(F32).astype(BF)
        found = [jnp.concatenate([ref[...] for ref in some], axis=0) for some in part_refs]
        logs = [dot(value[:, lat:], spread) for value in found]
        top = functools.reduce(jnp.maximum, logs)
        shares = [jnp.exp(log - top) for log in logs]
        total = functools.reduce(jnp.add, shares)
        summed = functools.reduce(
            jnp.add, [s * value[:, :lat].astype(F32) for s, value in zip(shares, found)]
        )
        attended = (summed / total).astype(BF)
        log_total = top + jnp.log(total)
        attended_t[...] = jnp.transpose(attended, (1, 0))

        run_all(gain_loads, "wait")
        gain = gain_vector(gains, lat, held_gain.lanes["mlp"], shards)
        run_all(loads[:1], "wait")
        mixed = x_ref[:, :lat].astype(F32) + dot(attended, wo[...])
        xhat, scale = standardize(mixed)
        normed = (xhat * gain).astype(BF)
        normed_t[...] = jnp.transpose(normed, (1, 0))
        run_all(loads[1:2], "wait")
        hidden = dot(normed, w1[...])
        activated = gelu(hidden).astype(BF)
        act_t[...] = jnp.transpose(activated, (1, 0))
        run_all(loads[2:], "wait")
        new_ref[...] = (mixed + dot(activated, w2[...])).astype(BF)
        cot = cot_ref[...]
        grad_hidden = (dot(cot, w2[...], ((1,), (1,))) * gelu_slope(hidden)).astype(BF)
        inner[...] = grad_hidden
        upstream = dot(grad_hidden, w1[...], ((1,), (1,)))
        grad_mixed = cot.astype(F32) + norm_pull(upstream, gain, xhat, scale)
        mixed_grad_ref[...] = grad_mixed
        grad_branch = grad_mixed.astype(BF)
        branch[...] = grad_branch
        grad_attended = dot(grad_branch, wo[...], ((1,), (1,))).astype(BF)
        product = grad_attended.astype(F32) * attended.astype(F32)
        out_lane = lax.broadcasted_iota(jnp.int32, (tokens, LANES), 1)
        ids = x_ref[:, lat : lat + 1].astype(F32)
        stats = jnp.where(out_lane == 6 * HEADS, ids, 0.0)
        for head in range(HEADS):
            at, shift = head_window(head)
            mask = head_lanes(head)
            inner_sum = jnp.sum(
                jnp.where(mask, product[:, at : at + WINDOW], 0.0), axis=-1, keepdims=True
            )
            first_lane = at + shift
            log_column = log_total[:, first_lane : first_lane + 1]
            terms = split_three(log_column) + split_three(inner_sum)
            for index, term in enumerate(terms):
                stats = jnp.where(out_lane == index * HEADS + head, term, stats)
        stats = stats.astype(BF)
        for (first, some), ref in zip(cuts, message_refs):
            ref[:, :lat] = grad_attended[first : first + some]
            ref[:, lat:] = stats[first : first + some]

    flat_parts = [array for some in parts for array in some]
    return pl.pallas_call(
        kernel,
        in_specs=[scalar_spec()]
        + [whole_spec()] * (len(flat_parts) + 2)
        + [any_spec()] * (gain_count + count),
        out_specs=[whole_spec()] * (7 + len(cuts)),
        out_shape=[shape((tokens, lat)), shape((tokens, lat), F32)]
        + [shape((some, lat + LANES)) for _, some in cuts]
        + [
            shape((lat, tokens)),
            shape((tokens, lat)),
            shape((lat, tokens)),
            shape((tokens, lat)),
            shape((lat, tokens)),
        ],
        scratch_shapes=[pltpu.VMEM((lat, lat), BF)] * 3
        + [
            pltpu.VMEM((held_gain.blocks * GAIN_ROWS, LANES), BF),
            pltpu.SemaphoreType.DMA((6 * count,)),
            pltpu.SemaphoreType.DMA((2 * gain_count,)),
        ],
        compiler_params=params(0),
        cost_estimate=SMALL,
        name="feed",
    )(place, *flat_parts, latent_message, cot_flat, *held_gain.flat, *held.flat)


def feed_grads_call(place, lefts, rights, n, far):
    lat, tokens = lefts[0].shape
    width = rights[0].shape[1]
    terms = len(lefts)

    def kernel(place_ref, *refs):
        left_refs, right_refs = refs[:terms], refs[terms : 2 * terms]
        outs = refs[2 * terms :]
        for distance in range(far):
            at = pl.multiple_of(jnp.bitwise_xor(place_ref[0], distance) * n, 16)
            for index in range(terms):
                chunk = left_refs[index][pl.ds(at, n), :]
                outs[distance][index * n : (index + 1) * n, :] = dot(
                    chunk, right_refs[index][...]
                ).astype(BF)

    return pl.pallas_call(
        kernel,
        in_specs=[scalar_spec()] + [whole_spec()] * (2 * terms),
        out_specs=[whole_spec()] * far,
        out_shape=[shape((terms * n, width))] * far,
        compiler_params=params(0),
        cost_estimate=SMALL,
        name="feed_grads",
    )(place, *lefts, *rights)


def attend_back_call(
    place, parts, queries, keys, values, byte_ids, held, groups, group, first, rows
):
    count_parts = len(parts)
    lat = keys.shape[1]
    block = byte_ids.shape[2]
    latents = groups * group
    count = len(held.flat)
    score_scale = 1.0 / math.sqrt(HEAD_DIM)

    def kernel(place_ref, *refs):
        refs = list(refs)
        take = lambda n: [refs.pop(0) for _ in range(n)]
        part_refs = take(count_parts)
        query_ref, key_ref, value_ref, bid_ref = take(4)
        piece_refs = take(count)
        grad_key_ref, grad_value_ref, grad_query_ref = take(3)
        up_refs = take(groups)
        wq, acc_q, acc_k, acc_v, sems = refs
        row = pl.program_id(0)

        def loads():
            return held.copies(("query",), piece_refs, (wq,), place_ref, sems)

        @pl.when(row == 0)
        def _():
            run_all(loads(), "start")

        message = jnp.concatenate(group_values(part_refs, place_ref), axis=0)
        stats = jnp.transpose(message[:, lat:].astype(F32), (1, 0))
        byte_ids = jnp.transpose(jnp.broadcast_to(bid_ref[0], (LANES, block)), (1, 0))[:, :1]
        allowed = byte_ids == stats[6 * HEADS : 6 * HEADS + 1, :]
        for head in range(HEADS):
            at, _ = head_window(head)
            mask = head_lanes(head)
            window = slice(at, at + WINDOW)
            stat = lambda k: stats[k * HEADS + head : k * HEADS + head + 1, :]
            log_total = stat(0) + stat(1) + stat(2)
            inner_sum = stat(3) + stat(4) + stat(5)
            query = jnp.where(mask, query_ref[:, window], jnp.zeros((), BF))
            grad = jnp.where(mask, message[:, window], jnp.zeros((), BF))
            key = key_ref[:, window]
            scores = dot(key, query, ((1,), (1,))) * score_scale
            probs = jnp.exp(jnp.where(allowed, scores - log_total, NEG_FILL))
            grad_probs = dot(value_ref[:, window], grad, ((1,), (1,)))
            grad_scores = (probs * (grad_probs - inner_sum)).astype(BF)
            found_k = dot(grad_scores, query)
            found_v = dot(probs.astype(BF), grad)
            found_q = dot(grad_scores, key, ((0,), (0,)))
            if head == 0:
                acc_k[:, window] = found_k
                acc_v[:, window] = found_v
                acc_q[:, window] = found_q
            else:
                acc_k[:, window] = jnp.where(mask, found_k, acc_k[:, window])
                acc_v[:, window] = jnp.where(mask, found_v, acc_v[:, window])
                acc_q[:, window] = jnp.where(mask, found_q, acc_q[:, window])

        grad_query = (acc_q[...] * score_scale).astype(BF)
        grad_key_ref[...] = (acc_k[...] * score_scale).astype(BF)
        grad_value_ref[...] = acc_v[...].astype(BF)
        grad_query_ref[...] = grad_query

        @pl.when(row == 0)
        def _():
            run_all(loads(), "wait")

        upstream = dot(grad_query, wq[...], ((1,), (1,))).astype(BF)
        for index, ref in enumerate(up_refs):
            ref[...] = upstream[index * group : (index + 1) * group, :]

    row_block = lambda i, p: (first + i, 0)
    own_block = lambda i, p: (i, 0)
    return pl.pallas_call(
        kernel,
        grid_spec=pltpu.PrefetchScalarGridSpec(
            num_scalar_prefetch=1,
            grid=(rows,),
            in_specs=[pl.BlockSpec((group, lat + LANES), own_block)] * count_parts
            + [
                pl.BlockSpec((latents, lat), own_block),
                pl.BlockSpec((block, lat), row_block),
                pl.BlockSpec((block, lat), row_block),
                pl.BlockSpec((1, 1, block), lambda i, p: (first + i, 0, 0)),
            ]
            + [any_spec()] * count,
            out_specs=[
                pl.BlockSpec((block, lat), own_block),
                pl.BlockSpec((block, lat), own_block),
                pl.BlockSpec((latents, lat), own_block),
            ]
            + [pl.BlockSpec((group, lat), own_block)] * groups,
            scratch_shapes=[
                pltpu.VMEM((lat, lat), BF),
                pltpu.VMEM((latents, lat), F32),
                pltpu.VMEM((block, lat), F32),
                pltpu.VMEM((block, lat), F32),
                pltpu.SemaphoreType.DMA((2 * count,)),
            ],
        ),
        out_shape=[shape((rows * block, lat))] * 2
        + [shape((rows * latents, lat))]
        + [shape((rows * group, lat))] * groups,
        compiler_params=params(1),
        cost_estimate=SMALL,
        name="attend_back",
    )(place, *parts, queries, keys, values, byte_ids, *held.flat)


def weight_grads_call(place, lefts, rights, some_rows, far):
    lat = rights[0][0].shape[1]
    chunk = sum(some_rows)
    left_counts, counts = [len(parts) for parts in lefts], [len(parts) for parts in rights]

    def kernel(place_ref, *refs):
        refs = list(refs)
        take = lambda n: [refs.pop(0) for _ in range(n)]
        left_refs = [take(n) for n in left_counts]
        right_refs = [take(n) for n in counts]
        outs = take(far)
        at = 0
        for index, (left, held) in enumerate(zip((0, 0, 1), refs)):
            factors, column, found = left_refs[left], 0, 0.0
            for part, right in enumerate(right_refs[index]):
                some = right.shape[0]
                if len(factors) > 1:
                    factor = factors[part][...]
                else:
                    factor = factors[0][:, column : column + some]
                found = found + dot(factor, right[...])
                column += some
            held[...] = found.astype(BF)
            some = some_rows[index]
            for distance in range(far):
                owner = jnp.bitwise_xor(place_ref[0], distance)
                outs[distance][at : at + some, :] = held[
                    pl.ds(pl.multiple_of(owner * some, 16), some), :
                ]
            at += some

    tile = lambda i, p: (0, i)
    flat_lefts = [left for parts in lefts for left in parts]
    flat_rights = [right for parts in rights for right in parts]
    return pl.pallas_call(
        kernel,
        grid_spec=pltpu.PrefetchScalarGridSpec(
            num_scalar_prefetch=1,
            grid=(lat // WINDOW,),
            in_specs=[full_block(left.shape) for left in flat_lefts]
            + [pl.BlockSpec((right.shape[0], WINDOW), tile) for right in flat_rights],
            out_specs=[pl.BlockSpec((chunk, WINDOW), tile)] * far,
            scratch_shapes=[pltpu.VMEM((lefts[i][0].shape[0], WINDOW), BF) for i in (0, 0, 1)],
        ),
        out_shape=[shape((chunk, lat))] * far,
        compiler_params=params(1),
        cost_estimate=SMALL,
        name="weight_grads",
    )(place, *flat_lefts, *flat_rights)


def byte_grad_call(place, bytes_flat, grads, held, rows, cuts):
    tokens, width = bytes_flat.shape
    block = tokens // rows
    lat = grads[0][0].shape[1]
    count = len(held.flat)
    shards = place_shards(held)

    def kernel(place_ref, x_ref, *refs):
        grad_refs = refs[: 2 * len(cuts)]
        piece_refs = refs[2 * len(cuts) : 2 * len(cuts) + count]
        out_ref, wk, wv, gains, gain, sems = refs[2 * len(cuts) + count :]
        row = pl.program_id(0)

        def loads():
            return held.copies(
                ("gains", "key", "value"), piece_refs, (gains, wk, wv), place_ref, sems
            )

        @pl.when(row == 0)
        def _():
            run_all(loads(), "start")

        xhat, scale = standardize(x_ref[...].astype(F32))

        @pl.when(row == 0)
        def _():
            run_all(loads(), "wait")
            gain[...] = gain_vector(gains, width, held.lanes["byte"], shards)

        for index, (first, some) in enumerate(cuts):

            @pl.when((row >= first) & (row < first + some))
            def _():
                upstream = dot(grad_refs[2 * index][...], wk[...], ((1,), (1,))) + dot(
                    grad_refs[2 * index + 1][...], wv[...], ((1,), (1,))
                )
                out_ref[...] = norm_pull(upstream, gain[...], xhat, scale)

    row_block = lambda i, p: (i, 0)

    def cut_block(first, some):
        return lambda i, p: (jnp.clip(i - first, 0, some - 1), 0)

    return pl.pallas_call(
        kernel,
        grid_spec=pltpu.PrefetchScalarGridSpec(
            num_scalar_prefetch=1,
            grid=(rows,),
            in_specs=[pl.BlockSpec((block, width), row_block)]
            + [pl.BlockSpec((block, lat), cut_block(*cut)) for cut in cuts for _ in range(2)]
            + [any_spec()] * count,
            out_specs=pl.BlockSpec((block, width), row_block),
            scratch_shapes=[
                pltpu.VMEM((width, lat), BF),
                pltpu.VMEM((width, lat), BF),
                pltpu.VMEM((held.blocks * GAIN_ROWS, LANES), BF),
                pltpu.VMEM((1, width), F32),
                pltpu.SemaphoreType.DMA((6 * count,)),
            ],
        ),
        out_shape=shape((tokens, width), F32),
        compiler_params=params(1),
        cost_estimate=SMALL,
        name="byte_grad",
    )(place, bytes_flat, *[g for some in grads for g in some], *held.flat)


def latent_grad_call(place, latent_message, grad_mixed, ups, held):
    tokens, lat = grad_mixed.shape
    cuts, groups = len(ups), len(ups[0])
    count = len(held.flat)
    shards = place_shards(held)

    def kernel(place_ref, x_ref, mixed_ref, *refs):
        up_refs = [refs[i * groups : (i + 1) * groups] for i in range(cuts)]
        piece_refs = refs[cuts * groups : cuts * groups + count]
        out_ref, gains, sems = refs[cuts * groups + count :]
        loads = held.copies(("gains",), piece_refs, (gains,), place_ref, sems)
        run_all(loads, "start")
        xhat, scale = standardize(x_ref[:, :lat].astype(F32))
        upstream = jnp.concatenate(
            [
                functools.reduce(jnp.add, [ref[...].astype(F32) for ref in some])
                for some in up_refs
            ],
            axis=0,
        )
        run_all(loads, "wait")
        gain = gain_vector(gains, lat, held.lanes["latent"], shards)
        out_ref[...] = mixed_ref[...] + norm_pull(upstream, gain, xhat, scale)

    return pl.pallas_call(
        kernel,
        in_specs=[scalar_spec()]
        + [whole_spec()] * (2 + cuts * groups)
        + [any_spec()] * count,
        out_specs=whole_spec(),
        out_shape=shape((tokens, lat), F32),
        scratch_shapes=[
            pltpu.VMEM((held.blocks * GAIN_ROWS, LANES), BF),
            pltpu.SemaphoreType.DMA((2 * count,)),
        ],
        compiler_params=params(0, 24),
        cost_estimate=SMALL,
        name="latent_grad",
    )(place, latent_message, grad_mixed, *[u for some in ups for u in some], *held.flat)


def swap(value, axis, size, distance):
    return lax.ppermute(value, axis, [(i, i ^ distance) for i in range(size)])


def tie(value, *earlier):
    return lax.optimization_barrier((value, *earlier))[0]


def passed(value, *earlier, cost):
    def kernel(in_ref, out_ref):
        pass

    return pl.pallas_call(
        kernel,
        in_specs=[any_spec()],
        out_specs=any_spec(),
        out_shape=shape(value.shape, value.dtype),
        input_output_aliases={0: 0},
        cost_estimate=pl.CostEstimate(
            flops=int(cost * 1.1e9), bytes_accessed=1, transcendentals=0
        ),
        name="passed",
    )(tie(value, *earlier))


def swap_all(parts, size):
    return [swap(parts[j], "fsdp", size, j) for j in range(1, size)]


def by_index(parts, own, size):
    if len(parts) == 5:
        parts = parts[:3] + [jnp.where((own == 0) | (own == 3), parts[4], parts[3])]
    return [lax.select_n(jnp.bitwise_xor(own, k), *parts) for k in range(size)]


def build_block(place, own, parts, sizes, size):
    segments, first, at = [], 0, 0
    for rows in sizes:
        segments.append((first, rows, at))
        first += rows
        at += rows * size
    total = up_to(at, 16)
    if all(first % 8 == 0 for first, _, _ in segments):
        return assemble_call(place, parts, segments, total, size)
    shards = by_index(parts, own, size)
    found = [s[first : first + rows] for first, rows, _ in segments for s in shards]
    return pad_rows(jnp.concatenate(found, axis=0), total)


def add(*values):
    return functools.reduce(jnp.add, [v.astype(F32) for v in values]).astype(BF)


def meet_call(first, high, second, low, half):
    rows, lat = first[0].shape

    def kernel(a, b, h, c, d, l, one, two):
        one[:half, :] = (a[:half, :].astype(F32) + b[:half, :].astype(F32)).astype(BF)
        one[half:, :] = (
            a[half:, :].astype(F32) + b[half:, :].astype(F32) + h[...].astype(F32)
        ).astype(BF)
        two[:half, :] = (
            c[:half, :].astype(F32) + d[:half, :].astype(F32) + l[...].astype(F32)
        ).astype(BF)
        two[half:, :] = (c[half:, :].astype(F32) + d[half:, :].astype(F32)).astype(BF)

    return pl.pallas_call(
        kernel,
        in_specs=[whole_spec()] * 6,
        out_specs=[whole_spec()] * 2,
        out_shape=[shape((rows, lat))] * 2,
        compiler_params=params(0, 24),
        cost_estimate=SMALL,
        name="meet",
    )(*first, high, *second, low)


def cut_call(place, terms, sizes, size):
    lat = terms[0].shape[1]
    rows = sum(sizes)

    def kernel(place_ref, *refs):
        term_refs, outs, acc = refs[: len(terms)], refs[len(terms) : -1], refs[-1]
        acc[...] = functools.reduce(jnp.add, [ref[...].astype(F32) for ref in term_refs])
        for distance, out in enumerate(outs):
            owner = jnp.bitwise_xor(place_ref[1], distance)
            found, at = [], 0
            for some in sizes:
                found.append(acc[pl.ds(pl.multiple_of(at + owner * some, 8), some), :])
                at += some * size
            out[...] = jnp.concatenate(found, axis=0).astype(out.dtype)

    return pl.pallas_call(
        kernel,
        in_specs=[scalar_spec()] + [whole_spec()] * len(terms),
        out_specs=[whole_spec()] * size,
        out_shape=[shape((rows, lat), F32)] + [shape((rows, lat))] * (size - 1),
        scratch_shapes=[pltpu.VMEM(terms[0].shape, F32)],
        compiler_params=params(0, 24),
        cost_estimate=SMALL,
        name="cut",
    )(place, *terms)


def cut_terms(place, own, terms, sizes, size):
    if all(some % 8 == 0 for some in sizes):
        return cut_call(place, terms, sizes, size)
    block = functools.reduce(jnp.add, [v.astype(F32) for v in terms])
    outs = []
    for distance in range(size):
        index = jnp.bitwise_xor(own, distance)
        found, at = [], 0
        for some in sizes:
            part = block[at : at + some * size].reshape(size, some, block.shape[1])
            found.append(lax.dynamic_index_in_dim(part, index, 0, keepdims=False))
            at += some * size
        value = jnp.concatenate(found, axis=0)
        outs.append(value if distance == 0 else value.astype(BF))
    return outs


def total(own, arrived):
    return functools.reduce(jnp.add, [v.astype(F32) for v in [own, *arrived]])


def split_rows(value, sizes):
    found, at = [], 0
    for some in sizes:
        found.append(value[at : at + some])
        at += some
    return found


def up_to(value, step):
    return -(-value // step) * step


def pad_rows(value, rows):
    return jnp.pad(value, ((0, rows - value.shape[0]), (0, 0)))


class Plan:
    def __init__(self, n_dp, n_f):
        self.n_dp, self.n_f = n_dp, n_f
        self.gate = ()

    def send(self, value, distance):
        return swap(tie(value, *self.gate), "dp", self.n_dp, distance)

    def pass_on(self, value, distance):
        return swap(tie(value, *self.gate), "fsdp", self.n_f, distance)

    def relay(self, own, two):
        middle = lax.ppermute(tie(own, *self.gate), "fsdp", [(1, 2), (2, 1)])
        return middle, lax.ppermute(tie(two, *self.gate), "fsdp", [(2, 3), (1, 0)])

    def spread(self, value):
        value = tie(value, *self.gate)
        middle = lax.ppermute(value, "fsdp", [(1, 2), (2, 1)])
        return middle, lax.ppermute(value, "fsdp", [(3, 2), (0, 1)])

    def tied(self, values):
        return [tie(values[0], *self.gate), *values[1:]]


def square_pieces(block, chips, half):
    rows = block.shape[0]
    full, halves = [(0, rows)], [(0, half), (half, rows)]
    pieces, flat = [], []
    for distance, parts, pairs in (
        (0, full, chips[:1]),
        (2, full, chips[1:2]),
        (4, full, chips[2:3]),
        (6, halves, chips[3:]),
    ):
        for core in range(2):
            pieces.append((distance + core, parts))
            flat.extend(pair[core] for pair in pairs)
    return pieces, flat


def local(n_dp, n_f, bytes_in, latents_in, cotangent, byte_segments, latent_segments,
          w_query, w_key, w_value, w_out, w_mlp_in, w_mlp_out,
          gain_latent, gain_byte, gain_mlp):
    rows, byte_local, width = bytes_in.shape
    _, group, lat = latents_in.shape
    dp, own = lax.axis_index("dp"), lax.axis_index("fsdp")
    place = jnp.stack([dp, own]).astype(jnp.int32)
    bytes_flat = bytes_in.reshape(rows * byte_local, width)
    latents_flat = latents_in.reshape(rows * group, lat)
    cot_flat = cotangent.reshape(rows * group, lat)
    kr, qr = w_key.shape[0], w_query.shape[0]
    key_rows, query_rows = n_f * kr, n_f * qr
    cuts = [(0, 1), (1, rows - 1)]
    cut_rows = [(first * group, some * group) for first, some in cuts]

    gains = jnp.concatenate([gain_latent, gain_byte, gain_mlp])
    gains = jnp.pad(gains, (0, lat - gains.shape[0]))[None, :]
    message_one = jnp.concatenate([w_key, w_value, w_query, gains], axis=0)
    message_one = pad_rows(message_one, up_to(2 * kr + qr + 1, 16))
    message_two = jnp.concatenate([w_out, w_mlp_in, w_mlp_out], axis=0)
    ids = latent_segments.reshape(rows * group, 1).astype(BF)
    ids = jnp.pad(ids, ((0, 0), (0, LANES - 1)))
    latent_message = jnp.concatenate([latents_flat, ids], axis=1)
    byte_ids = lax.dynamic_slice_in_dim(byte_segments, own * byte_local, byte_local, axis=1)
    byte_ids = byte_ids.astype(F32)
    byte_row = byte_ids[:, None, :]
    sizes_one, sizes_two = (kr, kr, qr), (qr, qr, qr)
    half_one, half_two = 2 * key_rows, up_to(3 * query_rows // 2, 16)
    spans_one = {
        "key": (0, key_rows),
        "value": (key_rows, key_rows),
        "query": (2 * key_rows, query_rows),
        "gains": (2 * key_rows + query_rows, GAIN_ROWS),
    }
    spans_two = {name: (i * query_rows, query_rows) for i, name in enumerate(("out", "inner", "outer"))}

    def held_one(pieces, flat):
        held = Held(pieces, flat, spans_one)
        held.blocks, held.size = n_dp, n_f
        held.lanes = {"latent": 0, "byte": qr, "mlp": qr + kr}
        return held

    def key_value(one, bytes_flat):
        return key_value_call(place, bytes_flat, one, rows)

    def attend(index, one, parts, keys, values):
        found = attend_call(
            place, parts, byte_row, keys, values, one, n_f, group, *cuts[index]
        )
        return found[0], found[1], found[2:]

    def feed(one, two, attended):
        return feed_call(place, attended, latent_message, cot_flat, one, two, cut_rows)

    def feed_grads(lefts, rights):
        return feed_grads_call(place, lefts, rights, query_rows, n_dp)

    def attend_back(index, one, parts, saved):
        return attend_back_call(
            place, parts, *saved, byte_row, one, n_f, group, *cuts[index]
        )

    def weight_grads(lefts, first, last):
        return weight_grads_call(
            place, lefts, list(zip(first, last)), (key_rows, key_rows, query_rows), n_dp
        )

    def byte_grad(one, grads):
        return byte_grad_call(place, bytes_flat, grads, one, rows, cuts)

    run = square if (n_dp, n_f) == (8, 4) else plain
    new, grad_latents, grad_bytes, grad_one, grad_two = run(**locals())

    def gain_grad(pairs, gain):
        found = sum(jnp.sum(w.astype(F32) * g, axis=1) for w, g in pairs)
        return found / gain.astype(F32)

    grad_key, grad_value, grad_query = split_rows(grad_one, sizes_one)
    grad_out, grad_inner, grad_outer = split_rows(grad_two, sizes_two)
    return (
        new.reshape(rows, group, lat),
        grad_latents.reshape(rows, group, lat),
        grad_bytes.reshape(rows, byte_local, width),
        grad_query,
        grad_key,
        grad_value,
        grad_out,
        grad_inner,
        grad_outer,
        gain_grad([(w_query, grad_query)], gain_latent),
        gain_grad([(w_key, grad_key), (w_value, grad_value)], gain_byte),
        gain_grad([(w_mlp_in, grad_inner)], gain_mlp),
    )


def plain(*, n_dp, n_f, place, own, bytes_flat, message_one, message_two, latent_message,
          sizes_one, sizes_two, spans_two, cot_flat, held_one, key_value, attend, feed,
          feed_grads, attend_back, weight_grads, byte_grad, **_):
    def gather(message, sizes):
        parts = [message, *swap_all([message] * n_f, n_f)]
        block = build_block(place, own, parts, sizes, n_f)
        flat = [block] + [swap(block, "dp", n_dp, d) for d in range(1, n_dp)]
        return [(d, [(0, block.shape[0])]) for d in range(n_dp)], flat

    def scatter(parts, sizes):
        terms = [parts[0]] + [swap(parts[d], "dp", n_dp, d) for d in range(1, n_dp)]
        cut = cut_terms(place, own, terms, sizes, n_f)
        return total(cut[0], swap_all(cut, n_f))

    one = held_one(*gather(message_one, (*sizes_one, 1)))
    two = Held(*gather(message_two, sizes_two), spans_two)
    byte_t, keys, values = key_value(one, bytes_flat)
    latent_parts = [latent_message, *swap_all([latent_message] * n_f, n_f)]
    latent_t, queries, found = zip(*[attend(i, one, latent_parts, keys, values) for i in range(2)])
    attended = list(zip(*[[f[0], *swap_all(f, n_f)] for f in found]))
    new, grad_mixed, *messages, attended_t, branch, normed_t, inner, act_t = feed(
        one, two, attended
    )
    grad_two = scatter(feed_grads((attended_t, normed_t, act_t), (branch, inner, cot_flat)), sizes_two)
    parts = [[m, *swap_all([m] * n_f, n_f)] for m in messages]
    first, last = [attend_back(i, one, parts[i], (queries[i], keys, values)) for i in range(2)]
    grad_bytes = byte_grad(one, (first[:2], last[:2]))
    grad_one = scatter(weight_grads(((byte_t,), latent_t), first[:3], last[:3]), sizes_one)
    ups = [[ups[0], *swap_all(ups, n_f)] for ups in (first[3:], last[3:])]
    grad_latents = latent_grad_call(place, latent_message, grad_mixed, ups, one)
    return new, grad_latents, grad_bytes, grad_one, grad_two


def square(*, n_dp, n_f, place, own, bytes_flat, message_one, message_two, latent_message,
           sizes_one, sizes_two, spans_two, half_one, half_two, cot_flat, held_one, key_value,
           attend, feed, feed_grads, attend_back, weight_grads, byte_grad, **_):
    plan = Plan(n_dp, n_f)
    send, pass_on = plan.send, plan.pass_on

    near = [pass_on(message_one, 2), pass_on(message_one, 1)]
    plan.gate = near
    parts = [message_one, near[1], near[0], *plan.relay(message_one, near[0])]
    block = build_block(place, own, parts, (*sizes_one, 1), n_f)
    plan.gate = [block]
    x, y, other = send(block, 2), send(block, 4), send(block, 1)
    latent_two, latent_one = pass_on(latent_message, 2), pass_on(latent_message, 1)
    plan.gate = [x, y]
    low, high = send(x[:half_one], 4), send(y[half_one:], 2)
    latent_two = passed(latent_two, latent_one, cost=12)
    plan.gate = [x, y, latent_two]
    latent_parts = [
        latent_message, latent_one, latent_two, *plan.relay(latent_message, latent_two)
    ]
    plan.gate = [low, high, other]
    others = [send(v, 1) for v in (x, y, low, high)]
    pairs = list(zip((block, x, y, low, high), (other, *others)))
    one = held_one(*square_pieces(block, pairs, half_one))
    plan.gate = [low, high, latent_two]
    two_two, two_one = pass_on(message_two, 2), pass_on(message_two, 1)
    plan.gate = others
    byte_t, keys, values = key_value(one, tie(bytes_flat, *plan.gate))
    plan.gate = [two_two, two_one, keys]
    parts = [message_two, two_one, two_two, *plan.relay(message_two, two_two)]
    latent_t_first, queries_first, found = attend(0, one, plan.tied(latent_parts), keys, values)
    plan.gate = [queries_first, *parts[3:]]
    block = build_block(place, own, plan.tied(parts), sizes_two, n_f)
    x, y = send(block, 2), send(block, 4)
    attended_first = [found[0], *[pass_on(found[j], j) for j in range(1, n_f)]]
    plan.gate = [block]
    latent_t_last, queries_last, found = attend(1, one, plan.tied(latent_parts), keys, values)
    plan.gate = attended_first[1:]
    attended_last = [found[0], *[pass_on(found[j], j) for j in range(1, n_f)]]
    plan.gate = [x, y, queries_last, *attended_first[1:]]
    low, high = send(x[:half_two], 4), send(y[half_two:], 2)
    attended_last[1] = passed(attended_last[1], *attended_last[2:], cost=4)
    plan.gate = [low, high, *attended_last[1:]]
    pairs = [(v, send(v, 1)) for v in (block, x, y, low, high)]
    two = Held(*square_pieces(block, pairs, half_two), spans_two)
    new, grad_mixed, first, last, attended_t, branch, normed_t, inner, act_t = feed(
        one, two, list(zip(attended_first, attended_last))
    )
    plan.gate = []
    near = [pass_on(first, 2), pass_on(first, 1)]
    grads = feed_grads((attended_t, normed_t, act_t), (branch, inner, cot_flat))
    plan.gate = near
    first_parts = [first, near[1], near[0], *plan.relay(first, near[0])]
    near = [pass_on(last, 2), pass_on(last, 1)]
    arrived = {d: send(grads[d + 1], 1) for d in (6, 4)}
    low = add(grads[6][:half_two], arrived[6][:half_two])
    high = add(grads[6][half_two:], arrived[6][half_two:])
    plan.gate = [*arrived.values(), *first_parts[3:]]
    low, high = send(low, 2), send(high, 4)
    arrived[2] = send(grads[3], 1)
    back_first = attend_back(0, one, plan.tied(first_parts), (queries_first, keys, values))
    plan.gate = [low, high, arrived[2], *near, back_first[0]]
    last_parts = [last, near[1], near[0], *plan.relay(last, near[0])]
    arrived[0] = send(grads[1], 1)
    x, y = meet_call(
        (grads[2], arrived[2]), tie(high, *plan.gate), (grads[4], arrived[4]), low, half_two
    )
    plan.gate = [x, y, arrived[0], *last_parts[3:]]
    terms_two = [grads[0], arrived[0], send(x, 2), send(y, 4)]
    ups_first = back_first[3:]
    ups_first = [ups_first[0], *[pass_on(ups_first[j], j) for j in range(1, n_f)]]
    back_last = attend_back(1, one, plan.tied(last_parts), (queries_last, keys, values))
    plan.gate = [back_last[0], *ups_first[1:]]
    ups = back_last[3:]
    near = [pass_on(ups[1], 1), *plan.spread(ups[3])]
    grads = weight_grads(
        ((byte_t,), (latent_t_first, latent_t_last)),
        back_first[:3],
        [tie(back_last[0], *plan.gate), *back_last[1:3]],
    )
    plan.gate = [*near, grads[0], *terms_two[2:]]
    arrived = {d: send(grads[d + 1], 1) for d in (6, 4, 2)}
    low = add(grads[6][:half_one], arrived[6][:half_one])
    high = add(grads[6][half_one:], arrived[6][half_one:])
    merged = add(tie(ups[2], *plan.gate), near[2])
    plan.gate = [low, high, merged, *arrived.values()]
    low, high = send(low, 2), send(high, 4)
    ups_last = [ups[0], *near[:2], pass_on(merged, 2)]
    cut_two = cut_terms(place, own, plan.tied(terms_two), sizes_two, n_f)
    plan.gate = [low, high, cut_two[0]]
    x, y = meet_call(
        (grads[2], arrived[2]), tie(high, *plan.gate), (grads[4], arrived[4]), low, half_one
    )
    arrived_two = [pass_on(cut_two[j], j) for j in range(1, n_f)]
    plan.gate = [x, y]
    terms_one = [grads[0], None, send(x, 2), send(y, 4)]
    grad_bytes = byte_grad(one, (plan.tied(back_first[:2]), back_last[:2]))
    plan.gate = [x, y, ups_last[-1]]
    terms_one[1] = send(grads[1], 1)
    plan.gate = [*terms_one[1:], grad_bytes]
    cut_one = cut_terms(place, own, plan.tied(terms_one), sizes_one, n_f)
    plan.gate = [cut_one[0]]
    grad_one = total(cut_one[0], [pass_on(cut_one[j], j) for j in range(1, n_f)])
    grad_two = total(cut_two[0], arrived_two)
    grad_latents = latent_grad_call(
        place, latent_message, tie(grad_mixed, *plan.gate), [ups_first, ups_last], one
    )
    return new, grad_latents, grad_bytes, grad_one, grad_two


def solution(mesh):
    rows3 = P("dp", "fsdp", None)
    split2 = P(("dp", "fsdp"), None)
    split1 = P(("dp", "fsdp"))
    in_specs = (rows3,) * 3 + (P("dp", None), P("dp", "fsdp")) + (split2,) * 6 + (split1,) * 3
    out_specs = (rows3,) * 3 + (split2,) * 6 + (split1,) * 3
    body = functools.partial(local, mesh.shape["dp"], mesh.shape["fsdp"])
    return jax.shard_map(
        body, mesh=mesh, in_specs=in_specs, out_specs=out_specs, check_vma=False
    )
```

```python
import functools
import math

import jax
import jax.numpy as jnp
from jax import lax
from jax.experimental import pallas as pl
from jax.experimental.pallas import tpu as pltpu
from jax.sharding import PartitionSpec as P

HEADS = 8
HEAD_DIM = 160
EPSILON = 1e-05
NEG_FILL = -1e30
LANES = 128
WINDOW = 256
BF = jnp.bfloat16
F32 = jnp.float32
GAIN_ROWS = 16
SMALL = pl.CostEstimate(flops=1, bytes_accessed=1, transcendentals=0)


def head_window(head):
    start = head * HEAD_DIM // LANES * LANES
    return start, head * HEAD_DIM - start


def head_lanes(head):
    _, shift = head_window(head)
    lane = lax.broadcasted_iota(jnp.int32, (1, WINDOW), 1)
    return (lane >= shift) & (lane < shift + HEAD_DIM)


def dot(a, b, dims=((1,), (0,))):
    return lax.dot_general(a, b, (dims, ((), ())), preferred_element_type=F32)


def standardize(values):
    centered = values - jnp.mean(values, axis=-1, keepdims=True)
    scale = lax.rsqrt(jnp.mean(centered * centered, axis=-1, keepdims=True) + EPSILON)
    return centered * scale, scale


def norm_pull(upstream, gain, xhat, scale):
    scaled = upstream * gain
    return scale * (
        scaled
        - jnp.mean(scaled, axis=-1, keepdims=True)
        - xhat * jnp.mean(scaled * xhat, axis=-1, keepdims=True)
    )


def split_three(values):
    first = values.astype(BF).astype(F32)
    rest = values - first
    second = rest.astype(BF).astype(F32)
    return first, second, rest - second


def gelu(values):
    inner = math.sqrt(2 / math.pi) * (values + 0.044715 * values * values * values)
    return 0.5 * values * (1.0 + jnp.tanh(inner))


def gelu_slope(values):
    square = values * values
    tanh = jnp.tanh(math.sqrt(2 / math.pi) * (values + 0.044715 * square * values))
    slope = math.sqrt(2 / math.pi) * (1.0 + 3 * 0.044715 * square)
    return 0.5 * (1.0 + tanh) + 0.5 * values * (1.0 - tanh * tanh) * slope


def piece_copies(pieces, flat_refs, first, rows, target, me, sems, base):
    copies = []
    lanes = target.shape[1]
    at = 0
    for distance, parts in pieces:
        owner = jnp.bitwise_xor(me, distance)
        for low, high in parts:
            ref = flat_refs[at]
            at += 1
            start, stop = max(low, first), min(high, first + rows)
            if start < stop:
                place = pl.multiple_of(owner * rows + (start - first), 16)
                copies.append(
                    pltpu.make_async_copy(
                        ref.at[pl.ds(start - low, stop - start), pl.ds(0, lanes)],
                        target.at[pl.ds(place, stop - start), :],
                        sems.at[base + len(copies)],
                    )
                )
    return copies


def group_values(refs, place):
    if len(refs) != 5:
        return [ref[...] for ref in refs]
    own = place[1]
    at_end = (own == 0) | (own == 3)
    values = [ref[...] for ref in refs[:3]]
    return values + [jnp.where(at_end, refs[4][...], refs[3][...])]


def gain_vector(held, size, lane_at, shards):
    per_shard = size // shards
    blocks = held.shape[0] // GAIN_ROWS
    per_block = shards // blocks
    lane = lax.broadcasted_iota(jnp.int32, (LANES, size), 0)
    column = lax.broadcasted_iota(jnp.int32, (LANES, size), 1)
    pick = (lane == lane_at + column % per_shard).astype(F32).astype(BF)
    spread = dot(held[...], pick)
    row = lax.broadcasted_iota(jnp.int32, spread.shape, 0)
    column = lax.broadcasted_iota(jnp.int32, spread.shape, 1) // per_shard
    owner = (row // GAIN_ROWS) * per_block + row % GAIN_ROWS
    right = (owner == column) & (row % GAIN_ROWS < per_block)
    return jnp.sum(jnp.where(right, spread, 0.0), axis=0, keepdims=True)


def params(grid_rank, mebibytes=60):
    return pltpu.CompilerParams(
        dimension_semantics=("arbitrary",) * grid_rank, vmem_limit_bytes=mebibytes << 20
    )


def whole_spec():
    return pl.BlockSpec(memory_space=pltpu.VMEM)


def any_spec():
    return pl.BlockSpec(memory_space=pltpu.HBM)


class Held:
    def __init__(self, pieces, flat, spans):
        self.pieces, self.flat, self.spans = pieces, flat, spans

    def crossed(self):
        at = 0
        for distance, parts in self.pieces:
            if distance == self.blocks - 2:
                return self.flat[at : at + len(parts)]
            at += len(parts)

    def copies(self, names, refs, targets, place, sems):
        found, base = [], 0
        for name, target in zip(names, targets):
            first, rows = self.spans[name]
            some = piece_copies(self.pieces, refs, first, rows, target, place[0], sems, base)
            base += len(some)
            found.append(some)
        return found


def run_all(groups, action):
    for group in groups:
        for copy in group:
            getattr(copy, action)()


def shape(dims, dtype=BF):
    return jax.ShapeDtypeStruct(dims, dtype)


def full_block(dims):
    return pl.BlockSpec(
        dims, lambda i, p: (0,) * len(dims), pipeline_mode=pl.Buffered(buffer_count=1)
    )


def scalar_spec():
    return pl.BlockSpec(memory_space=pltpu.SMEM)


def assemble_call(place, parts, segments, total, size):
    def kernel(place_ref, *refs):
        part_refs, out_ref, acc = refs[: len(parts)], refs[len(parts)], refs[len(parts) + 1]
        values = [v.astype(F32) for v in group_values(part_refs, place_ref)]
        end = max(at + size * rows for _, rows, at in segments)
        if end < total:
            first = end // 8 * 8
            acc[first:, :] = jnp.zeros((total - first, acc.shape[1]), F32)
        for index in range(size):
            want = jnp.bitwise_xor(place_ref[1], index)
            value = values[size - 1]
            for distance in range(size - 2, -1, -1):
                value = jnp.where(want == distance, values[distance], value)
            for first, rows, at in segments:
                acc[at + index * rows : at + (index + 1) * rows, :] = value[first : first + rows]
        out_ref[...] = acc[...].astype(BF)

    lat = parts[0].shape[1]
    return pl.pallas_call(
        kernel,
        in_specs=[scalar_spec()] + [whole_spec()] * len(parts),
        out_specs=whole_spec(),
        out_shape=shape((total, lat)),
        scratch_shapes=[pltpu.VMEM((total, lat), F32)],
        compiler_params=params(0, 24),
        cost_estimate=SMALL,
        name="assemble",
    )(place, *parts)


def key_value_call(place, bytes_flat, held, rows):
    tokens, width = bytes_flat.shape
    block = tokens // rows
    lat = held.flat[0].shape[1]
    count = len(held.flat)
    shards = place_shards(held)

    def kernel(place_ref, x_ref, *refs):
        piece_refs = refs[:count]
        normed_t_ref, key_ref, value_ref, wk, wv, gains, gain, sems = refs[count:]
        first = pl.program_id(0) == 0

        def loads():
            return held.copies(
                ("gains", "key", "value"), piece_refs, (gains, wk, wv), place_ref, sems
            )

        @pl.when(first)
        def _():
            run_all(loads(), "start")

        xhat, _ = standardize(x_ref[...].astype(F32))

        @pl.when(first)
        def _():
            run_all(loads(), "wait")
            gain[...] = gain_vector(gains, width, held.lanes["byte"], shards)

        normed = (xhat * gain[...]).astype(BF)
        key_ref[...] = dot(normed, wk[...]).astype(BF)
        value_ref[...] = dot(normed, wv[...]).astype(BF)
        normed_t_ref[...] = jnp.transpose(normed, (1, 0))

    row_block = lambda i, p: (i, 0)
    return pl.pallas_call(
        kernel,
        grid_spec=pltpu.PrefetchScalarGridSpec(
            num_scalar_prefetch=1,
            grid=(rows,),
            in_specs=[pl.BlockSpec((block, width), row_block)] + [any_spec()] * count,
            out_specs=[
                pl.BlockSpec((width, block), lambda i, p: (0, i)),
                pl.BlockSpec((block, lat), row_block),
                pl.BlockSpec((block, lat), row_block),
            ],
            scratch_shapes=[
                pltpu.VMEM((width, lat), BF),
                pltpu.VMEM((width, lat), BF),
                pltpu.VMEM((held.blocks * GAIN_ROWS, LANES), BF),
                pltpu.VMEM((1, width), F32),
                pltpu.SemaphoreType.DMA((6 * count,)),
            ],
        ),
        out_shape=[shape((width, tokens)), shape((tokens, lat)), shape((tokens, lat))],
        compiler_params=params(1),
        cost_estimate=SMALL,
        name="keys_values",
    )(place, bytes_flat, *held.flat)


def place_shards(held):
    return held.blocks * held.size


def attend_call(place, latent_parts, byte_ids, keys, values, held, groups, group, first, rows):
    parts = len(latent_parts)
    lat = keys.shape[1]
    block = byte_ids.shape[2]
    latents = groups * group
    count = len(held.flat)
    shards = place_shards(held)
    score_scale = 1.0 / math.sqrt(HEAD_DIM)

    def kernel(place_ref, *refs):
        part_refs = refs[:parts]
        bid_ref, key_ref, value_ref = refs[parts : parts + 3]
        piece_refs = refs[parts + 3 : parts + 3 + count]
        rest = refs[parts + 3 + count :]
        normed_t_ref, query_ref = rest[:2]
        out_refs = rest[2 : 2 + groups]
        wq, gains, gain, acc, sems = rest[2 + groups :]
        start = pl.program_id(0) == 0

        def loads():
            return held.copies(("gains", "query"), piece_refs, (gains, wq), place_ref, sems)

        @pl.when(start)
        def _():
            run_all(loads(), "start")

        message = jnp.concatenate(group_values(part_refs, place_ref), axis=0)
        ids = message[:, lat : lat + 1].astype(F32)
        xhat, _ = standardize(message[:, :lat].astype(F32))

        @pl.when(start)
        def _():
            run_all(loads(), "wait")
            gain[...] = gain_vector(gains, lat, held.lanes["latent"], shards)

        normed = (xhat * gain[...]).astype(BF)
        query_ref[...] = dot(normed, wq[...]).astype(BF)
        normed_t_ref[...] = jnp.transpose(normed, (1, 0))
        allowed = ids == bid_ref[0]
        lane = lax.broadcasted_iota(jnp.int32, (latents, LANES), 1)
        stats = jnp.zeros((latents, LANES), F32)
        for head in range(HEADS):
            at, _ = head_window(head)
            mask = head_lanes(head)
            window = slice(at, at + WINDOW)
            query = jnp.where(mask, query_ref[:, window], jnp.zeros((), BF))
            scores = dot(query, key_ref[:, window], ((1,), (1,))) * score_scale
            scores = jnp.where(allowed, scores, NEG_FILL)
            top = jnp.max(scores, axis=-1, keepdims=True)
            exponent = jnp.exp(scores - top)
            total = jnp.sum(exponent, axis=-1, keepdims=True)
            found = dot(exponent.astype(BF), value_ref[:, window]) / total
            if head == 0:
                acc[:, window] = found
            else:
                acc[:, window] = jnp.where(mask, found, acc[:, window])
            log_total = jnp.where(top > -1e29, top + jnp.log(total), NEG_FILL)
            for index, term in enumerate(split_three(log_total)):
                stats = jnp.where(lane == index * HEADS + head, term, stats)
        for index, ref in enumerate(out_refs):
            chunk = slice(index * group, (index + 1) * group)
            ref[:, :lat] = acc[chunk, :].astype(BF)
            ref[:, lat:] = stats[chunk, :].astype(BF)

    row_block = lambda i, p: (first + i, 0)
    own_block = lambda i, p: (i, 0)
    return pl.pallas_call(
        kernel,
        grid_spec=pltpu.PrefetchScalarGridSpec(
            num_scalar_prefetch=1,
            grid=(rows,),
            in_specs=[pl.BlockSpec((group, lat + LANES), row_block)] * parts
            + [
                pl.BlockSpec((1, 1, block), lambda i, p: (first + i, 0, 0)),
                pl.BlockSpec((block, lat), row_block),
                pl.BlockSpec((block, lat), row_block),
            ]
            + [any_spec()] * count,
            out_specs=[
                pl.BlockSpec((lat, latents), lambda i, p: (0, i)),
                pl.BlockSpec((latents, lat), own_block),
            ]
            + [pl.BlockSpec((group, lat + LANES), own_block)] * groups,
            scratch_shapes=[
                pltpu.VMEM((lat, lat), BF),
                pltpu.VMEM((held.blocks * GAIN_ROWS, LANES), BF),
                pltpu.VMEM((1, lat), F32),
                pltpu.VMEM((latents, lat), F32),
                pltpu.SemaphoreType.DMA((4 * count,)),
            ],
        ),
        out_shape=[shape((lat, rows * latents)), shape((rows * latents, lat))]
        + [shape((rows * group, lat + LANES))] * groups,
        compiler_params=params(1),
        cost_estimate=SMALL,
        name="attend",
    )(place, *latent_parts, byte_ids, keys, values, *held.flat)


def feed_call(place, parts, latent_message, cot_flat, held_gain, held, cuts):
    groups, pieces_of = len(parts), len(parts[0])
    tokens, lat = cot_flat.shape
    count, gain_count = len(held.flat), len(held_gain.flat)
    shards = place_shards(held_gain)

    def kernel(place_ref, *refs):
        refs = list(refs)
        take = lambda n: [refs.pop(0) for _ in range(n)]
        part_refs = [take(pieces_of) for _ in range(groups)]
        x_ref, cot_ref = take(2)
        gain_refs, piece_refs = take(gain_count), take(count)
        new_ref, mixed_grad_ref = take(2)
        message_refs = take(len(cuts))
        attended_t, branch, normed_t, inner, act_t = take(5)
        wo, w1, w2, gains, sems, gain_sems = refs
        gain_loads = held_gain.copies(("gains",), gain_refs, (gains,), place_ref, gain_sems)
        loads = held.copies(("out", "inner", "outer"), piece_refs, (wo, w1, w2), place_ref, sems)
        run_all(gain_loads, "start")
        run_all(loads, "start")

        lane = lax.broadcasted_iota(jnp.int32, (LANES, lat), 0)
        column = lax.broadcasted_iota(jnp.int32, (LANES, lat), 1)
        spread = jnp.zeros((LANES, lat), jnp.bool_)
        for head in range(HEADS):
            inside = (column >= head * HEAD_DIM) & (column < (head + 1) * HEAD_DIM)
            own = (lane == head) | (lane == HEADS + head) | (lane == 2 * HEADS + head)
            spread = spread | (inside & own)
        spread = spread.astype(F32).astype(BF)
        found = [jnp.concatenate([ref[...] for ref in some], axis=0) for some in part_refs]
        logs = [dot(value[:, lat:], spread) for value in found]
        top = functools.reduce(jnp.maximum, logs)
        shares = [jnp.exp(log - top) for log in logs]
        total = functools.reduce(jnp.add, shares)
        summed = functools.reduce(
            jnp.add, [s * value[:, :lat].astype(F32) for s, value in zip(shares, found)]
        )
        attended = (summed / total).astype(BF)
        log_total = top + jnp.log(total)
        attended_t[...] = jnp.transpose(attended, (1, 0))

        run_all(gain_loads, "wait")
        gain = gain_vector(gains, lat, held_gain.lanes["mlp"], shards)
        run_all(loads[:1], "wait")
        mixed = x_ref[:, :lat].astype(F32) + dot(attended, wo[...])
        xhat, scale = standardize(mixed)
        normed = (xhat * gain).astype(BF)
        normed_t[...] = jnp.transpose(normed, (1, 0))
        run_all(loads[1:2], "wait")
        hidden = dot(normed, w1[...])
        activated = gelu(hidden).astype(BF)
        act_t[...] = jnp.transpose(activated, (1, 0))
        run_all(loads[2:], "wait")
        new_ref[...] = (mixed + dot(activated, w2[...])).astype(BF)
        cot = cot_ref[...]
        grad_hidden = (dot(cot, w2[...], ((1,), (1,))) * gelu_slope(hidden)).astype(BF)
        inner[...] = grad_hidden
        upstream = dot(grad_hidden, w1[...], ((1,), (1,)))
        grad_mixed = cot.astype(F32) + norm_pull(upstream, gain, xhat, scale)
        mixed_grad_ref[...] = grad_mixed
        grad_branch = grad_mixed.astype(BF)
        branch[...] = grad_branch
        grad_attended = dot(grad_branch, wo[...], ((1,), (1,))).astype(BF)
        product = grad_attended.astype(F32) * attended.astype(F32)
        out_lane = lax.broadcasted_iota(jnp.int32, (tokens, LANES), 1)
        ids = x_ref[:, lat : lat + 1].astype(F32)
        stats = jnp.where(out_lane == 6 * HEADS, ids, 0.0)
        for head in range(HEADS):
            at, shift = head_window(head)
            mask = head_lanes(head)
            inner_sum = jnp.sum(
                jnp.where(mask, product[:, at : at + WINDOW], 0.0), axis=-1, keepdims=True
            )
            first_lane = at + shift
            log_column = log_total[:, first_lane : first_lane + 1]
            terms = split_three(log_column) + split_three(inner_sum)
            for index, term in enumerate(terms):
                stats = jnp.where(out_lane == index * HEADS + head, term, stats)
        stats = stats.astype(BF)
        for (first, some), ref in zip(cuts, message_refs):
            ref[:, :lat] = grad_attended[first : first + some]
            ref[:, lat:] = stats[first : first + some]

    flat_parts = [array for some in parts for array in some]
    return pl.pallas_call(
        kernel,
        in_specs=[scalar_spec()]
        + [whole_spec()] * (len(flat_parts) + 2)
        + [any_spec()] * (gain_count + count),
        out_specs=[whole_spec()] * (7 + len(cuts)),
        out_shape=[shape((tokens, lat)), shape((tokens, lat), F32)]
        + [shape((some, lat + LANES)) for _, some in cuts]
        + [
            shape((lat, tokens)),
            shape((tokens, lat)),
            shape((lat, tokens)),
            shape((tokens, lat)),
            shape((lat, tokens)),
        ],
        scratch_shapes=[pltpu.VMEM((lat, lat), BF)] * 3
        + [
            pltpu.VMEM((held_gain.blocks * GAIN_ROWS, LANES), BF),
            pltpu.SemaphoreType.DMA((6 * count,)),
            pltpu.SemaphoreType.DMA((2 * gain_count,)),
        ],
        compiler_params=params(0),
        cost_estimate=SMALL,
        name="feed",
    )(place, *flat_parts, latent_message, cot_flat, *held_gain.flat, *held.flat)


def feed_grads_call(place, lefts, rights, n, groups):
    lat, tokens = lefts[0].shape
    width = rights[0].shape[1]
    terms = len(lefts)

    def kernel(place_ref, *refs):
        left_refs, right_refs = refs[:terms], refs[terms : 2 * terms]
        for out, group in zip(refs[2 * terms :], groups):
            for number, distance in enumerate(group):
                at = pl.multiple_of(jnp.bitwise_xor(place_ref[0], distance) * n, 16)
                for index in range(terms):
                    chunk = left_refs[index][pl.ds(at, n), :]
                    first = (number * terms + index) * n
                    out[first : first + n, :] = dot(chunk, right_refs[index][...]).astype(BF)

    return pl.pallas_call(
        kernel,
        in_specs=[scalar_spec()] + [whole_spec()] * (2 * terms),
        out_specs=[whole_spec()] * len(groups),
        out_shape=[shape((len(group) * terms * n, width)) for group in groups],
        compiler_params=params(0),
        cost_estimate=SMALL,
        name="feed_grads",
    )(place, *lefts, *rights)


def attend_back_call(
    place, parts, queries, keys, values, byte_ids, held, groups, group, first, rows
):
    count_parts = len(parts)
    lat = keys.shape[1]
    block = byte_ids.shape[2]
    latents = groups * group
    count = len(held.flat)
    score_scale = 1.0 / math.sqrt(HEAD_DIM)

    def kernel(place_ref, *refs):
        refs = list(refs)
        take = lambda n: [refs.pop(0) for _ in range(n)]
        part_refs = take(count_parts)
        query_ref, key_ref, value_ref, bid_ref = take(4)
        piece_refs = take(count)
        grad_key_ref, grad_value_ref, grad_query_ref = take(3)
        up_refs = take(groups)
        wq, acc_q, acc_k, acc_v, sems = refs
        row = pl.program_id(0)

        def loads():
            return held.copies(("query",), piece_refs, (wq,), place_ref, sems)

        @pl.when(row == 0)
        def _():
            run_all(loads(), "start")

        message = jnp.concatenate(group_values(part_refs, place_ref), axis=0)
        stats = jnp.transpose(message[:, lat:].astype(F32), (1, 0))
        byte_ids = jnp.transpose(jnp.broadcast_to(bid_ref[0], (LANES, block)), (1, 0))[:, :1]
        allowed = byte_ids == stats[6 * HEADS : 6 * HEADS + 1, :]
        for head in range(HEADS):
            at, _ = head_window(head)
            mask = head_lanes(head)
            window = slice(at, at + WINDOW)
            stat = lambda k: stats[k * HEADS + head : k * HEADS + head + 1, :]
            log_total = stat(0) + stat(1) + stat(2)
            inner_sum = stat(3) + stat(4) + stat(5)
            query = jnp.where(mask, query_ref[:, window], jnp.zeros((), BF))
            grad = jnp.where(mask, message[:, window], jnp.zeros((), BF))
            key = key_ref[:, window]
            scores = dot(key, query, ((1,), (1,))) * score_scale
            probs = jnp.exp(jnp.where(allowed, scores - log_total, NEG_FILL))
            grad_probs = dot(value_ref[:, window], grad, ((1,), (1,)))
            grad_scores = (probs * (grad_probs - inner_sum)).astype(BF)
            found_k = dot(grad_scores, query)
            found_v = dot(probs.astype(BF), grad)
            found_q = dot(grad_scores, key, ((0,), (0,)))
            if head == 0:
                acc_k[:, window] = found_k
                acc_v[:, window] = found_v
                acc_q[:, window] = found_q
            else:
                acc_k[:, window] = jnp.where(mask, found_k, acc_k[:, window])
                acc_v[:, window] = jnp.where(mask, found_v, acc_v[:, window])
                acc_q[:, window] = jnp.where(mask, found_q, acc_q[:, window])

        grad_query = (acc_q[...] * score_scale).astype(BF)
        grad_key_ref[...] = (acc_k[...] * score_scale).astype(BF)
        grad_value_ref[...] = acc_v[...].astype(BF)
        grad_query_ref[...] = grad_query

        @pl.when(row == 0)
        def _():
            run_all(loads(), "wait")

        upstream = dot(grad_query, wq[...], ((1,), (1,))).astype(BF)
        for index, ref in enumerate(up_refs):
            ref[...] = upstream[index * group : (index + 1) * group, :]

    row_block = lambda i, p: (first + i, 0)
    own_block = lambda i, p: (i, 0)
    return pl.pallas_call(
        kernel,
        grid_spec=pltpu.PrefetchScalarGridSpec(
            num_scalar_prefetch=1,
            grid=(rows,),
            in_specs=[pl.BlockSpec((group, lat + LANES), own_block)] * count_parts
            + [
                pl.BlockSpec((latents, lat), own_block),
                pl.BlockSpec((block, lat), row_block),
                pl.BlockSpec((block, lat), row_block),
                pl.BlockSpec((1, 1, block), lambda i, p: (first + i, 0, 0)),
            ]
            + [any_spec()] * count,
            out_specs=[
                pl.BlockSpec((block, lat), own_block),
                pl.BlockSpec((block, lat), own_block),
                pl.BlockSpec((latents, lat), own_block),
            ]
            + [pl.BlockSpec((group, lat), own_block)] * groups,
            scratch_shapes=[
                pltpu.VMEM((lat, lat), BF),
                pltpu.VMEM((latents, lat), F32),
                pltpu.VMEM((block, lat), F32),
                pltpu.VMEM((block, lat), F32),
                pltpu.SemaphoreType.DMA((2 * count,)),
            ],
        ),
        out_shape=[shape((rows * block, lat))] * 2
        + [shape((rows * latents, lat))]
        + [shape((rows * group, lat))] * groups,
        compiler_params=params(1),
        cost_estimate=SMALL,
        name="attend_back",
    )(place, *parts, queries, keys, values, byte_ids, *held.flat)


def weight_grads_call(place, lefts, rights, some_rows, groups):
    lat = rights[0][0].shape[1]
    chunk = sum(some_rows)
    left_counts, counts = [len(parts) for parts in lefts], [len(parts) for parts in rights]

    def kernel(place_ref, *refs):
        refs = list(refs)
        take = lambda n: [refs.pop(0) for _ in range(n)]
        left_refs = [take(n) for n in left_counts]
        right_refs = [take(n) for n in counts]
        outs = take(len(groups))
        at = 0
        for index, (left, held) in enumerate(zip((0, 0, 1), refs)):
            factors, column, found = left_refs[left], 0, 0.0
            for part, right in enumerate(right_refs[index]):
                some = right.shape[0]
                if len(factors) > 1:
                    factor = factors[part][...]
                else:
                    factor = factors[0][:, column : column + some]
                found = found + dot(factor, right[...])
                column += some
            held[...] = found.astype(BF)
            some = some_rows[index]
            for out, group in zip(outs, groups):
                for number, distance in enumerate(group):
                    owner = jnp.bitwise_xor(place_ref[0], distance)
                    first = number * chunk + at
                    out[first : first + some, :] = held[
                        pl.ds(pl.multiple_of(owner * some, 16), some), :
                    ]
            at += some

    tile = lambda i, p: (0, i)
    flat_lefts = [left for parts in lefts for left in parts]
    flat_rights = [right for parts in rights for right in parts]
    return pl.pallas_call(
        kernel,
        grid_spec=pltpu.PrefetchScalarGridSpec(
            num_scalar_prefetch=1,
            grid=(lat // WINDOW,),
            in_specs=[full_block(left.shape) for left in flat_lefts]
            + [pl.BlockSpec((right.shape[0], WINDOW), tile) for right in flat_rights],
            out_specs=[pl.BlockSpec((len(group) * chunk, WINDOW), tile) for group in groups],
            scratch_shapes=[pltpu.VMEM((lefts[i][0].shape[0], WINDOW), BF) for i in (0, 0, 1)],
        ),
        out_shape=[shape((len(group) * chunk, lat)) for group in groups],
        compiler_params=params(1),
        cost_estimate=SMALL,
        name="weight_grads",
    )(place, *flat_lefts, *flat_rights)


def byte_grad_call(place, bytes_flat, grads, held, rows, cuts):
    tokens, width = bytes_flat.shape
    block = tokens // rows
    lat = grads[0][0].shape[1]
    count = len(held.flat)
    shards = place_shards(held)

    def kernel(place_ref, x_ref, *refs):
        grad_refs = refs[: 2 * len(cuts)]
        piece_refs = refs[2 * len(cuts) : 2 * len(cuts) + count]
        out_ref, wk, wv, gains, gain, sems = refs[2 * len(cuts) + count :]
        row = pl.program_id(0)

        def loads():
            return held.copies(
                ("gains", "key", "value"), piece_refs, (gains, wk, wv), place_ref, sems
            )

        @pl.when(row == 0)
        def _():
            run_all(loads(), "start")

        xhat, scale = standardize(x_ref[...].astype(F32))

        @pl.when(row == 0)
        def _():
            run_all(loads(), "wait")
            gain[...] = gain_vector(gains, width, held.lanes["byte"], shards)

        for index, (first, some) in enumerate(cuts):

            @pl.when((row >= first) & (row < first + some))
            def _():
                upstream = dot(grad_refs[2 * index][...], wk[...], ((1,), (1,))) + dot(
                    grad_refs[2 * index + 1][...], wv[...], ((1,), (1,))
                )
                out_ref[...] = norm_pull(upstream, gain[...], xhat, scale)

    row_block = lambda i, p: (i, 0)

    def cut_block(first, some):
        return lambda i, p: (jnp.clip(i - first, 0, some - 1), 0)

    return pl.pallas_call(
        kernel,
        grid_spec=pltpu.PrefetchScalarGridSpec(
            num_scalar_prefetch=1,
            grid=(rows,),
            in_specs=[pl.BlockSpec((block, width), row_block)]
            + [pl.BlockSpec((block, lat), cut_block(*cut)) for cut in cuts for _ in range(2)]
            + [any_spec()] * count,
            out_specs=pl.BlockSpec((block, width), row_block),
            scratch_shapes=[
                pltpu.VMEM((width, lat), BF),
                pltpu.VMEM((width, lat), BF),
                pltpu.VMEM((held.blocks * GAIN_ROWS, LANES), BF),
                pltpu.VMEM((1, width), F32),
                pltpu.SemaphoreType.DMA((6 * count,)),
            ],
        ),
        out_shape=shape((tokens, width), F32),
        compiler_params=params(1),
        cost_estimate=SMALL,
        name="byte_grad",
    )(place, bytes_flat, *[g for some in grads for g in some], *held.flat)


def latent_grad_call(place, latent_message, grad_mixed, ups, held):
    tokens, lat = grad_mixed.shape
    cuts, groups = len(ups), len(ups[0])
    count = len(held.flat)
    shards = place_shards(held)

    def kernel(place_ref, x_ref, mixed_ref, *refs):
        up_refs = [refs[i * groups : (i + 1) * groups] for i in range(cuts)]
        piece_refs = refs[cuts * groups : cuts * groups + count]
        out_ref, gains, sems = refs[cuts * groups + count :]
        loads = held.copies(("gains",), piece_refs, (gains,), place_ref, sems)
        run_all(loads, "start")
        xhat, scale = standardize(x_ref[:, :lat].astype(F32))
        upstream = jnp.concatenate(
            [
                functools.reduce(jnp.add, [ref[...].astype(F32) for ref in some])
                for some in up_refs
            ],
            axis=0,
        )
        run_all(loads, "wait")
        gain = gain_vector(gains, lat, held.lanes["latent"], shards)
        out_ref[...] = mixed_ref[...] + norm_pull(upstream, gain, xhat, scale)

    return pl.pallas_call(
        kernel,
        in_specs=[scalar_spec()]
        + [whole_spec()] * (2 + cuts * groups)
        + [any_spec()] * count,
        out_specs=whole_spec(),
        out_shape=shape((tokens, lat), F32),
        scratch_shapes=[
            pltpu.VMEM((held.blocks * GAIN_ROWS, LANES), BF),
            pltpu.SemaphoreType.DMA((2 * count,)),
        ],
        compiler_params=params(0, 24),
        cost_estimate=SMALL,
        name="latent_grad",
    )(place, latent_message, grad_mixed, *[u for some in ups for u in some], *held.flat)


def swap(value, axis, size, distance):
    return lax.ppermute(value, axis, [(i, i ^ distance) for i in range(size)])


def tie(value, *earlier):
    return lax.optimization_barrier((value, *earlier))[0]


def passed(value, *earlier, cost):
    def kernel(in_ref, out_ref):
        pass

    return pl.pallas_call(
        kernel,
        in_specs=[any_spec()],
        out_specs=any_spec(),
        out_shape=shape(value.shape, value.dtype),
        input_output_aliases={0: 0},
        cost_estimate=pl.CostEstimate(
            flops=int(cost * 1.1e9), bytes_accessed=1, transcendentals=0
        ),
        name="passed",
    )(tie(value, *earlier))


def swap_all(parts, size):
    return [swap(parts[j], "fsdp", size, j) for j in range(1, size)]


def by_index(parts, own, size):
    if len(parts) == 5:
        parts = parts[:3] + [jnp.where((own == 0) | (own == 3), parts[4], parts[3])]
    return [lax.select_n(jnp.bitwise_xor(own, k), *parts) for k in range(size)]


def build_block(place, own, parts, sizes, size):
    segments, first, at = [], 0, 0
    for rows in sizes:
        segments.append((first, rows, at))
        first += rows
        at += rows * size
    total = up_to(at, 16)
    if all(first % 8 == 0 for first, _, _ in segments):
        return assemble_call(place, parts, segments, total, size)
    shards = by_index(parts, own, size)
    found = [s[first : first + rows] for first, rows, _ in segments for s in shards]
    return pad_rows(jnp.concatenate(found, axis=0), total)


def add(*values):
    return functools.reduce(jnp.add, [v.astype(F32) for v in values]).astype(BF)


def meet_call(first, high, second, low, others, half):
    rows, lat = first.shape

    def kernel(a, h, c, l, o, one, two):
        def both(ref, start, stop, offset):
            return ref[start:stop, :].astype(F32) + o[
                offset + start : offset + stop, :
            ].astype(F32)

        one[:half, :] = both(a, 0, half, rows).astype(BF)
        one[half:, :] = (both(a, half, rows, rows) + h[...].astype(F32)).astype(BF)
        two[:half, :] = (both(c, 0, half, 0) + l[...].astype(F32)).astype(BF)
        two[half:, :] = both(c, half, rows, 0).astype(BF)

    return pl.pallas_call(
        kernel,
        in_specs=[whole_spec()] * 5,
        out_specs=[whole_spec()] * 2,
        out_shape=[shape((rows, lat))] * 2,
        compiler_params=params(0, 24),
        cost_estimate=SMALL,
        name="meet",
    )(first, high, second, low, others)


def cut_call(place, terms, sizes, size):
    lat = terms[0].shape[1]
    rows = sum(sizes)

    def kernel(place_ref, *refs):
        term_refs, outs, acc = refs[: len(terms)], refs[len(terms) : -1], refs[-1]
        total_rows = acc.shape[0]
        acc[...] = functools.reduce(
            jnp.add, [ref[ref.shape[0] - total_rows :, :].astype(F32) for ref in term_refs]
        )
        for distance, out in enumerate(outs):
            owner = jnp.bitwise_xor(place_ref[1], distance)
            found, at = [], 0
            for some in sizes:
                found.append(acc[pl.ds(pl.multiple_of(at + owner * some, 8), some), :])
                at += some * size
            out[...] = jnp.concatenate(found, axis=0).astype(out.dtype)

    return pl.pallas_call(
        kernel,
        in_specs=[scalar_spec()] + [whole_spec()] * len(terms),
        out_specs=[whole_spec()] * size,
        out_shape=[shape((rows, lat), F32)] + [shape((rows, lat))] * (size - 1),
        scratch_shapes=[pltpu.VMEM(terms[0].shape, F32)],
        compiler_params=params(0, 24),
        cost_estimate=SMALL,
        name="cut",
    )(place, *terms)


def cut_terms(place, own, terms, sizes, size):
    if all(some % 8 == 0 for some in sizes):
        return cut_call(place, terms, sizes, size)
    block = functools.reduce(jnp.add, [v.astype(F32) for v in terms])
    outs = []
    for distance in range(size):
        index = jnp.bitwise_xor(own, distance)
        found, at = [], 0
        for some in sizes:
            part = block[at : at + some * size].reshape(size, some, block.shape[1])
            found.append(lax.dynamic_index_in_dim(part, index, 0, keepdims=False))
            at += some * size
        value = jnp.concatenate(found, axis=0)
        outs.append(value if distance == 0 else value.astype(BF))
    return outs


def total(own, arrived):
    return functools.reduce(jnp.add, [v.astype(F32) for v in [own, *arrived]])


def split_rows(value, sizes):
    found, at = [], 0
    for some in sizes:
        found.append(value[at : at + some])
        at += some
    return found


def up_to(value, step):
    return -(-value // step) * step


def pad_rows(value, rows):
    return jnp.pad(value, ((0, rows - value.shape[0]), (0, 0)))


class Plan:
    def __init__(self, n_dp, n_f):
        self.n_dp, self.n_f = n_dp, n_f
        self.gate = ()

    def send(self, value, distance):
        return swap(tie(value, *self.gate), "dp", self.n_dp, distance)

    def pass_on(self, value, distance):
        return swap(tie(value, *self.gate), "fsdp", self.n_f, distance)

    def relay(self, own, two):
        middle = lax.ppermute(tie(own, *self.gate), "fsdp", [(1, 2), (2, 1)])
        return middle, lax.ppermute(tie(two, *self.gate), "fsdp", [(2, 3), (1, 0)])

    def spread(self, value):
        value = tie(value, *self.gate)
        middle = lax.ppermute(value, "fsdp", [(1, 2), (2, 1)])
        return middle, lax.ppermute(value, "fsdp", [(3, 2), (0, 1)])

    def tied(self, values):
        return [tie(values[0], *self.gate), *values[1:]]


def square_pieces(block, chips, half):
    rows = block.shape[0]
    full, halves = [(0, rows)], [(0, half), (half, rows)]
    pieces, flat = [], []
    for distance, parts, pairs in (
        (0, full, chips[:1]),
        (2, full, chips[1:2]),
        (4, full, chips[2:3]),
        (6, halves, chips[3:]),
    ):
        for core in range(2):
            pieces.append((distance + core, parts))
            flat.extend(pair[core] for pair in pairs)
    return pieces, flat


def local(n_dp, n_f, bytes_in, latents_in, cotangent, byte_segments, latent_segments,
          w_query, w_key, w_value, w_out, w_mlp_in, w_mlp_out,
          gain_latent, gain_byte, gain_mlp):
    rows, byte_local, width = bytes_in.shape
    _, group, lat = latents_in.shape
    dp, own = lax.axis_index("dp"), lax.axis_index("fsdp")
    place = jnp.stack([dp, own]).astype(jnp.int32)
    bytes_flat = bytes_in.reshape(rows * byte_local, width)
    latents_flat = latents_in.reshape(rows * group, lat)
    cot_flat = cotangent.reshape(rows * group, lat)
    kr, qr = w_key.shape[0], w_query.shape[0]
    key_rows, query_rows = n_f * kr, n_f * qr
    cuts = [(0, 1), (1, rows - 1)]
    cut_rows = [(first * group, some * group) for first, some in cuts]

    gains = jnp.concatenate([gain_latent, gain_byte, gain_mlp])
    gains = jnp.pad(gains, (0, lat - gains.shape[0]))[None, :]
    message_one = jnp.concatenate([w_key, w_value, w_query, gains], axis=0)
    message_one = pad_rows(message_one, up_to(2 * kr + qr + 1, 16))
    message_two = jnp.concatenate([w_out, w_mlp_in, w_mlp_out], axis=0)
    ids = latent_segments.reshape(rows * group, 1).astype(BF)
    ids = jnp.pad(ids, ((0, 0), (0, LANES - 1)))
    latent_message = jnp.concatenate([latents_flat, ids], axis=1)
    byte_ids = lax.dynamic_slice_in_dim(byte_segments, own * byte_local, byte_local, axis=1)
    byte_ids = byte_ids.astype(F32)
    byte_row = byte_ids[:, None, :]
    sizes_one, sizes_two = (kr, kr, qr), (qr, qr, qr)
    half_one, half_two = 2 * key_rows, up_to(3 * query_rows // 2, 16)
    spans_one = {
        "key": (0, key_rows),
        "value": (key_rows, key_rows),
        "query": (2 * key_rows, query_rows),
        "gains": (2 * key_rows + query_rows, GAIN_ROWS),
    }
    spans_two = {name: (i * query_rows, query_rows) for i, name in enumerate(("out", "inner", "outer"))}

    def held_one(pieces, flat):
        held = Held(pieces, flat, spans_one)
        held.blocks, held.size = n_dp, n_f
        held.lanes = {"latent": 0, "byte": qr, "mlp": qr + kr}
        return held

    def key_value(one, bytes_flat):
        return key_value_call(place, bytes_flat, one, rows)

    def attend(index, one, parts, keys, values):
        found = attend_call(
            place, parts, byte_row, keys, values, one, n_f, group, *cuts[index]
        )
        return found[0], found[1], found[2:]

    def feed(one, two, attended):
        return feed_call(place, attended, latent_message, cot_flat, one, two, cut_rows)

    def feed_grads(lefts, rights, groups):
        return feed_grads_call(place, lefts, rights, query_rows, groups)

    def attend_back(index, one, parts, saved):
        return attend_back_call(
            place, parts, *saved, byte_row, one, n_f, group, *cuts[index]
        )

    def weight_grads(lefts, first, last, groups):
        some = (key_rows, key_rows, query_rows)
        return weight_grads_call(place, lefts, list(zip(first, last)), some, groups)

    def byte_grad(one, grads):
        return byte_grad_call(place, bytes_flat, grads, one, rows, cuts)

    run = square if (n_dp, n_f) == (8, 4) else plain
    new, grad_latents, grad_bytes, grad_one, grad_two = run(**locals())

    def gain_grad(pairs, gain):
        found = sum(jnp.sum(w.astype(F32) * g, axis=1) for w, g in pairs)
        return found / gain.astype(F32)

    grad_key, grad_value, grad_query = split_rows(grad_one, sizes_one)
    grad_out, grad_inner, grad_outer = split_rows(grad_two, sizes_two)
    return (
        new.reshape(rows, group, lat),
        grad_latents.reshape(rows, group, lat),
        grad_bytes.reshape(rows, byte_local, width),
        grad_query,
        grad_key,
        grad_value,
        grad_out,
        grad_inner,
        grad_outer,
        gain_grad([(w_query, grad_query)], gain_latent),
        gain_grad([(w_key, grad_key), (w_value, grad_value)], gain_byte),
        gain_grad([(w_mlp_in, grad_inner)], gain_mlp),
    )


def plain(*, n_dp, n_f, place, own, bytes_flat, message_one, message_two, latent_message,
          sizes_one, sizes_two, spans_two, cot_flat, held_one, key_value, attend, feed,
          feed_grads, attend_back, weight_grads, byte_grad, **_):
    def gather(message, sizes):
        parts = [message, *swap_all([message] * n_f, n_f)]
        block = build_block(place, own, parts, sizes, n_f)
        flat = [block] + [swap(block, "dp", n_dp, d) for d in range(1, n_dp)]
        return [(d, [(0, block.shape[0])]) for d in range(n_dp)], flat

    def scatter(parts, sizes):
        terms = [parts[0]] + [swap(parts[d], "dp", n_dp, d) for d in range(1, n_dp)]
        cut = cut_terms(place, own, terms, sizes, n_f)
        return total(cut[0], swap_all(cut, n_f))

    one = held_one(*gather(message_one, (*sizes_one, 1)))
    two = Held(*gather(message_two, sizes_two), spans_two)
    byte_t, keys, values = key_value(one, bytes_flat)
    latent_parts = [latent_message, *swap_all([latent_message] * n_f, n_f)]
    latent_t, queries, found = zip(*[attend(i, one, latent_parts, keys, values) for i in range(2)])
    attended = list(zip(*[[f[0], *swap_all(f, n_f)] for f in found]))
    new, grad_mixed, *messages, attended_t, branch, normed_t, inner, act_t = feed(
        one, two, attended
    )
    each = [(d,) for d in range(n_dp)]
    grads = feed_grads((attended_t, normed_t, act_t), (branch, inner, cot_flat), each)
    grad_two = scatter(grads, sizes_two)
    parts = [[m, *swap_all([m] * n_f, n_f)] for m in messages]
    first, last = [attend_back(i, one, parts[i], (queries[i], keys, values)) for i in range(2)]
    grad_bytes = byte_grad(one, (first[:2], last[:2]))
    grad_one = scatter(
        weight_grads(((byte_t,), latent_t), first[:3], last[:3], each), sizes_one
    )
    ups = [[ups[0], *swap_all(ups, n_f)] for ups in (first[3:], last[3:])]
    grad_latents = latent_grad_call(place, latent_message, grad_mixed, ups, one)
    return new, grad_latents, grad_bytes, grad_one, grad_two


def square(*, n_dp, n_f, place, own, bytes_flat, message_one, message_two, latent_message,
           sizes_one, sizes_two, spans_two, half_one, half_two, cot_flat, held_one, key_value,
           attend, feed, feed_grads, attend_back, weight_grads, byte_grad, **_):
    plan = Plan(n_dp, n_f)
    send, pass_on = plan.send, plan.pass_on

    near = [pass_on(message_one, 2), pass_on(message_one, 1)]
    plan.gate = near
    parts = [message_one, near[1], near[0], *plan.relay(message_one, near[0])]
    block = build_block(place, own, parts, (*sizes_one, 1), n_f)
    plan.gate = [block]
    x, y, other = send(block, 2), send(block, 4), send(block, 1)
    latent_two, latent_one = pass_on(latent_message, 2), pass_on(latent_message, 1)
    plan.gate = [x, y]
    low, high = send(x[:half_one], 4), send(y[half_one:], 2)
    latent_two = passed(latent_two, latent_one, cost=12)
    plan.gate = [x, y, latent_two]
    latent_parts = [
        latent_message, latent_one, latent_two, *plan.relay(latent_message, latent_two)
    ]
    plan.gate = [low, high, other]
    others = [send(v, 1) for v in (x, y, low, high)]
    pairs = list(zip((block, x, y, low, high), (other, *others)))
    one = held_one(*square_pieces(block, pairs, half_one))
    plan.gate = [low, high, latent_two]
    two_two, two_one = pass_on(message_two, 2), pass_on(message_two, 1)
    plan.gate = others
    byte_t, keys, values = key_value(one, tie(bytes_flat, *plan.gate))
    plan.gate = [two_two, two_one, keys]
    parts = [message_two, two_one, two_two, *plan.relay(message_two, two_two)]
    latent_t_first, queries_first, found = attend(0, one, plan.tied(latent_parts), keys, values)
    plan.gate = [queries_first, *parts[3:]]
    block = build_block(place, own, plan.tied(parts), sizes_two, n_f)
    x, y = send(block, 2), send(block, 4)
    attended_first = [found[0], *[pass_on(found[j], j) for j in range(1, n_f)]]
    plan.gate = [block]
    latent_t_last, queries_last, found = attend(1, one, plan.tied(latent_parts), keys, values)
    plan.gate = attended_first[1:]
    attended_last = [found[0], *[pass_on(found[j], j) for j in range(1, n_f)]]
    plan.gate = [x, y, queries_last, *attended_first[1:]]
    low, high = send(x[:half_two], 4), send(y[half_two:], 2)
    attended_last[1] = passed(attended_last[1], *attended_last[2:], cost=4)
    plan.gate = [low, high, *attended_last[1:]]
    pairs = [(v, send(v, 1)) for v in (block, x, y, low, high)]
    two = Held(*square_pieces(block, pairs, half_two), spans_two)
    new, grad_mixed, first, last, attended_t, branch, normed_t, inner, act_t = feed(
        one, two, list(zip(attended_first, attended_last))
    )
    groups = [(0,), (2,), (4,), (6,), (7,), (5, 3, 1)]
    plan.gate = []
    near = [pass_on(first, 2), pass_on(first, 1)]
    grads = feed_grads((attended_t, normed_t, act_t), (branch, inner, cot_flat), groups)
    plan.gate = near
    first_parts = [first, near[1], near[0], *plan.relay(first, near[0])]
    near = [pass_on(last, 2), pass_on(last, 1)]
    crossing = send(grads[4], 1)
    low = add(grads[3][:half_two], crossing[:half_two])
    high = add(grads[3][half_two:], crossing[half_two:])
    plan.gate = [crossing, *first_parts[3:]]
    low, high = send(low, 2), send(high, 4)
    others = send(grads[5], 1)
    back_first = attend_back(0, one, plan.tied(first_parts), (queries_first, keys, values))
    plan.gate = [low, high, others, *near, back_first[0]]
    last_parts = [last, near[1], near[0], *plan.relay(last, near[0])]
    x, y = meet_call(grads[1], tie(high, *plan.gate), grads[2], low, others, half_two)
    plan.gate = [x, y, *last_parts[3:]]
    terms_two = [grads[0], others, send(x, 2), send(y, 4)]
    ups_first = back_first[3:]
    ups_first = [ups_first[0], *[pass_on(ups_first[j], j) for j in range(1, n_f)]]
    back_last = attend_back(1, one, plan.tied(last_parts), (queries_last, keys, values))
    plan.gate = [back_last[0], *ups_first[1:]]
    ups = back_last[3:]
    near = [pass_on(ups[1], 1), *plan.spread(ups[3])]
    grads = weight_grads(
        ((byte_t,), (latent_t_first, latent_t_last)),
        back_first[:3],
        [tie(back_last[0], *plan.gate), *back_last[1:3]],
        groups,
    )
    plan.gate = [*near, grads[0], *terms_two[2:]]
    crossing = send(grads[4], 1)
    others = send(tie(grads[5], crossing), 1)
    low = add(grads[3][:half_one], crossing[:half_one])
    high = add(grads[3][half_one:], crossing[half_one:])
    merged = add(tie(ups[2], *plan.gate), near[2])
    plan.gate = [low, high, merged]
    low, high = send(low, 2), send(high, 4)
    ups_last = [ups[0], *near[:2], pass_on(merged, 2)]
    cut_two = cut_terms(place, own, plan.tied(terms_two), sizes_two, n_f)
    plan.gate = [low, high, cut_two[0], others]
    x, y = meet_call(grads[1], tie(high, *plan.gate), grads[2], low, others, half_one)
    plan.gate = [x, y, ups_last[-1]]
    arrived_two = [pass_on(cut_two[j], j) for j in range(1, n_f)]
    plan.gate = [x, y]
    terms_one = [grads[0], others, send(x, 2), send(y, 4)]
    grad_bytes = byte_grad(one, (plan.tied(back_first[:2]), back_last[:2]))
    plan.gate = [*terms_one[2:], grad_bytes]
    cut_one = cut_terms(place, own, plan.tied(terms_one), sizes_one, n_f)
    plan.gate = [cut_one[0]]
    grad_one = total(cut_one[0], [pass_on(cut_one[j], j) for j in range(1, n_f)])
    grad_two = total(cut_two[0], arrived_two)
    grad_latents = latent_grad_call(
        place, latent_message, tie(grad_mixed, *plan.gate), [ups_first, ups_last], one
    )
    return new, grad_latents, grad_bytes, grad_one, grad_two


def solution(mesh):
    rows3 = P("dp", "fsdp", None)
    split2 = P(("dp", "fsdp"), None)
    split1 = P(("dp", "fsdp"))
    in_specs = (rows3,) * 3 + (P("dp", None), P("dp", "fsdp")) + (split2,) * 6 + (split1,) * 3
    out_specs = (rows3,) * 3 + (split2,) * 6 + (split1,) * 3
    body = functools.partial(local, mesh.shape["dp"], mesh.shape["fsdp"])
    return jax.shard_map(
        body, mesh=mesh, in_specs=in_specs, out_specs=out_specs, check_vma=False
    )
```

```python
import functools
import math

import jax
import jax.numpy as jnp
from jax import lax
from jax.experimental import pallas as pl
from jax.experimental.pallas import tpu as pltpu
from jax.sharding import PartitionSpec as P

HEADS = 8
HEAD_DIM = 160
EPSILON = 1e-05
NEG_FILL = -1e30
LANES = 128
WINDOW = 256
BF = jnp.bfloat16
F32 = jnp.float32
GAIN_ROWS = 16
SMALL = pl.CostEstimate(flops=1, bytes_accessed=1, transcendentals=0)


def head_window(head):
    start = head * HEAD_DIM // LANES * LANES
    return start, head * HEAD_DIM - start


def head_lanes(head):
    _, shift = head_window(head)
    lane = lax.broadcasted_iota(jnp.int32, (1, WINDOW), 1)
    return (lane >= shift) & (lane < shift + HEAD_DIM)


def dot(a, b, dims=((1,), (0,))):
    return lax.dot_general(a, b, (dims, ((), ())), preferred_element_type=F32)


def standardize(values):
    centered = values - jnp.mean(values, axis=-1, keepdims=True)
    scale = lax.rsqrt(jnp.mean(centered * centered, axis=-1, keepdims=True) + EPSILON)
    return centered * scale, scale


def norm_pull(upstream, gain, xhat, scale):
    scaled = upstream * gain
    return scale * (
        scaled
        - jnp.mean(scaled, axis=-1, keepdims=True)
        - xhat * jnp.mean(scaled * xhat, axis=-1, keepdims=True)
    )


def split_three(values):
    first = values.astype(BF).astype(F32)
    rest = values - first
    second = rest.astype(BF).astype(F32)
    return first, second, rest - second


def gelu(values):
    inner = math.sqrt(2 / math.pi) * (values + 0.044715 * values * values * values)
    return 0.5 * values * (1.0 + jnp.tanh(inner))


def gelu_slope(values):
    square = values * values
    tanh = jnp.tanh(math.sqrt(2 / math.pi) * (values + 0.044715 * square * values))
    slope = math.sqrt(2 / math.pi) * (1.0 + 3 * 0.044715 * square)
    return 0.5 * (1.0 + tanh) + 0.5 * values * (1.0 - tanh * tanh) * slope


def piece_copies(pieces, flat_refs, first, rows, target, me, sems, base):
    copies = []
    lanes = target.shape[1]
    at = 0
    for distance, parts in pieces:
        owner = jnp.bitwise_xor(me, distance)
        for low, high in parts:
            ref = flat_refs[at]
            at += 1
            start, stop = max(low, first), min(high, first + rows)
            if start < stop:
                place = pl.multiple_of(owner * rows + (start - first), 16)
                copies.append(
                    pltpu.make_async_copy(
                        ref.at[pl.ds(start - low, stop - start), pl.ds(0, lanes)],
                        target.at[pl.ds(place, stop - start), :],
                        sems.at[base + len(copies)],
                    )
                )
    return copies


def group_values(refs, place):
    if len(refs) != 5:
        return [ref[...] for ref in refs]
    own = place[1]
    at_end = (own == 0) | (own == 3)
    values = [ref[...] for ref in refs[:3]]
    return values + [jnp.where(at_end, refs[4][...], refs[3][...])]


def gain_vector(held, size, lane_at, shards):
    per_shard = size // shards
    blocks = held.shape[0] // GAIN_ROWS
    per_block = shards // blocks
    lane = lax.broadcasted_iota(jnp.int32, (LANES, size), 0)
    column = lax.broadcasted_iota(jnp.int32, (LANES, size), 1)
    pick = (lane == lane_at + column % per_shard).astype(F32).astype(BF)
    spread = dot(held[...], pick)
    row = lax.broadcasted_iota(jnp.int32, spread.shape, 0)
    column = lax.broadcasted_iota(jnp.int32, spread.shape, 1) // per_shard
    owner = (row // GAIN_ROWS) * per_block + row % GAIN_ROWS
    right = (owner == column) & (row % GAIN_ROWS < per_block)
    return jnp.sum(jnp.where(right, spread, 0.0), axis=0, keepdims=True)


def params(grid_rank, mebibytes=60):
    return pltpu.CompilerParams(
        dimension_semantics=("arbitrary",) * grid_rank, vmem_limit_bytes=mebibytes << 20
    )


def whole_spec():
    return pl.BlockSpec(memory_space=pltpu.VMEM)


def any_spec():
    return pl.BlockSpec(memory_space=pltpu.HBM)


class Held:
    def __init__(self, pieces, flat, spans):
        self.pieces, self.flat, self.spans = pieces, flat, spans

    def crossed(self):
        at = 0
        for distance, parts in self.pieces:
            if distance == self.blocks - 2:
                return self.flat[at : at + len(parts)]
            at += len(parts)

    def copies(self, names, refs, targets, place, sems):
        found, base = [], 0
        for name, target in zip(names, targets):
            first, rows = self.spans[name]
            some = piece_copies(self.pieces, refs, first, rows, target, place[0], sems, base)
            base += len(some)
            found.append(some)
        return found


def run_all(groups, action):
    for group in groups:
        for copy in group:
            getattr(copy, action)()


def shape(dims, dtype=BF):
    return jax.ShapeDtypeStruct(dims, dtype)


def full_block(dims):
    return pl.BlockSpec(
        dims, lambda i, p: (0,) * len(dims), pipeline_mode=pl.Buffered(buffer_count=1)
    )


def scalar_spec():
    return pl.BlockSpec(memory_space=pltpu.SMEM)


def assemble_call(place, parts, segments, total, size):
    def kernel(place_ref, *refs):
        part_refs, out_ref, acc = refs[: len(parts)], refs[len(parts)], refs[len(parts) + 1]
        values = [v.astype(F32) for v in group_values(part_refs, place_ref)]
        end = max(at + size * rows for _, rows, at in segments)
        if end < total:
            first = end // 8 * 8
            acc[first:, :] = jnp.zeros((total - first, acc.shape[1]), F32)
        for index in range(size):
            want = jnp.bitwise_xor(place_ref[1], index)
            value = values[size - 1]
            for distance in range(size - 2, -1, -1):
                value = jnp.where(want == distance, values[distance], value)
            for first, rows, at in segments:
                acc[at + index * rows : at + (index + 1) * rows, :] = value[first : first + rows]
        out_ref[...] = acc[...].astype(BF)

    lat = parts[0].shape[1]
    return pl.pallas_call(
        kernel,
        in_specs=[scalar_spec()] + [whole_spec()] * len(parts),
        out_specs=whole_spec(),
        out_shape=shape((total, lat)),
        scratch_shapes=[pltpu.VMEM((total, lat), F32)],
        compiler_params=params(0, 24),
        cost_estimate=SMALL,
        name="assemble",
    )(place, *parts)


def key_value_call(place, bytes_flat, held, rows):
    tokens, width = bytes_flat.shape
    block = tokens // rows
    lat = held.flat[0].shape[1]
    count = len(held.flat)
    shards = place_shards(held)

    def kernel(place_ref, x_ref, *refs):
        piece_refs = refs[:count]
        normed_t_ref, key_ref, value_ref, wk, wv, gains, gain, sems = refs[count:]
        first = pl.program_id(0) == 0

        def loads():
            return held.copies(
                ("gains", "key", "value"), piece_refs, (gains, wk, wv), place_ref, sems
            )

        @pl.when(first)
        def _():
            run_all(loads(), "start")

        xhat, _ = standardize(x_ref[...].astype(F32))

        @pl.when(first)
        def _():
            run_all(loads(), "wait")
            gain[...] = gain_vector(gains, width, held.lanes["byte"], shards)

        normed = (xhat * gain[...]).astype(BF)
        key_ref[...] = dot(normed, wk[...]).astype(BF)
        value_ref[...] = dot(normed, wv[...]).astype(BF)
        normed_t_ref[...] = jnp.transpose(normed, (1, 0))

    row_block = lambda i, p: (i, 0)
    return pl.pallas_call(
        kernel,
        grid_spec=pltpu.PrefetchScalarGridSpec(
            num_scalar_prefetch=1,
            grid=(rows,),
            in_specs=[pl.BlockSpec((block, width), row_block)] + [any_spec()] * count,
            out_specs=[
                pl.BlockSpec((width, block), lambda i, p: (0, i)),
                pl.BlockSpec((block, lat), row_block),
                pl.BlockSpec((block, lat), row_block),
            ],
            scratch_shapes=[
                pltpu.VMEM((width, lat), BF),
                pltpu.VMEM((width, lat), BF),
                pltpu.VMEM((held.blocks * GAIN_ROWS, LANES), BF),
                pltpu.VMEM((1, width), F32),
                pltpu.SemaphoreType.DMA((6 * count,)),
            ],
        ),
        out_shape=[shape((width, tokens)), shape((tokens, lat)), shape((tokens, lat))],
        compiler_params=params(1),
        cost_estimate=SMALL,
        name="keys_values",
    )(place, bytes_flat, *held.flat)


def place_shards(held):
    return held.blocks * held.size


def attend_call(place, latent_parts, byte_ids, keys, values, held, groups, group, first, rows):
    parts = len(latent_parts)
    lat = keys.shape[1]
    block = byte_ids.shape[2]
    latents = groups * group
    count = len(held.flat)
    shards = place_shards(held)
    score_scale = 1.0 / math.sqrt(HEAD_DIM)

    def kernel(place_ref, *refs):
        part_refs = refs[:parts]
        bid_ref, key_ref, value_ref = refs[parts : parts + 3]
        piece_refs = refs[parts + 3 : parts + 3 + count]
        rest = refs[parts + 3 + count :]
        normed_t_ref, query_ref = rest[:2]
        out_refs = rest[2 : 2 + groups]
        wq, gains, gain, acc, sems = rest[2 + groups :]
        start = pl.program_id(0) == 0

        def loads():
            return held.copies(("gains", "query"), piece_refs, (gains, wq), place_ref, sems)

        @pl.when(start)
        def _():
            run_all(loads(), "start")

        message = jnp.concatenate(group_values(part_refs, place_ref), axis=0)
        ids = message[:, lat : lat + 1].astype(F32)
        xhat, _ = standardize(message[:, :lat].astype(F32))

        @pl.when(start)
        def _():
            run_all(loads(), "wait")
            gain[...] = gain_vector(gains, lat, held.lanes["latent"], shards)

        normed = (xhat * gain[...]).astype(BF)
        query_ref[...] = dot(normed, wq[...]).astype(BF)
        normed_t_ref[...] = jnp.transpose(normed, (1, 0))
        allowed = ids == bid_ref[0]
        lane = lax.broadcasted_iota(jnp.int32, (latents, LANES), 1)
        stats = jnp.zeros((latents, LANES), F32)
        for head in range(HEADS):
            at, _ = head_window(head)
            mask = head_lanes(head)
            window = slice(at, at + WINDOW)
            query = jnp.where(mask, query_ref[:, window], jnp.zeros((), BF))
            scores = dot(query, key_ref[:, window], ((1,), (1,))) * score_scale
            scores = jnp.where(allowed, scores, NEG_FILL)
            top = jnp.max(scores, axis=-1, keepdims=True)
            exponent = jnp.exp(scores - top)
            total = jnp.sum(exponent, axis=-1, keepdims=True)
            found = dot(exponent.astype(BF), value_ref[:, window]) / total
            if head == 0:
                acc[:, window] = found
            else:
                acc[:, window] = jnp.where(mask, found, acc[:, window])
            log_total = jnp.where(top > -1e29, top + jnp.log(total), NEG_FILL)
            for index, term in enumerate(split_three(log_total)):
                stats = jnp.where(lane == index * HEADS + head, term, stats)
        for index, ref in enumerate(out_refs):
            chunk = slice(index * group, (index + 1) * group)
            ref[:, :lat] = acc[chunk, :].astype(BF)
            ref[:, lat:] = stats[chunk, :].astype(BF)

    row_block = lambda i, p: (first + i, 0)
    own_block = lambda i, p: (i, 0)
    return pl.pallas_call(
        kernel,
        grid_spec=pltpu.PrefetchScalarGridSpec(
            num_scalar_prefetch=1,
            grid=(rows,),
            in_specs=[pl.BlockSpec((group, lat + LANES), row_block)] * parts
            + [
                pl.BlockSpec((1, 1, block), lambda i, p: (first + i, 0, 0)),
                pl.BlockSpec((block, lat), row_block),
                pl.BlockSpec((block, lat), row_block),
            ]
            + [any_spec()] * count,
            out_specs=[
                pl.BlockSpec((lat, latents), lambda i, p: (0, i)),
                pl.BlockSpec((latents, lat), own_block),
            ]
            + [pl.BlockSpec((group, lat + LANES), own_block)] * groups,
            scratch_shapes=[
                pltpu.VMEM((lat, lat), BF),
                pltpu.VMEM((held.blocks * GAIN_ROWS, LANES), BF),
                pltpu.VMEM((1, lat), F32),
                pltpu.VMEM((latents, lat), F32),
                pltpu.SemaphoreType.DMA((4 * count,)),
            ],
        ),
        out_shape=[shape((lat, rows * latents)), shape((rows * latents, lat))]
        + [shape((rows * group, lat + LANES))] * groups,
        compiler_params=params(1),
        cost_estimate=SMALL,
        name="attend",
    )(place, *latent_parts, byte_ids, keys, values, *held.flat)


def feed_call(place, parts, latent_message, cot_flat, held_gain, held, cuts):
    groups, pieces_of = len(parts), len(parts[0])
    tokens, lat = cot_flat.shape
    count, gain_count = len(held.flat), len(held_gain.flat)
    shards = place_shards(held_gain)

    def kernel(place_ref, *refs):
        refs = list(refs)
        take = lambda n: [refs.pop(0) for _ in range(n)]
        part_refs = [take(pieces_of) for _ in range(groups)]
        x_ref, cot_ref = take(2)
        gain_refs, piece_refs = take(gain_count), take(count)
        new_ref, mixed_grad_ref = take(2)
        message_refs = take(len(cuts))
        attended_t, branch, normed_t, inner, act_t = take(5)
        wo, w1, w2, gains, sems, gain_sems = refs
        gain_loads = held_gain.copies(("gains",), gain_refs, (gains,), place_ref, gain_sems)
        loads = held.copies(("out", "inner", "outer"), piece_refs, (wo, w1, w2), place_ref, sems)
        run_all(gain_loads, "start")
        run_all(loads, "start")

        lane = lax.broadcasted_iota(jnp.int32, (LANES, lat), 0)
        column = lax.broadcasted_iota(jnp.int32, (LANES, lat), 1)
        spread = jnp.zeros((LANES, lat), jnp.bool_)
        for head in range(HEADS):
            inside = (column >= head * HEAD_DIM) & (column < (head + 1) * HEAD_DIM)
            own = (lane == head) | (lane == HEADS + head) | (lane == 2 * HEADS + head)
            spread = spread | (inside & own)
        spread = spread.astype(F32).astype(BF)
        found = [jnp.concatenate([ref[...] for ref in some], axis=0) for some in part_refs]
        logs = [dot(value[:, lat:], spread) for value in found]
        top = functools.reduce(jnp.maximum, logs)
        shares = [jnp.exp(log - top) for log in logs]
        total = functools.reduce(jnp.add, shares)
        summed = functools.reduce(
            jnp.add, [s * value[:, :lat].astype(F32) for s, value in zip(shares, found)]
        )
        attended = (summed / total).astype(BF)
        log_total = top + jnp.log(total)
        attended_t[...] = jnp.transpose(attended, (1, 0))

        run_all(gain_loads, "wait")
        gain = gain_vector(gains, lat, held_gain.lanes["mlp"], shards)
        run_all(loads[:1], "wait")
        mixed = x_ref[:, :lat].astype(F32) + dot(attended, wo[...])
        xhat, scale = standardize(mixed)
        normed = (xhat * gain).astype(BF)
        normed_t[...] = jnp.transpose(normed, (1, 0))
        run_all(loads[1:2], "wait")
        hidden = dot(normed, w1[...])
        activated = gelu(hidden).astype(BF)
        act_t[...] = jnp.transpose(activated, (1, 0))
        run_all(loads[2:], "wait")
        new_ref[...] = (mixed + dot(activated, w2[...])).astype(BF)
        cot = cot_ref[...]
        grad_hidden = (dot(cot, w2[...], ((1,), (1,))) * gelu_slope(hidden)).astype(BF)
        inner[...] = grad_hidden
        upstream = dot(grad_hidden, w1[...], ((1,), (1,)))
        grad_mixed = cot.astype(F32) + norm_pull(upstream, gain, xhat, scale)
        mixed_grad_ref[...] = grad_mixed
        grad_branch = grad_mixed.astype(BF)
        branch[...] = grad_branch
        grad_attended = dot(grad_branch, wo[...], ((1,), (1,))).astype(BF)
        product = grad_attended.astype(F32) * attended.astype(F32)
        out_lane = lax.broadcasted_iota(jnp.int32, (tokens, LANES), 1)
        ids = x_ref[:, lat : lat + 1].astype(F32)
        stats = jnp.where(out_lane == 6 * HEADS, ids, 0.0)
        for head in range(HEADS):
            at, shift = head_window(head)
            mask = head_lanes(head)
            inner_sum = jnp.sum(
                jnp.where(mask, product[:, at : at + WINDOW], 0.0), axis=-1, keepdims=True
            )
            first_lane = at + shift
            log_column = log_total[:, first_lane : first_lane + 1]
            terms = split_three(log_column) + split_three(inner_sum)
            for index, term in enumerate(terms):
                stats = jnp.where(out_lane == index * HEADS + head, term, stats)
        stats = stats.astype(BF)
        for (first, some), ref in zip(cuts, message_refs):
            ref[:, :lat] = grad_attended[first : first + some]
            ref[:, lat:] = stats[first : first + some]

    flat_parts = [array for some in parts for array in some]
    return pl.pallas_call(
        kernel,
        in_specs=[scalar_spec()]
        + [whole_spec()] * (len(flat_parts) + 2)
        + [any_spec()] * (gain_count + count),
        out_specs=[whole_spec()] * (7 + len(cuts)),
        out_shape=[shape((tokens, lat)), shape((tokens, lat), F32)]
        + [shape((some, lat + LANES)) for _, some in cuts]
        + [
            shape((lat, tokens)),
            shape((tokens, lat)),
            shape((lat, tokens)),
            shape((tokens, lat)),
            shape((lat, tokens)),
        ],
        scratch_shapes=[pltpu.VMEM((lat, lat), BF)] * 3
        + [
            pltpu.VMEM((held_gain.blocks * GAIN_ROWS, LANES), BF),
            pltpu.SemaphoreType.DMA((6 * count,)),
            pltpu.SemaphoreType.DMA((2 * gain_count,)),
        ],
        compiler_params=params(0),
        cost_estimate=SMALL,
        name="feed",
    )(place, *flat_parts, latent_message, cot_flat, *held_gain.flat, *held.flat)


def feed_grads_call(place, lefts, rights, n, groups):
    lat, tokens = lefts[0].shape
    width = rights[0].shape[1]
    terms = len(lefts)

    def kernel(place_ref, *refs):
        left_refs, right_refs = refs[:terms], refs[terms : 2 * terms]
        for out, group in zip(refs[2 * terms :], groups):
            for number, distance in enumerate(group):
                at = pl.multiple_of(jnp.bitwise_xor(place_ref[0], distance) * n, 16)
                for index in range(terms):
                    chunk = left_refs[index][pl.ds(at, n), :]
                    first = (number * terms + index) * n
                    out[first : first + n, :] = dot(chunk, right_refs[index][...]).astype(BF)

    return pl.pallas_call(
        kernel,
        in_specs=[scalar_spec()] + [whole_spec()] * (2 * terms),
        out_specs=[whole_spec()] * len(groups),
        out_shape=[shape((len(group) * terms * n, width)) for group in groups],
        compiler_params=params(0),
        cost_estimate=SMALL,
        name="feed_grads",
    )(place, *lefts, *rights)


def attend_back_call(
    place, parts, queries, keys, values, byte_ids, held, groups, group, first, rows
):
    count_parts = len(parts)
    lat = keys.shape[1]
    block = byte_ids.shape[2]
    latents = groups * group
    count = len(held.flat)
    score_scale = 1.0 / math.sqrt(HEAD_DIM)

    def kernel(place_ref, *refs):
        refs = list(refs)
        take = lambda n: [refs.pop(0) for _ in range(n)]
        part_refs = take(count_parts)
        query_ref, key_ref, value_ref, bid_ref = take(4)
        piece_refs = take(count)
        grad_key_ref, grad_value_ref, grad_query_ref = take(3)
        up_refs = take(groups)
        wq, acc_q, acc_k, acc_v, sems = refs
        row = pl.program_id(0)

        def loads():
            return held.copies(("query",), piece_refs, (wq,), place_ref, sems)

        @pl.when(row == 0)
        def _():
            run_all(loads(), "start")

        message = jnp.concatenate(group_values(part_refs, place_ref), axis=0)
        stats = jnp.transpose(message[:, lat:].astype(F32), (1, 0))
        byte_ids = jnp.transpose(jnp.broadcast_to(bid_ref[0], (LANES, block)), (1, 0))[:, :1]
        allowed = byte_ids == stats[6 * HEADS : 6 * HEADS + 1, :]
        for head in range(HEADS):
            at, _ = head_window(head)
            mask = head_lanes(head)
            window = slice(at, at + WINDOW)
            stat = lambda k: stats[k * HEADS + head : k * HEADS + head + 1, :]
            log_total = stat(0) + stat(1) + stat(2)
            inner_sum = stat(3) + stat(4) + stat(5)
            query = jnp.where(mask, query_ref[:, window], jnp.zeros((), BF))
            grad = jnp.where(mask, message[:, window], jnp.zeros((), BF))
            key = key_ref[:, window]
            scores = dot(key, query, ((1,), (1,))) * score_scale
            probs = jnp.exp(jnp.where(allowed, scores - log_total, NEG_FILL))
            grad_probs = dot(value_ref[:, window], grad, ((1,), (1,)))
            grad_scores = (probs * (grad_probs - inner_sum)).astype(BF)
            found_k = dot(grad_scores, query)
            found_v = dot(probs.astype(BF), grad)
            found_q = dot(grad_scores, key, ((0,), (0,)))
            if head == 0:
                acc_k[:, window] = found_k
                acc_v[:, window] = found_v
                acc_q[:, window] = found_q
            else:
                acc_k[:, window] = jnp.where(mask, found_k, acc_k[:, window])
                acc_v[:, window] = jnp.where(mask, found_v, acc_v[:, window])
                acc_q[:, window] = jnp.where(mask, found_q, acc_q[:, window])

        grad_query = (acc_q[...] * score_scale).astype(BF)
        grad_key_ref[...] = (acc_k[...] * score_scale).astype(BF)
        grad_value_ref[...] = acc_v[...].astype(BF)
        grad_query_ref[...] = grad_query

        @pl.when(row == 0)
        def _():
            run_all(loads(), "wait")

        upstream = dot(grad_query, wq[...], ((1,), (1,))).astype(BF)
        for index, ref in enumerate(up_refs):
            ref[...] = upstream[index * group : (index + 1) * group, :]

    row_block = lambda i, p: (first + i, 0)
    own_block = lambda i, p: (i, 0)
    return pl.pallas_call(
        kernel,
        grid_spec=pltpu.PrefetchScalarGridSpec(
            num_scalar_prefetch=1,
            grid=(rows,),
            in_specs=[pl.BlockSpec((group, lat + LANES), own_block)] * count_parts
            + [
                pl.BlockSpec((latents, lat), own_block),
                pl.BlockSpec((block, lat), row_block),
                pl.BlockSpec((block, lat), row_block),
                pl.BlockSpec((1, 1, block), lambda i, p: (first + i, 0, 0)),
            ]
            + [any_spec()] * count,
            out_specs=[
                pl.BlockSpec((block, lat), own_block),
                pl.BlockSpec((block, lat), own_block),
                pl.BlockSpec((latents, lat), own_block),
            ]
            + [pl.BlockSpec((group, lat), own_block)] * groups,
            scratch_shapes=[
                pltpu.VMEM((lat, lat), BF),
                pltpu.VMEM((latents, lat), F32),
                pltpu.VMEM((block, lat), F32),
                pltpu.VMEM((block, lat), F32),
                pltpu.SemaphoreType.DMA((2 * count,)),
            ],
        ),
        out_shape=[shape((rows * block, lat))] * 2
        + [shape((rows * latents, lat))]
        + [shape((rows * group, lat))] * groups,
        compiler_params=params(1),
        cost_estimate=SMALL,
        name="attend_back",
    )(place, *parts, queries, keys, values, byte_ids, *held.flat)


def weight_grads_call(place, lefts, rights, some_rows, groups):
    lat = rights[0][0].shape[1]
    chunk = sum(some_rows)
    left_counts, counts = [len(parts) for parts in lefts], [len(parts) for parts in rights]

    def kernel(place_ref, *refs):
        refs = list(refs)
        take = lambda n: [refs.pop(0) for _ in range(n)]
        left_refs = [take(n) for n in left_counts]
        right_refs = [take(n) for n in counts]
        outs = take(len(groups))
        at = 0
        for index, (left, held) in enumerate(zip((0, 0, 1), refs)):
            factors, column, found = left_refs[left], 0, 0.0
            for part, right in enumerate(right_refs[index]):
                some = right.shape[0]
                if len(factors) > 1:
                    factor = factors[part][...]
                else:
                    factor = factors[0][:, column : column + some]
                found = found + dot(factor, right[...])
                column += some
            held[...] = found.astype(BF)
            some = some_rows[index]
            for out, group in zip(outs, groups):
                for number, distance in enumerate(group):
                    owner = jnp.bitwise_xor(place_ref[0], distance)
                    first = number * chunk + at
                    out[first : first + some, :] = held[
                        pl.ds(pl.multiple_of(owner * some, 16), some), :
                    ]
            at += some

    tile = lambda i, p: (0, i)
    flat_lefts = [left for parts in lefts for left in parts]
    flat_rights = [right for parts in rights for right in parts]
    return pl.pallas_call(
        kernel,
        grid_spec=pltpu.PrefetchScalarGridSpec(
            num_scalar_prefetch=1,
            grid=(lat // WINDOW,),
            in_specs=[full_block(left.shape) for left in flat_lefts]
            + [pl.BlockSpec((right.shape[0], WINDOW), tile) for right in flat_rights],
            out_specs=[pl.BlockSpec((len(group) * chunk, WINDOW), tile) for group in groups],
            scratch_shapes=[pltpu.VMEM((lefts[i][0].shape[0], WINDOW), BF) for i in (0, 0, 1)],
        ),
        out_shape=[shape((len(group) * chunk, lat)) for group in groups],
        compiler_params=params(1),
        cost_estimate=SMALL,
        name="weight_grads",
    )(place, *flat_lefts, *flat_rights)


def byte_grad_call(place, bytes_flat, grads, held, rows, cuts):
    tokens, width = bytes_flat.shape
    block = tokens // rows
    lat = grads[0][0].shape[1]
    count = len(held.flat)
    shards = place_shards(held)

    def kernel(place_ref, x_ref, *refs):
        grad_refs = refs[: 2 * len(cuts)]
        piece_refs = refs[2 * len(cuts) : 2 * len(cuts) + count]
        out_ref, wk, wv, gains, gain, sems = refs[2 * len(cuts) + count :]
        row = pl.program_id(0)

        def loads():
            return held.copies(
                ("gains", "key", "value"), piece_refs, (gains, wk, wv), place_ref, sems
            )

        @pl.when(row == 0)
        def _():
            run_all(loads(), "start")

        xhat, scale = standardize(x_ref[...].astype(F32))

        @pl.when(row == 0)
        def _():
            run_all(loads(), "wait")
            gain[...] = gain_vector(gains, width, held.lanes["byte"], shards)

        for index, (first, some) in enumerate(cuts):

            @pl.when((row >= first) & (row < first + some))
            def _():
                upstream = dot(grad_refs[2 * index][...], wk[...], ((1,), (1,))) + dot(
                    grad_refs[2 * index + 1][...], wv[...], ((1,), (1,))
                )
                out_ref[...] = norm_pull(upstream, gain[...], xhat, scale)

    row_block = lambda i, p: (i, 0)

    def cut_block(first, some):
        return lambda i, p: (jnp.clip(i - first, 0, some - 1), 0)

    return pl.pallas_call(
        kernel,
        grid_spec=pltpu.PrefetchScalarGridSpec(
            num_scalar_prefetch=1,
            grid=(rows,),
            in_specs=[pl.BlockSpec((block, width), row_block)]
            + [pl.BlockSpec((block, lat), cut_block(*cut)) for cut in cuts for _ in range(2)]
            + [any_spec()] * count,
            out_specs=pl.BlockSpec((block, width), row_block),
            scratch_shapes=[
                pltpu.VMEM((width, lat), BF),
                pltpu.VMEM((width, lat), BF),
                pltpu.VMEM((held.blocks * GAIN_ROWS, LANES), BF),
                pltpu.VMEM((1, width), F32),
                pltpu.SemaphoreType.DMA((6 * count,)),
            ],
        ),
        out_shape=shape((tokens, width), F32),
        compiler_params=params(1),
        cost_estimate=SMALL,
        name="byte_grad",
    )(place, bytes_flat, *[g for some in grads for g in some], *held.flat)


def latent_grad_call(place, latent_message, grad_mixed, ups, held):
    tokens, lat = grad_mixed.shape
    cuts, groups = len(ups), len(ups[0])
    count = len(held.flat)
    shards = place_shards(held)

    def kernel(place_ref, x_ref, mixed_ref, *refs):
        up_refs = [refs[i * groups : (i + 1) * groups] for i in range(cuts)]
        piece_refs = refs[cuts * groups : cuts * groups + count]
        out_ref, gains, sems = refs[cuts * groups + count :]
        loads = held.copies(("gains",), piece_refs, (gains,), place_ref, sems)
        run_all(loads, "start")
        xhat, scale = standardize(x_ref[:, :lat].astype(F32))
        upstream = jnp.concatenate(
            [
                functools.reduce(jnp.add, [ref[...].astype(F32) for ref in some])
                for some in up_refs
            ],
            axis=0,
        )
        run_all(loads, "wait")
        gain = gain_vector(gains, lat, held.lanes["latent"], shards)
        out_ref[...] = mixed_ref[...] + norm_pull(upstream, gain, xhat, scale)

    return pl.pallas_call(
        kernel,
        in_specs=[scalar_spec()]
        + [whole_spec()] * (2 + cuts * groups)
        + [any_spec()] * count,
        out_specs=whole_spec(),
        out_shape=shape((tokens, lat), F32),
        scratch_shapes=[
            pltpu.VMEM((held.blocks * GAIN_ROWS, LANES), BF),
            pltpu.SemaphoreType.DMA((2 * count,)),
        ],
        compiler_params=params(0, 24),
        cost_estimate=SMALL,
        name="latent_grad",
    )(place, latent_message, grad_mixed, *[u for some in ups for u in some], *held.flat)


def swap(value, axis, size, distance):
    return lax.ppermute(value, axis, [(i, i ^ distance) for i in range(size)])


def tie(value, *earlier):
    return lax.optimization_barrier((value, *earlier))[0]


def passed(value, *earlier, cost):
    def kernel(in_ref, out_ref):
        pass

    return pl.pallas_call(
        kernel,
        in_specs=[any_spec()],
        out_specs=any_spec(),
        out_shape=shape(value.shape, value.dtype),
        input_output_aliases={0: 0},
        cost_estimate=pl.CostEstimate(
            flops=int(cost * 1.1e9), bytes_accessed=1, transcendentals=0
        ),
        name="passed",
    )(tie(value, *earlier))


def swap_all(parts, size):
    return [swap(parts[j], "fsdp", size, j) for j in range(1, size)]


def by_index(parts, own, size):
    if len(parts) == 5:
        parts = parts[:3] + [jnp.where((own == 0) | (own == 3), parts[4], parts[3])]
    return [lax.select_n(jnp.bitwise_xor(own, k), *parts) for k in range(size)]


def build_block(place, own, parts, sizes, size):
    segments, first, at = [], 0, 0
    for rows in sizes:
        segments.append((first, rows, at))
        first += rows
        at += rows * size
    total = up_to(at, 16)
    if all(first % 8 == 0 for first, _, _ in segments):
        return assemble_call(place, parts, segments, total, size)
    shards = by_index(parts, own, size)
    found = [s[first : first + rows] for first, rows, _ in segments for s in shards]
    return pad_rows(jnp.concatenate(found, axis=0), total)


def add(*values):
    return functools.reduce(jnp.add, [v.astype(F32) for v in values]).astype(BF)


def meet_call(first, high, second, low, others, half):
    rows, lat = first.shape

    def kernel(a, h, c, l, o, one, two):
        def both(ref, start, stop, offset):
            return ref[start:stop, :].astype(F32) + o[
                offset + start : offset + stop, :
            ].astype(F32)

        one[:half, :] = both(a, 0, half, rows).astype(BF)
        one[half:, :] = (both(a, half, rows, rows) + h[...].astype(F32)).astype(BF)
        two[:half, :] = (both(c, 0, half, 0) + l[...].astype(F32)).astype(BF)
        two[half:, :] = both(c, half, rows, 0).astype(BF)

    return pl.pallas_call(
        kernel,
        in_specs=[whole_spec()] * 5,
        out_specs=[whole_spec()] * 2,
        out_shape=[shape((rows, lat))] * 2,
        compiler_params=params(0, 24),
        cost_estimate=SMALL,
        name="meet",
    )(first, high, second, low, others)


def cut_call(place, terms, sizes, size):
    lat = terms[0].shape[1]
    rows = sum(sizes)

    def kernel(place_ref, *refs):
        term_refs, outs, acc = refs[: len(terms)], refs[len(terms) : -1], refs[-1]
        total_rows = acc.shape[0]
        acc[...] = functools.reduce(
            jnp.add, [ref[ref.shape[0] - total_rows :, :].astype(F32) for ref in term_refs]
        )
        for distance, out in enumerate(outs):
            owner = jnp.bitwise_xor(place_ref[1], distance)
            found, at = [], 0
            for some in sizes:
                found.append(acc[pl.ds(pl.multiple_of(at + owner * some, 8), some), :])
                at += some * size
            out[...] = jnp.concatenate(found, axis=0).astype(out.dtype)

    return pl.pallas_call(
        kernel,
        in_specs=[scalar_spec()] + [whole_spec()] * len(terms),
        out_specs=[whole_spec()] * size,
        out_shape=[shape((rows, lat), F32)] + [shape((rows, lat))] * (size - 1),
        scratch_shapes=[pltpu.VMEM(terms[0].shape, F32)],
        compiler_params=params(0, 24),
        cost_estimate=SMALL,
        name="cut",
    )(place, *terms)


def cut_terms(place, own, terms, sizes, size):
    if all(some % 8 == 0 for some in sizes):
        return cut_call(place, terms, sizes, size)
    block = functools.reduce(jnp.add, [v.astype(F32) for v in terms])
    outs = []
    for distance in range(size):
        index = jnp.bitwise_xor(own, distance)
        found, at = [], 0
        for some in sizes:
            part = block[at : at + some * size].reshape(size, some, block.shape[1])
            found.append(lax.dynamic_index_in_dim(part, index, 0, keepdims=False))
            at += some * size
        value = jnp.concatenate(found, axis=0)
        outs.append(value if distance == 0 else value.astype(BF))
    return outs


def total(own, arrived):
    return functools.reduce(jnp.add, [v.astype(F32) for v in [own, *arrived]])


def split_rows(value, sizes):
    found, at = [], 0
    for some in sizes:
        found.append(value[at : at + some])
        at += some
    return found


def up_to(value, step):
    return -(-value // step) * step


def pad_rows(value, rows):
    return jnp.pad(value, ((0, rows - value.shape[0]), (0, 0)))


class Plan:
    def __init__(self, n_dp, n_f):
        self.n_dp, self.n_f = n_dp, n_f
        self.gate = ()

    def send(self, value, distance):
        return swap(tie(value, *self.gate), "dp", self.n_dp, distance)

    def pass_on(self, value, distance):
        return swap(tie(value, *self.gate), "fsdp", self.n_f, distance)

    def relay(self, own, two):
        middle = lax.ppermute(tie(own, *self.gate), "fsdp", [(1, 2), (2, 1)])
        return middle, lax.ppermute(tie(two, *self.gate), "fsdp", [(2, 3), (1, 0)])

    def spread(self, value):
        value = tie(value, *self.gate)
        middle = lax.ppermute(value, "fsdp", [(1, 2), (2, 1)])
        return middle, lax.ppermute(value, "fsdp", [(3, 2), (0, 1)])

    def tied(self, values):
        return [tie(values[0], *self.gate), *values[1:]]


def square_pieces(block, chips, half):
    rows = block.shape[0]
    full, halves = [(0, rows)], [(0, half), (half, rows)]
    pieces, flat = [], []
    for distance, parts, pairs in (
        (0, full, chips[:1]),
        (2, full, chips[1:2]),
        (4, full, chips[2:3]),
        (6, halves, chips[3:]),
    ):
        for core in range(2):
            pieces.append((distance + core, parts))
            flat.extend(pair[core] for pair in pairs)
    return pieces, flat


def local(n_dp, n_f, bytes_in, latents_in, cotangent, byte_segments, latent_segments,
          w_query, w_key, w_value, w_out, w_mlp_in, w_mlp_out,
          gain_latent, gain_byte, gain_mlp):
    rows, byte_local, width = bytes_in.shape
    _, group, lat = latents_in.shape
    dp, own = lax.axis_index("dp"), lax.axis_index("fsdp")
    place = jnp.stack([dp, own]).astype(jnp.int32)
    bytes_flat = bytes_in.reshape(rows * byte_local, width)
    latents_flat = latents_in.reshape(rows * group, lat)
    cot_flat = cotangent.reshape(rows * group, lat)
    kr, qr = w_key.shape[0], w_query.shape[0]
    key_rows, query_rows = n_f * kr, n_f * qr
    cuts = [(0, 1), (1, rows - 1)]
    cut_rows = [(first * group, some * group) for first, some in cuts]

    gains = jnp.concatenate([gain_latent, gain_byte, gain_mlp])
    gains = jnp.pad(gains, (0, lat - gains.shape[0]))[None, :]
    message_one = jnp.concatenate([w_key, w_value, w_query, gains], axis=0)
    message_one = pad_rows(message_one, up_to(2 * kr + qr + 1, 16))
    message_two = jnp.concatenate([w_out, w_mlp_in, w_mlp_out], axis=0)
    ids = latent_segments.reshape(rows * group, 1).astype(BF)
    ids = jnp.pad(ids, ((0, 0), (0, LANES - 1)))
    latent_message = jnp.concatenate([latents_flat, ids], axis=1)
    byte_ids = lax.dynamic_slice_in_dim(byte_segments, own * byte_local, byte_local, axis=1)
    byte_ids = byte_ids.astype(F32)
    byte_row = byte_ids[:, None, :]
    sizes_one, sizes_two = (kr, kr, qr), (qr, qr, qr)
    half_one, half_two = 2 * key_rows, up_to(3 * query_rows // 2, 16)
    spans_one = {
        "key": (0, key_rows),
        "value": (key_rows, key_rows),
        "query": (2 * key_rows, query_rows),
        "gains": (2 * key_rows + query_rows, GAIN_ROWS),
    }
    spans_two = {name: (i * query_rows, query_rows) for i, name in enumerate(("out", "inner", "outer"))}

    def held_one(pieces, flat):
        held = Held(pieces, flat, spans_one)
        held.blocks, held.size = n_dp, n_f
        held.lanes = {"latent": 0, "byte": qr, "mlp": qr + kr}
        return held

    def key_value(one, bytes_flat):
        return key_value_call(place, bytes_flat, one, rows)

    def attend(index, one, parts, keys, values):
        found = attend_call(
            place, parts, byte_row, keys, values, one, n_f, group, *cuts[index]
        )
        return found[0], found[1], found[2:]

    def feed(one, two, attended):
        return feed_call(place, attended, latent_message, cot_flat, one, two, cut_rows)

    def feed_grads(lefts, rights, groups):
        return feed_grads_call(place, lefts, rights, query_rows, groups)

    def attend_back(index, one, parts, saved):
        return attend_back_call(
            place, parts, *saved, byte_row, one, n_f, group, *cuts[index]
        )

    def weight_grads(lefts, first, last, groups):
        some = (key_rows, key_rows, query_rows)
        return weight_grads_call(place, lefts, list(zip(first, last)), some, groups)

    def byte_grad(one, grads):
        return byte_grad_call(place, bytes_flat, grads, one, rows, cuts)

    run = square if (n_dp, n_f) == (8, 4) else plain
    new, grad_latents, grad_bytes, grad_one, grad_two = run(**locals())

    def gain_grad(pairs, gain):
        found = sum(jnp.sum(w.astype(F32) * g, axis=1) for w, g in pairs)
        return found / gain.astype(F32)

    grad_key, grad_value, grad_query = split_rows(grad_one, sizes_one)
    grad_out, grad_inner, grad_outer = split_rows(grad_two, sizes_two)
    return (
        new.reshape(rows, group, lat),
        grad_latents.reshape(rows, group, lat),
        grad_bytes.reshape(rows, byte_local, width),
        grad_query,
        grad_key,
        grad_value,
        grad_out,
        grad_inner,
        grad_outer,
        gain_grad([(w_query, grad_query)], gain_latent),
        gain_grad([(w_key, grad_key), (w_value, grad_value)], gain_byte),
        gain_grad([(w_mlp_in, grad_inner)], gain_mlp),
    )


def plain(*, n_dp, n_f, place, own, bytes_flat, message_one, message_two, latent_message,
          sizes_one, sizes_two, spans_two, cot_flat, held_one, key_value, attend, feed,
          feed_grads, attend_back, weight_grads, byte_grad, **_):
    def gather(message, sizes):
        parts = [message, *swap_all([message] * n_f, n_f)]
        block = build_block(place, own, parts, sizes, n_f)
        flat = [block] + [swap(block, "dp", n_dp, d) for d in range(1, n_dp)]
        return [(d, [(0, block.shape[0])]) for d in range(n_dp)], flat

    def scatter(parts, sizes):
        terms = [parts[0]] + [swap(parts[d], "dp", n_dp, d) for d in range(1, n_dp)]
        cut = cut_terms(place, own, terms, sizes, n_f)
        return total(cut[0], swap_all(cut, n_f))

    one = held_one(*gather(message_one, (*sizes_one, 1)))
    two = Held(*gather(message_two, sizes_two), spans_two)
    byte_t, keys, values = key_value(one, bytes_flat)
    latent_parts = [latent_message, *swap_all([latent_message] * n_f, n_f)]
    latent_t, queries, found = zip(*[attend(i, one, latent_parts, keys, values) for i in range(2)])
    attended = list(zip(*[[f[0], *swap_all(f, n_f)] for f in found]))
    new, grad_mixed, *messages, attended_t, branch, normed_t, inner, act_t = feed(
        one, two, attended
    )
    each = [(d,) for d in range(n_dp)]
    grads = feed_grads((attended_t, normed_t, act_t), (branch, inner, cot_flat), each)
    grad_two = scatter(grads, sizes_two)
    parts = [[m, *swap_all([m] * n_f, n_f)] for m in messages]
    first, last = [attend_back(i, one, parts[i], (queries[i], keys, values)) for i in range(2)]
    grad_bytes = byte_grad(one, (first[:2], last[:2]))
    grad_one = scatter(
        weight_grads(((byte_t,), latent_t), first[:3], last[:3], each), sizes_one
    )
    ups = [[ups[0], *swap_all(ups, n_f)] for ups in (first[3:], last[3:])]
    grad_latents = latent_grad_call(place, latent_message, grad_mixed, ups, one)
    return new, grad_latents, grad_bytes, grad_one, grad_two


def square(*, n_dp, n_f, place, own, bytes_flat, message_one, message_two, latent_message,
           sizes_one, sizes_two, spans_two, half_one, half_two, cot_flat, held_one, key_value,
           attend, feed, feed_grads, attend_back, weight_grads, byte_grad, **_):
    plan = Plan(n_dp, n_f)
    send, pass_on = plan.send, plan.pass_on

    near = [pass_on(message_one, 2), pass_on(message_one, 1)]
    plan.gate = near
    parts = [message_one, near[1], near[0], *plan.relay(message_one, near[0])]
    block = build_block(place, own, parts, (*sizes_one, 1), n_f)
    plan.gate = [block]
    x, y, other = send(block, 2), send(block, 4), send(block, 1)
    latent_two, latent_one = pass_on(latent_message, 2), pass_on(latent_message, 1)
    plan.gate = [x, y]
    low, high = send(x[:half_one], 4), send(y[half_one:], 2)
    latent_two = passed(latent_two, latent_one, cost=12)
    plan.gate = [x, y, latent_two]
    latent_parts = [
        latent_message, latent_one, latent_two, *plan.relay(latent_message, latent_two)
    ]
    plan.gate = [low, high, other]
    others = [send(v, 1) for v in (x, y, low, high)]
    pairs = list(zip((block, x, y, low, high), (other, *others)))
    one = held_one(*square_pieces(block, pairs, half_one))
    plan.gate = [low, high, latent_two]
    two_two, two_one = pass_on(message_two, 2), pass_on(message_two, 1)
    plan.gate = others
    byte_t, keys, values = key_value(one, tie(bytes_flat, *plan.gate))
    plan.gate = [two_two, two_one, keys]
    parts = [message_two, two_one, two_two, *plan.relay(message_two, two_two)]
    latent_t_first, queries_first, found = attend(0, one, plan.tied(latent_parts), keys, values)
    plan.gate = [queries_first, *parts[3:]]
    block = build_block(place, own, plan.tied(parts), sizes_two, n_f)
    x, y = send(block, 2), send(block, 4)
    attended_first = [found[0], *[pass_on(found[j], j) for j in range(1, n_f)]]
    plan.gate = [block]
    latent_t_last, queries_last, found = attend(1, one, plan.tied(latent_parts), keys, values)
    plan.gate = attended_first[1:]
    attended_last = [found[0], *[pass_on(found[j], j) for j in range(1, n_f)]]
    plan.gate = [x, y, queries_last, *attended_first[1:]]
    low, high = send(x[:half_two], 4), send(y[half_two:], 2)
    attended_last[1] = passed(attended_last[1], *attended_last[2:], cost=4)
    plan.gate = [low, high, *attended_last[1:]]
    pairs = [(v, send(v, 1)) for v in (block, x, y, low, high)]
    two = Held(*square_pieces(block, pairs, half_two), spans_two)
    new, grad_mixed, first, last, attended_t, branch, normed_t, inner, act_t = feed(
        one, two, list(zip(attended_first, attended_last))
    )
    groups = [(0,), (2,), (4,), (6,), (7,), (5, 3, 1)]
    plan.gate = []
    near = [pass_on(first, 2), pass_on(first, 1)]
    grads = feed_grads((attended_t, normed_t, act_t), (branch, inner, cot_flat), groups)
    plan.gate = near
    first_parts = [first, near[1], near[0], *plan.relay(first, near[0])]
    near = [pass_on(last, 2), pass_on(last, 1)]
    crossing = send(grads[4], 1)
    low = add(grads[3][:half_two], crossing[:half_two])
    high = add(grads[3][half_two:], crossing[half_two:])
    plan.gate = [crossing, *first_parts[3:]]
    low, high = send(low, 2), send(high, 4)
    others = send(grads[5], 1)
    back_first = attend_back(0, one, plan.tied(first_parts), (queries_first, keys, values))
    near[0] = passed(near[0], near[1], back_first[0], cost=5)
    plan.gate = [low, high, others, *near, back_first[0]]
    last_parts = [last, near[1], near[0], *plan.relay(last, near[0])]
    x, y = meet_call(grads[1], tie(high, *plan.gate), grads[2], low, others, half_two)
    plan.gate = [x, y, *last_parts[3:]]
    terms_two = [grads[0], others, send(x, 2), send(y, 4)]
    ups_first = back_first[3:]
    ups_first = [ups_first[0], *[pass_on(ups_first[j], j) for j in range(1, n_f)]]
    back_last = attend_back(1, one, plan.tied(last_parts), (queries_last, keys, values))
    plan.gate = [back_last[0], *ups_first[1:]]
    ups = back_last[3:]
    near = [pass_on(ups[1], 1), *plan.spread(ups[3])]
    grads = weight_grads(
        ((byte_t,), (latent_t_first, latent_t_last)),
        back_first[:3],
        [tie(back_last[0], *plan.gate), *back_last[1:3]],
        groups,
    )
    plan.gate = [*near, grads[0], *terms_two[2:]]
    crossing = send(grads[4], 1)
    others = send(tie(grads[5], crossing), 1)
    low = add(grads[3][:half_one], crossing[:half_one])
    high = add(grads[3][half_one:], crossing[half_one:])
    merged = add(tie(ups[2], *plan.gate), near[2])
    plan.gate = [low, high, merged]
    low, high = send(low, 2), send(high, 4)
    ups_last = [ups[0], *near[:2], pass_on(merged, 2)]
    cut_two = cut_terms(place, own, plan.tied(terms_two), sizes_two, n_f)
    plan.gate = [low, high, cut_two[0], others]
    x, y = meet_call(grads[1], tie(high, *plan.gate), grads[2], low, others, half_one)
    plan.gate = [x, y, ups_last[-1]]
    arrived_two = [pass_on(cut_two[j], j) for j in range(1, n_f)]
    plan.gate = [x, y]
    terms_one = [grads[0], others, send(x, 2), send(y, 4)]
    grad_bytes = byte_grad(one, (plan.tied(back_first[:2]), back_last[:2]))
    plan.gate = [*terms_one[2:], grad_bytes]
    cut_one = cut_terms(place, own, plan.tied(terms_one), sizes_one, n_f)
    plan.gate = [cut_one[0]]
    grad_one = total(cut_one[0], [pass_on(cut_one[j], j) for j in range(1, n_f)])
    grad_two = total(cut_two[0], arrived_two)
    grad_latents = latent_grad_call(
        place, latent_message, tie(grad_mixed, *plan.gate), [ups_first, ups_last], one
    )
    return new, grad_latents, grad_bytes, grad_one, grad_two


def solution(mesh):
    rows3 = P("dp", "fsdp", None)
    split2 = P(("dp", "fsdp"), None)
    split1 = P(("dp", "fsdp"))
    in_specs = (rows3,) * 3 + (P("dp", None), P("dp", "fsdp")) + (split2,) * 6 + (split1,) * 3
    out_specs = (rows3,) * 3 + (split2,) * 6 + (split1,) * 3
    body = functools.partial(local, mesh.shape["dp"], mesh.shape["fsdp"])
    return jax.shard_map(
        body, mesh=mesh, in_specs=in_specs, out_specs=out_specs, check_vma=False
    )
```

```python
import functools
import math

import jax
import jax.numpy as jnp
from jax import lax
from jax.experimental import pallas as pl
from jax.experimental.pallas import tpu as pltpu
from jax.sharding import PartitionSpec as P

HEADS = 8
HEAD_DIM = 160
EPSILON = 1e-05
NEG_FILL = -1e30
LANES = 128
WINDOW = 256
BF = jnp.bfloat16
F32 = jnp.float32
GAIN_ROWS = 16
SMALL = pl.CostEstimate(flops=1, bytes_accessed=1, transcendentals=0)


def head_window(head):
    start = head * HEAD_DIM // LANES * LANES
    return start, head * HEAD_DIM - start


def head_lanes(head):
    _, shift = head_window(head)
    lane = lax.broadcasted_iota(jnp.int32, (1, WINDOW), 1)
    return (lane >= shift) & (lane < shift + HEAD_DIM)


def dot(a, b, dims=((1,), (0,))):
    return lax.dot_general(a, b, (dims, ((), ())), preferred_element_type=F32)


def standardize(values):
    centered = values - jnp.mean(values, axis=-1, keepdims=True)
    scale = lax.rsqrt(jnp.mean(centered * centered, axis=-1, keepdims=True) + EPSILON)
    return centered * scale, scale


def norm_pull(upstream, gain, xhat, scale):
    scaled = upstream * gain
    return scale * (
        scaled
        - jnp.mean(scaled, axis=-1, keepdims=True)
        - xhat * jnp.mean(scaled * xhat, axis=-1, keepdims=True)
    )


def split_three(values):
    first = values.astype(BF).astype(F32)
    rest = values - first
    second = rest.astype(BF).astype(F32)
    return first, second, rest - second


def gelu(values):
    inner = math.sqrt(2 / math.pi) * (values + 0.044715 * values * values * values)
    return 0.5 * values * (1.0 + jnp.tanh(inner))


def gelu_slope(values):
    square = values * values
    tanh = jnp.tanh(math.sqrt(2 / math.pi) * (values + 0.044715 * square * values))
    slope = math.sqrt(2 / math.pi) * (1.0 + 3 * 0.044715 * square)
    return 0.5 * (1.0 + tanh) + 0.5 * values * (1.0 - tanh * tanh) * slope


def piece_copies(pieces, flat_refs, first, rows, target, me, sems, base):
    copies = []
    lanes = target.shape[1]
    at = 0
    for distance, parts in pieces:
        owner = jnp.bitwise_xor(me, distance)
        for low, high in parts:
            ref = flat_refs[at]
            at += 1
            start, stop = max(low, first), min(high, first + rows)
            if start < stop:
                place = pl.multiple_of(owner * rows + (start - first), 16)
                copies.append(
                    pltpu.make_async_copy(
                        ref.at[pl.ds(start - low, stop - start), pl.ds(0, lanes)],
                        target.at[pl.ds(place, stop - start), :],
                        sems.at[base + len(copies)],
                    )
                )
    return copies


def group_values(refs, place):
    if len(refs) != 5:
        return [ref[...] for ref in refs]
    own = place[1]
    at_end = (own == 0) | (own == 3)
    values = [ref[...] for ref in refs[:3]]
    return values + [jnp.where(at_end, refs[4][...], refs[3][...])]


def gain_vector(held, size, lane_at, shards):
    per_shard = size // shards
    blocks = held.shape[0] // GAIN_ROWS
    per_block = shards // blocks
    lane = lax.broadcasted_iota(jnp.int32, (LANES, size), 0)
    column = lax.broadcasted_iota(jnp.int32, (LANES, size), 1)
    pick = (lane == lane_at + column % per_shard).astype(F32).astype(BF)
    spread = dot(held[...], pick)
    row = lax.broadcasted_iota(jnp.int32, spread.shape, 0)
    column = lax.broadcasted_iota(jnp.int32, spread.shape, 1) // per_shard
    owner = (row // GAIN_ROWS) * per_block + row % GAIN_ROWS
    right = (owner == column) & (row % GAIN_ROWS < per_block)
    return jnp.sum(jnp.where(right, spread, 0.0), axis=0, keepdims=True)


def params(grid_rank, mebibytes=60):
    return pltpu.CompilerParams(
        dimension_semantics=("arbitrary",) * grid_rank, vmem_limit_bytes=mebibytes << 20
    )


def whole_spec():
    return pl.BlockSpec(memory_space=pltpu.VMEM)


def any_spec():
    return pl.BlockSpec(memory_space=pltpu.HBM)


class Held:
    def __init__(self, pieces, flat, spans):
        self.pieces, self.flat, self.spans = pieces, flat, spans

    def crossed(self):
        at = 0
        for distance, parts in self.pieces:
            if distance == self.blocks - 2:
                return self.flat[at : at + len(parts)]
            at += len(parts)

    def copies(self, names, refs, targets, place, sems):
        found, base = [], 0
        for name, target in zip(names, targets):
            first, rows = self.spans[name]
            some = piece_copies(self.pieces, refs, first, rows, target, place[0], sems, base)
            base += len(some)
            found.append(some)
        return found


def run_all(groups, action):
    for group in groups:
        for copy in group:
            getattr(copy, action)()


def shape(dims, dtype=BF):
    return jax.ShapeDtypeStruct(dims, dtype)


def full_block(dims):
    return pl.BlockSpec(
        dims, lambda i, p: (0,) * len(dims), pipeline_mode=pl.Buffered(buffer_count=1)
    )


def scalar_spec():
    return pl.BlockSpec(memory_space=pltpu.SMEM)


def assemble_call(place, parts, segments, total, size):
    def kernel(place_ref, *refs):
        part_refs, out_ref, acc = refs[: len(parts)], refs[len(parts)], refs[len(parts) + 1]
        values = [v.astype(F32) for v in group_values(part_refs, place_ref)]
        end = max(at + size * rows for _, rows, at in segments)
        if end < total:
            first = end // 8 * 8
            acc[first:, :] = jnp.zeros((total - first, acc.shape[1]), F32)
        for index in range(size):
            want = jnp.bitwise_xor(place_ref[1], index)
            value = values[size - 1]
            for distance in range(size - 2, -1, -1):
                value = jnp.where(want == distance, values[distance], value)
            for first, rows, at in segments:
                acc[at + index * rows : at + (index + 1) * rows, :] = value[first : first + rows]
        out_ref[...] = acc[...].astype(BF)

    lat = parts[0].shape[1]
    return pl.pallas_call(
        kernel,
        in_specs=[scalar_spec()] + [whole_spec()] * len(parts),
        out_specs=whole_spec(),
        out_shape=shape((total, lat)),
        scratch_shapes=[pltpu.VMEM((total, lat), F32)],
        compiler_params=params(0, 24),
        cost_estimate=SMALL,
        name="assemble",
    )(place, *parts)


def key_value_call(place, bytes_flat, held, rows):
    tokens, width = bytes_flat.shape
    block = tokens // rows
    lat = held.flat[0].shape[1]
    count = len(held.flat)
    shards = place_shards(held)

    def kernel(place_ref, x_ref, *refs):
        piece_refs = refs[:count]
        normed_t_ref, key_ref, value_ref, wk, wv, gains, gain, sems = refs[count:]
        first = pl.program_id(0) == 0

        def loads():
            return held.copies(
                ("gains", "key", "value"), piece_refs, (gains, wk, wv), place_ref, sems
            )

        @pl.when(first)
        def _():
            run_all(loads(), "start")

        xhat, _ = standardize(x_ref[...].astype(F32))

        @pl.when(first)
        def _():
            run_all(loads(), "wait")
            gain[...] = gain_vector(gains, width, held.lanes["byte"], shards)

        normed = (xhat * gain[...]).astype(BF)
        key_ref[...] = dot(normed, wk[...]).astype(BF)
        value_ref[...] = dot(normed, wv[...]).astype(BF)
        normed_t_ref[...] = jnp.transpose(normed, (1, 0))

    row_block = lambda i, p: (i, 0)
    return pl.pallas_call(
        kernel,
        grid_spec=pltpu.PrefetchScalarGridSpec(
            num_scalar_prefetch=1,
            grid=(rows,),
            in_specs=[pl.BlockSpec((block, width), row_block)] + [any_spec()] * count,
            out_specs=[
                pl.BlockSpec((width, block), lambda i, p: (0, i)),
                pl.BlockSpec((block, lat), row_block),
                pl.BlockSpec((block, lat), row_block),
            ],
            scratch_shapes=[
                pltpu.VMEM((width, lat), BF),
                pltpu.VMEM((width, lat), BF),
                pltpu.VMEM((held.blocks * GAIN_ROWS, LANES), BF),
                pltpu.VMEM((1, width), F32),
                pltpu.SemaphoreType.DMA((6 * count,)),
            ],
        ),
        out_shape=[shape((width, tokens)), shape((tokens, lat)), shape((tokens, lat))],
        compiler_params=params(1),
        cost_estimate=SMALL,
        name="keys_values",
    )(place, bytes_flat, *held.flat)


def place_shards(held):
    return held.blocks * held.size


def attend_call(place, latent_parts, byte_ids, keys, values, held, groups, group, first, rows):
    parts = len(latent_parts)
    lat = keys.shape[1]
    block = byte_ids.shape[2]
    latents = groups * group
    count = len(held.flat)
    shards = place_shards(held)
    score_scale = 1.0 / math.sqrt(HEAD_DIM)

    def kernel(place_ref, *refs):
        part_refs = refs[:parts]
        bid_ref, key_ref, value_ref = refs[parts : parts + 3]
        piece_refs = refs[parts + 3 : parts + 3 + count]
        rest = refs[parts + 3 + count :]
        normed_t_ref, query_ref = rest[:2]
        out_refs = rest[2 : 2 + groups]
        wq, gains, gain, acc, sems = rest[2 + groups :]
        start = pl.program_id(0) == 0

        def loads():
            return held.copies(("gains", "query"), piece_refs, (gains, wq), place_ref, sems)

        @pl.when(start)
        def _():
            run_all(loads(), "start")

        message = jnp.concatenate(group_values(part_refs, place_ref), axis=0)
        ids = message[:, lat : lat + 1].astype(F32)
        xhat, _ = standardize(message[:, :lat].astype(F32))

        @pl.when(start)
        def _():
            run_all(loads(), "wait")
            gain[...] = gain_vector(gains, lat, held.lanes["latent"], shards)

        normed = (xhat * gain[...]).astype(BF)
        query_ref[...] = dot(normed, wq[...]).astype(BF)
        normed_t_ref[...] = jnp.transpose(normed, (1, 0))
        allowed = ids == bid_ref[0]
        lane = lax.broadcasted_iota(jnp.int32, (latents, LANES), 1)
        stats = jnp.zeros((latents, LANES), F32)
        for head in range(HEADS):
            at, _ = head_window(head)
            mask = head_lanes(head)
            window = slice(at, at + WINDOW)
            query = jnp.where(mask, query_ref[:, window], jnp.zeros((), BF))
            scores = dot(query, key_ref[:, window], ((1,), (1,))) * score_scale
            scores = jnp.where(allowed, scores, NEG_FILL)
            top = jnp.max(scores, axis=-1, keepdims=True)
            exponent = jnp.exp(scores - top)
            total = jnp.sum(exponent, axis=-1, keepdims=True)
            found = dot(exponent.astype(BF), value_ref[:, window]) * (1.0 / total)
            if head == 0:
                acc[:, window] = found
            else:
                acc[:, window] = jnp.where(mask, found, acc[:, window])
            log_total = jnp.where(top > -1e29, top + jnp.log(total), NEG_FILL)
            for index, term in enumerate(split_three(log_total)):
                stats = jnp.where(lane == index * HEADS + head, term, stats)
        for index, ref in enumerate(out_refs):
            chunk = slice(index * group, (index + 1) * group)
            ref[:, :lat] = acc[chunk, :].astype(BF)
            ref[:, lat:] = stats[chunk, :].astype(BF)

    row_block = lambda i, p: (first + i, 0)
    own_block = lambda i, p: (i, 0)
    return pl.pallas_call(
        kernel,
        grid_spec=pltpu.PrefetchScalarGridSpec(
            num_scalar_prefetch=1,
            grid=(rows,),
            in_specs=[pl.BlockSpec((group, lat + LANES), row_block)] * parts
            + [
                pl.BlockSpec((1, 1, block), lambda i, p: (first + i, 0, 0)),
                pl.BlockSpec((block, lat), row_block),
                pl.BlockSpec((block, lat), row_block),
            ]
            + [any_spec()] * count,
            out_specs=[
                pl.BlockSpec((lat, latents), lambda i, p: (0, i)),
                pl.BlockSpec((latents, lat), own_block),
            ]
            + [pl.BlockSpec((group, lat + LANES), own_block)] * groups,
            scratch_shapes=[
                pltpu.VMEM((lat, lat), BF),
                pltpu.VMEM((held.blocks * GAIN_ROWS, LANES), BF),
                pltpu.VMEM((1, lat), F32),
                pltpu.VMEM((latents, lat), F32),
                pltpu.SemaphoreType.DMA((4 * count,)),
            ],
        ),
        out_shape=[shape((lat, rows * latents)), shape((rows * latents, lat))]
        + [shape((rows * group, lat + LANES))] * groups,
        compiler_params=params(1),
        cost_estimate=SMALL,
        name="attend",
    )(place, *latent_parts, byte_ids, keys, values, *held.flat)


def feed_call(place, parts, latent_message, cot_flat, held_gain, held, cuts):
    groups, pieces_of = len(parts), len(parts[0])
    tokens, lat = cot_flat.shape
    count, gain_count = len(held.flat), len(held_gain.flat)
    shards = place_shards(held_gain)

    def kernel(place_ref, *refs):
        refs = list(refs)
        take = lambda n: [refs.pop(0) for _ in range(n)]
        part_refs = [take(pieces_of) for _ in range(groups)]
        x_ref, cot_ref = take(2)
        gain_refs, piece_refs = take(gain_count), take(count)
        new_ref, mixed_grad_ref = take(2)
        message_refs = take(len(cuts))
        attended_t, branch, normed_t, inner, act_t = take(5)
        wo, w1, w2, gains, sems, gain_sems = refs
        gain_loads = held_gain.copies(("gains",), gain_refs, (gains,), place_ref, gain_sems)
        loads = held.copies(("out", "inner", "outer"), piece_refs, (wo, w1, w2), place_ref, sems)
        run_all(gain_loads, "start")
        run_all(loads, "start")

        lane = lax.broadcasted_iota(jnp.int32, (LANES, lat), 0)
        column = lax.broadcasted_iota(jnp.int32, (LANES, lat), 1)
        spread = jnp.zeros((LANES, lat), jnp.bool_)
        for head in range(HEADS):
            inside = (column >= head * HEAD_DIM) & (column < (head + 1) * HEAD_DIM)
            own = (lane == head) | (lane == HEADS + head) | (lane == 2 * HEADS + head)
            spread = spread | (inside & own)
        spread = spread.astype(F32).astype(BF)
        found = [jnp.concatenate([ref[...] for ref in some], axis=0) for some in part_refs]
        logs = [dot(value[:, lat:], spread) for value in found]
        top = functools.reduce(jnp.maximum, logs)
        shares = [jnp.exp(log - top) for log in logs]
        total = functools.reduce(jnp.add, shares)
        summed = functools.reduce(
            jnp.add, [s * value[:, :lat].astype(F32) for s, value in zip(shares, found)]
        )
        attended = (summed * (1.0 / total)).astype(BF)
        log_total = top + jnp.log(total)
        attended_t[...] = jnp.transpose(attended, (1, 0))

        run_all(gain_loads, "wait")
        gain = gain_vector(gains, lat, held_gain.lanes["mlp"], shards)
        run_all(loads[:1], "wait")
        mixed = x_ref[:, :lat].astype(F32) + dot(attended, wo[...])
        xhat, scale = standardize(mixed)
        normed = (xhat * gain).astype(BF)
        normed_t[...] = jnp.transpose(normed, (1, 0))
        run_all(loads[1:2], "wait")
        hidden = dot(normed, w1[...])
        activated = gelu(hidden).astype(BF)
        act_t[...] = jnp.transpose(activated, (1, 0))
        run_all(loads[2:], "wait")
        new_ref[...] = (mixed + dot(activated, w2[...])).astype(BF)
        cot = cot_ref[...]
        grad_hidden = (dot(cot, w2[...], ((1,), (1,))) * gelu_slope(hidden)).astype(BF)
        inner[...] = grad_hidden
        upstream = dot(grad_hidden, w1[...], ((1,), (1,)))
        grad_mixed = cot.astype(F32) + norm_pull(upstream, gain, xhat, scale)
        mixed_grad_ref[...] = grad_mixed
        grad_branch = grad_mixed.astype(BF)
        branch[...] = grad_branch
        grad_attended = dot(grad_branch, wo[...], ((1,), (1,))).astype(BF)
        product = grad_attended.astype(F32) * attended.astype(F32)
        out_lane = lax.broadcasted_iota(jnp.int32, (tokens, LANES), 1)
        ids = x_ref[:, lat : lat + 1].astype(F32)
        stats = jnp.where(out_lane == 6 * HEADS, ids, 0.0)
        for head in range(HEADS):
            at, shift = head_window(head)
            mask = head_lanes(head)
            inner_sum = jnp.sum(
                jnp.where(mask, product[:, at : at + WINDOW], 0.0), axis=-1, keepdims=True
            )
            first_lane = at + shift
            log_column = log_total[:, first_lane : first_lane + 1]
            terms = split_three(log_column) + split_three(inner_sum)
            for index, term in enumerate(terms):
                stats = jnp.where(out_lane == index * HEADS + head, term, stats)
        stats = stats.astype(BF)
        for (first, some), ref in zip(cuts, message_refs):
            ref[:, :lat] = grad_attended[first : first + some]
            ref[:, lat:] = stats[first : first + some]

    flat_parts = [array for some in parts for array in some]
    return pl.pallas_call(
        kernel,
        in_specs=[scalar_spec()]
        + [whole_spec()] * (len(flat_parts) + 2)
        + [any_spec()] * (gain_count + count),
        out_specs=[whole_spec()] * (7 + len(cuts)),
        out_shape=[shape((tokens, lat)), shape((tokens, lat), F32)]
        + [shape((some, lat + LANES)) for _, some in cuts]
        + [
            shape((lat, tokens)),
            shape((tokens, lat)),
            shape((lat, tokens)),
            shape((tokens, lat)),
            shape((lat, tokens)),
        ],
        scratch_shapes=[pltpu.VMEM((lat, lat), BF)] * 3
        + [
            pltpu.VMEM((held_gain.blocks * GAIN_ROWS, LANES), BF),
            pltpu.SemaphoreType.DMA((6 * count,)),
            pltpu.SemaphoreType.DMA((2 * gain_count,)),
        ],
        compiler_params=params(0),
        cost_estimate=SMALL,
        name="feed",
    )(place, *flat_parts, latent_message, cot_flat, *held_gain.flat, *held.flat)


def feed_grads_call(place, lefts, rights, n, groups):
    lat, tokens = lefts[0].shape
    width = rights[0].shape[1]
    terms = len(lefts)

    def kernel(place_ref, *refs):
        left_refs, right_refs = refs[:terms], refs[terms : 2 * terms]
        for out, group in zip(refs[2 * terms :], groups):
            for number, distance in enumerate(group):
                at = pl.multiple_of(jnp.bitwise_xor(place_ref[0], distance) * n, 16)
                for index in range(terms):
                    chunk = left_refs[index][pl.ds(at, n), :]
                    first = (number * terms + index) * n
                    out[first : first + n, :] = dot(chunk, right_refs[index][...]).astype(BF)

    return pl.pallas_call(
        kernel,
        in_specs=[scalar_spec()] + [whole_spec()] * (2 * terms),
        out_specs=[whole_spec()] * len(groups),
        out_shape=[shape((len(group) * terms * n, width)) for group in groups],
        compiler_params=params(0),
        cost_estimate=SMALL,
        name="feed_grads",
    )(place, *lefts, *rights)


def attend_back_call(
    place, parts, queries, keys, values, byte_ids, held, groups, group, first, rows
):
    count_parts = len(parts)
    lat = keys.shape[1]
    block = byte_ids.shape[2]
    latents = groups * group
    count = len(held.flat)
    score_scale = 1.0 / math.sqrt(HEAD_DIM)

    def kernel(place_ref, *refs):
        refs = list(refs)
        take = lambda n: [refs.pop(0) for _ in range(n)]
        part_refs = take(count_parts)
        query_ref, key_ref, value_ref, bid_ref = take(4)
        piece_refs = take(count)
        grad_key_ref, grad_value_ref, grad_query_ref = take(3)
        up_refs = take(groups)
        wq, acc_q, acc_k, acc_v, sems = refs
        row = pl.program_id(0)

        def loads():
            return held.copies(("query",), piece_refs, (wq,), place_ref, sems)

        @pl.when(row == 0)
        def _():
            run_all(loads(), "start")

        message = jnp.concatenate(group_values(part_refs, place_ref), axis=0)
        stats = jnp.transpose(message[:, lat:].astype(F32), (1, 0))
        byte_ids = jnp.transpose(jnp.broadcast_to(bid_ref[0], (LANES, block)), (1, 0))[:, :1]
        allowed = byte_ids == stats[6 * HEADS : 6 * HEADS + 1, :]
        for head in range(HEADS):
            at, _ = head_window(head)
            mask = head_lanes(head)
            window = slice(at, at + WINDOW)
            stat = lambda k: stats[k * HEADS + head : k * HEADS + head + 1, :]
            log_total = stat(0) + stat(1) + stat(2)
            inner_sum = stat(3) + stat(4) + stat(5)
            query = jnp.where(mask, query_ref[:, window], jnp.zeros((), BF))
            grad = jnp.where(mask, message[:, window], jnp.zeros((), BF))
            key = key_ref[:, window]
            scores = dot(key, query, ((1,), (1,))) * score_scale
            probs = jnp.exp(jnp.where(allowed, scores - log_total, NEG_FILL))
            grad_probs = dot(value_ref[:, window], grad, ((1,), (1,)))
            grad_scores = (probs * (grad_probs - inner_sum)).astype(BF)
            found_k = dot(grad_scores, query)
            found_v = dot(probs.astype(BF), grad)
            found_q = dot(grad_scores, key, ((0,), (0,)))
            if head == 0:
                acc_k[:, window] = found_k
                acc_v[:, window] = found_v
                acc_q[:, window] = found_q
            else:
                acc_k[:, window] = jnp.where(mask, found_k, acc_k[:, window])
                acc_v[:, window] = jnp.where(mask, found_v, acc_v[:, window])
                acc_q[:, window] = jnp.where(mask, found_q, acc_q[:, window])

        grad_query = (acc_q[...] * score_scale).astype(BF)
        grad_key_ref[...] = (acc_k[...] * score_scale).astype(BF)
        grad_value_ref[...] = acc_v[...].astype(BF)
        grad_query_ref[...] = grad_query

        @pl.when(row == 0)
        def _():
            run_all(loads(), "wait")

        upstream = dot(grad_query, wq[...], ((1,), (1,))).astype(BF)
        for index, ref in enumerate(up_refs):
            ref[...] = upstream[index * group : (index + 1) * group, :]

    row_block = lambda i, p: (first + i, 0)
    own_block = lambda i, p: (i, 0)
    return pl.pallas_call(
        kernel,
        grid_spec=pltpu.PrefetchScalarGridSpec(
            num_scalar_prefetch=1,
            grid=(rows,),
            in_specs=[pl.BlockSpec((group, lat + LANES), own_block)] * count_parts
            + [
                pl.BlockSpec((latents, lat), own_block),
                pl.BlockSpec((block, lat), row_block),
                pl.BlockSpec((block, lat), row_block),
                pl.BlockSpec((1, 1, block), lambda i, p: (first + i, 0, 0)),
            ]
            + [any_spec()] * count,
            out_specs=[
                pl.BlockSpec((block, lat), own_block),
                pl.BlockSpec((block, lat), own_block),
                pl.BlockSpec((latents, lat), own_block),
            ]
            + [pl.BlockSpec((group, lat), own_block)] * groups,
            scratch_shapes=[
                pltpu.VMEM((lat, lat), BF),
                pltpu.VMEM((latents, lat), F32),
                pltpu.VMEM((block, lat), F32),
                pltpu.VMEM((block, lat), F32),
                pltpu.SemaphoreType.DMA((2 * count,)),
            ],
        ),
        out_shape=[shape((rows * block, lat))] * 2
        + [shape((rows * latents, lat))]
        + [shape((rows * group, lat))] * groups,
        compiler_params=params(1),
        cost_estimate=SMALL,
        name="attend_back",
    )(place, *parts, queries, keys, values, byte_ids, *held.flat)


def weight_grads_call(place, lefts, rights, some_rows, groups):
    lat = rights[0][0].shape[1]
    chunk = sum(some_rows)
    left_counts, counts = [len(parts) for parts in lefts], [len(parts) for parts in rights]

    def kernel(place_ref, *refs):
        refs = list(refs)
        take = lambda n: [refs.pop(0) for _ in range(n)]
        left_refs = [take(n) for n in left_counts]
        right_refs = [take(n) for n in counts]
        outs = take(len(groups))
        at = 0
        for index, (left, held) in enumerate(zip((0, 0, 1), refs)):
            factors, column, found = left_refs[left], 0, 0.0
            for part, right in enumerate(right_refs[index]):
                some = right.shape[0]
                if len(factors) > 1:
                    factor = factors[part][...]
                else:
                    factor = factors[0][:, column : column + some]
                found = found + dot(factor, right[...])
                column += some
            held[...] = found.astype(BF)
            some = some_rows[index]
            for out, group in zip(outs, groups):
                for number, distance in enumerate(group):
                    owner = jnp.bitwise_xor(place_ref[0], distance)
                    first = number * chunk + at
                    out[first : first + some, :] = held[
                        pl.ds(pl.multiple_of(owner * some, 16), some), :
                    ]
            at += some

    tile = lambda i, p: (0, i)
    flat_lefts = [left for parts in lefts for left in parts]
    flat_rights = [right for parts in rights for right in parts]
    return pl.pallas_call(
        kernel,
        grid_spec=pltpu.PrefetchScalarGridSpec(
            num_scalar_prefetch=1,
            grid=(lat // WINDOW,),
            in_specs=[full_block(left.shape) for left in flat_lefts]
            + [pl.BlockSpec((right.shape[0], WINDOW), tile) for right in flat_rights],
            out_specs=[pl.BlockSpec((len(group) * chunk, WINDOW), tile) for group in groups],
            scratch_shapes=[pltpu.VMEM((lefts[i][0].shape[0], WINDOW), BF) for i in (0, 0, 1)],
        ),
        out_shape=[shape((len(group) * chunk, lat)) for group in groups],
        compiler_params=params(1),
        cost_estimate=SMALL,
        name="weight_grads",
    )(place, *flat_lefts, *flat_rights)


def byte_grad_call(place, bytes_flat, grads, held, rows, cuts):
    tokens, width = bytes_flat.shape
    block = tokens // rows
    lat = grads[0][0].shape[1]
    count = len(held.flat)
    shards = place_shards(held)

    def kernel(place_ref, x_ref, *refs):
        grad_refs = refs[: 2 * len(cuts)]
        piece_refs = refs[2 * len(cuts) : 2 * len(cuts) + count]
        out_ref, wk, wv, gains, gain, sems = refs[2 * len(cuts) + count :]
        row = pl.program_id(0)

        def loads():
            return held.copies(
                ("gains", "key", "value"), piece_refs, (gains, wk, wv), place_ref, sems
            )

        @pl.when(row == 0)
        def _():
            run_all(loads(), "start")

        xhat, scale = standardize(x_ref[...].astype(F32))

        @pl.when(row == 0)
        def _():
            run_all(loads(), "wait")
            gain[...] = gain_vector(gains, width, held.lanes["byte"], shards)

        for index, (first, some) in enumerate(cuts):

            @pl.when((row >= first) & (row < first + some))
            def _():
                upstream = dot(grad_refs[2 * index][...], wk[...], ((1,), (1,))) + dot(
                    grad_refs[2 * index + 1][...], wv[...], ((1,), (1,))
                )
                out_ref[...] = norm_pull(upstream, gain[...], xhat, scale)

    row_block = lambda i, p: (i, 0)

    def cut_block(first, some):
        return lambda i, p: (jnp.clip(i - first, 0, some - 1), 0)

    return pl.pallas_call(
        kernel,
        grid_spec=pltpu.PrefetchScalarGridSpec(
            num_scalar_prefetch=1,
            grid=(rows,),
            in_specs=[pl.BlockSpec((block, width), row_block)]
            + [pl.BlockSpec((block, lat), cut_block(*cut)) for cut in cuts for _ in range(2)]
            + [any_spec()] * count,
            out_specs=pl.BlockSpec((block, width), row_block),
            scratch_shapes=[
                pltpu.VMEM((width, lat), BF),
                pltpu.VMEM((width, lat), BF),
                pltpu.VMEM((held.blocks * GAIN_ROWS, LANES), BF),
                pltpu.VMEM((1, width), F32),
                pltpu.SemaphoreType.DMA((6 * count,)),
            ],
        ),
        out_shape=shape((tokens, width), F32),
        compiler_params=params(1),
        cost_estimate=SMALL,
        name="byte_grad",
    )(place, bytes_flat, *[g for some in grads for g in some], *held.flat)


def latent_grad_call(place, latent_message, grad_mixed, ups, held):
    tokens, lat = grad_mixed.shape
    cuts, groups = len(ups), len(ups[0])
    count = len(held.flat)
    shards = place_shards(held)

    def kernel(place_ref, x_ref, mixed_ref, *refs):
        up_refs = [refs[i * groups : (i + 1) * groups] for i in range(cuts)]
        piece_refs = refs[cuts * groups : cuts * groups + count]
        out_ref, gains, sems = refs[cuts * groups + count :]
        loads = held.copies(("gains",), piece_refs, (gains,), place_ref, sems)
        run_all(loads, "start")
        xhat, scale = standardize(x_ref[:, :lat].astype(F32))
        upstream = jnp.concatenate(
            [
                functools.reduce(jnp.add, [ref[...].astype(F32) for ref in some])
                for some in up_refs
            ],
            axis=0,
        )
        run_all(loads, "wait")
        gain = gain_vector(gains, lat, held.lanes["latent"], shards)
        out_ref[...] = mixed_ref[...] + norm_pull(upstream, gain, xhat, scale)

    return pl.pallas_call(
        kernel,
        in_specs=[scalar_spec()]
        + [whole_spec()] * (2 + cuts * groups)
        + [any_spec()] * count,
        out_specs=whole_spec(),
        out_shape=shape((tokens, lat), F32),
        scratch_shapes=[
            pltpu.VMEM((held.blocks * GAIN_ROWS, LANES), BF),
            pltpu.SemaphoreType.DMA((2 * count,)),
        ],
        compiler_params=params(0, 24),
        cost_estimate=SMALL,
        name="latent_grad",
    )(place, latent_message, grad_mixed, *[u for some in ups for u in some], *held.flat)


def swap(value, axis, size, distance):
    return lax.ppermute(value, axis, [(i, i ^ distance) for i in range(size)])


def tie(value, *earlier):
    return lax.optimization_barrier((value, *earlier))[0]


def passed(value, *earlier, cost):
    def kernel(in_ref, out_ref):
        pass

    return pl.pallas_call(
        kernel,
        in_specs=[any_spec()],
        out_specs=any_spec(),
        out_shape=shape(value.shape, value.dtype),
        input_output_aliases={0: 0},
        cost_estimate=pl.CostEstimate(
            flops=int(cost * 1.1e9), bytes_accessed=1, transcendentals=0
        ),
        name="passed",
    )(tie(value, *earlier))


def swap_all(parts, size):
    return [swap(parts[j], "fsdp", size, j) for j in range(1, size)]


def by_index(parts, own, size):
    if len(parts) == 5:
        parts = parts[:3] + [jnp.where((own == 0) | (own == 3), parts[4], parts[3])]
    return [lax.select_n(jnp.bitwise_xor(own, k), *parts) for k in range(size)]


def build_block(place, own, parts, sizes, size):
    segments, first, at = [], 0, 0
    for rows in sizes:
        segments.append((first, rows, at))
        first += rows
        at += rows * size
    total = up_to(at, 16)
    if all(first % 8 == 0 for first, _, _ in segments):
        return assemble_call(place, parts, segments, total, size)
    shards = by_index(parts, own, size)
    found = [s[first : first + rows] for first, rows, _ in segments for s in shards]
    return pad_rows(jnp.concatenate(found, axis=0), total)


def add(*values):
    return functools.reduce(jnp.add, [v.astype(F32) for v in values]).astype(BF)


def meet_call(first, high, second, low, others, half):
    rows, lat = first.shape

    def kernel(a, h, c, l, o, one, two):
        def both(ref, start, stop, offset):
            return ref[start:stop, :].astype(F32) + o[
                offset + start : offset + stop, :
            ].astype(F32)

        one[:half, :] = both(a, 0, half, rows).astype(BF)
        one[half:, :] = (both(a, half, rows, rows) + h[...].astype(F32)).astype(BF)
        two[:half, :] = (both(c, 0, half, 0) + l[...].astype(F32)).astype(BF)
        two[half:, :] = both(c, half, rows, 0).astype(BF)

    return pl.pallas_call(
        kernel,
        in_specs=[whole_spec()] * 5,
        out_specs=[whole_spec()] * 2,
        out_shape=[shape((rows, lat))] * 2,
        compiler_params=params(0, 24),
        cost_estimate=SMALL,
        name="meet",
    )(first, high, second, low, others)


def cut_call(place, terms, sizes, size):
    lat = terms[0].shape[1]
    rows = sum(sizes)

    def kernel(place_ref, *refs):
        term_refs, outs, acc = refs[: len(terms)], refs[len(terms) : -1], refs[-1]
        total_rows = acc.shape[0]
        acc[...] = functools.reduce(
            jnp.add, [ref[ref.shape[0] - total_rows :, :].astype(F32) for ref in term_refs]
        )
        for distance, out in enumerate(outs):
            owner = jnp.bitwise_xor(place_ref[1], distance)
            found, at = [], 0
            for some in sizes:
                found.append(acc[pl.ds(pl.multiple_of(at + owner * some, 8), some), :])
                at += some * size
            out[...] = jnp.concatenate(found, axis=0).astype(out.dtype)

    return pl.pallas_call(
        kernel,
        in_specs=[scalar_spec()] + [whole_spec()] * len(terms),
        out_specs=[whole_spec()] * size,
        out_shape=[shape((rows, lat), F32)] + [shape((rows, lat))] * (size - 1),
        scratch_shapes=[pltpu.VMEM(terms[0].shape, F32)],
        compiler_params=params(0, 24),
        cost_estimate=SMALL,
        name="cut",
    )(place, *terms)


def cut_terms(place, own, terms, sizes, size):
    if all(some % 8 == 0 for some in sizes):
        return cut_call(place, terms, sizes, size)
    block = functools.reduce(jnp.add, [v.astype(F32) for v in terms])
    outs = []
    for distance in range(size):
        index = jnp.bitwise_xor(own, distance)
        found, at = [], 0
        for some in sizes:
            part = block[at : at + some * size].reshape(size, some, block.shape[1])
            found.append(lax.dynamic_index_in_dim(part, index, 0, keepdims=False))
            at += some * size
        value = jnp.concatenate(found, axis=0)
        outs.append(value if distance == 0 else value.astype(BF))
    return outs


def total(own, arrived):
    return functools.reduce(jnp.add, [v.astype(F32) for v in [own, *arrived]])


def split_rows(value, sizes):
    found, at = [], 0
    for some in sizes:
        found.append(value[at : at + some])
        at += some
    return found


def up_to(value, step):
    return -(-value // step) * step


def pad_rows(value, rows):
    return jnp.pad(value, ((0, rows - value.shape[0]), (0, 0)))


class Plan:
    def __init__(self, n_dp, n_f):
        self.n_dp, self.n_f = n_dp, n_f
        self.gate = ()

    def send(self, value, distance):
        return swap(tie(value, *self.gate), "dp", self.n_dp, distance)

    def pass_on(self, value, distance):
        return swap(tie(value, *self.gate), "fsdp", self.n_f, distance)

    def relay(self, own, two):
        middle = lax.ppermute(tie(own, *self.gate), "fsdp", [(1, 2), (2, 1)])
        return middle, lax.ppermute(tie(two, *self.gate), "fsdp", [(2, 3), (1, 0)])

    def spread(self, value):
        value = tie(value, *self.gate)
        middle = lax.ppermute(value, "fsdp", [(1, 2), (2, 1)])
        return middle, lax.ppermute(value, "fsdp", [(3, 2), (0, 1)])

    def tied(self, values):
        return [tie(values[0], *self.gate), *values[1:]]


def square_pieces(block, chips, half):
    rows = block.shape[0]
    full, halves = [(0, rows)], [(0, half), (half, rows)]
    pieces, flat = [], []
    for distance, parts, pairs in (
        (0, full, chips[:1]),
        (2, full, chips[1:2]),
        (4, full, chips[2:3]),
        (6, halves, chips[3:]),
    ):
        for core in range(2):
            pieces.append((distance + core, parts))
            flat.extend(pair[core] for pair in pairs)
    return pieces, flat


def local(n_dp, n_f, bytes_in, latents_in, cotangent, byte_segments, latent_segments,
          w_query, w_key, w_value, w_out, w_mlp_in, w_mlp_out,
          gain_latent, gain_byte, gain_mlp):
    rows, byte_local, width = bytes_in.shape
    _, group, lat = latents_in.shape
    dp, own = lax.axis_index("dp"), lax.axis_index("fsdp")
    place = jnp.stack([dp, own]).astype(jnp.int32)
    bytes_flat = bytes_in.reshape(rows * byte_local, width)
    latents_flat = latents_in.reshape(rows * group, lat)
    cot_flat = cotangent.reshape(rows * group, lat)
    kr, qr = w_key.shape[0], w_query.shape[0]
    key_rows, query_rows = n_f * kr, n_f * qr
    cuts = [(0, 1), (1, rows - 1)]
    cut_rows = [(first * group, some * group) for first, some in cuts]

    gains = jnp.concatenate([gain_latent, gain_byte, gain_mlp])
    gains = jnp.pad(gains, (0, lat - gains.shape[0]))[None, :]
    message_one = jnp.concatenate([w_key, w_value, w_query, gains], axis=0)
    message_one = pad_rows(message_one, up_to(2 * kr + qr + 1, 16))
    message_two = jnp.concatenate([w_out, w_mlp_in, w_mlp_out], axis=0)
    ids = latent_segments.reshape(rows * group, 1).astype(BF)
    ids = jnp.pad(ids, ((0, 0), (0, LANES - 1)))
    latent_message = jnp.concatenate([latents_flat, ids], axis=1)
    byte_ids = lax.dynamic_slice_in_dim(byte_segments, own * byte_local, byte_local, axis=1)
    byte_ids = byte_ids.astype(F32)
    byte_row = byte_ids[:, None, :]
    sizes_one, sizes_two = (kr, kr, qr), (qr, qr, qr)
    half_one, half_two = 2 * key_rows, up_to(3 * query_rows // 2, 16)
    spans_one = {
        "key": (0, key_rows),
        "value": (key_rows, key_rows),
        "query": (2 * key_rows, query_rows),
        "gains": (2 * key_rows + query_rows, GAIN_ROWS),
    }
    spans_two = {name: (i * query_rows, query_rows) for i, name in enumerate(("out", "inner", "outer"))}

    def held_one(pieces, flat):
        held = Held(pieces, flat, spans_one)
        held.blocks, held.size = n_dp, n_f
        held.lanes = {"latent": 0, "byte": qr, "mlp": qr + kr}
        return held

    def key_value(one, bytes_flat):
        return key_value_call(place, bytes_flat, one, rows)

    def attend(index, one, parts, keys, values):
        found = attend_call(
            place, parts, byte_row, keys, values, one, n_f, group, *cuts[index]
        )
        return found[0], found[1], found[2:]

    def feed(one, two, attended):
        return feed_call(place, attended, latent_message, cot_flat, one, two, cut_rows)

    def feed_grads(lefts, rights, groups):
        return feed_grads_call(place, lefts, rights, query_rows, groups)

    def attend_back(index, one, parts, saved):
        return attend_back_call(
            place, parts, *saved, byte_row, one, n_f, group, *cuts[index]
        )

    def weight_grads(lefts, first, last, groups):
        some = (key_rows, key_rows, query_rows)
        return weight_grads_call(place, lefts, list(zip(first, last)), some, groups)

    def byte_grad(one, grads):
        return byte_grad_call(place, bytes_flat, grads, one, rows, cuts)

    run = square if (n_dp, n_f) == (8, 4) else plain
    new, grad_latents, grad_bytes, grad_one, grad_two = run(**locals())

    def gain_grad(pairs, gain):
        found = sum(jnp.sum(w.astype(F32) * g, axis=1) for w, g in pairs)
        return found / gain.astype(F32)

    grad_key, grad_value, grad_query = split_rows(grad_one, sizes_one)
    grad_out, grad_inner, grad_outer = split_rows(grad_two, sizes_two)
    return (
        new.reshape(rows, group, lat),
        grad_latents.reshape(rows, group, lat),
        grad_bytes.reshape(rows, byte_local, width),
        grad_query,
        grad_key,
        grad_value,
        grad_out,
        grad_inner,
        grad_outer,
        gain_grad([(w_query, grad_query)], gain_latent),
        gain_grad([(w_key, grad_key), (w_value, grad_value)], gain_byte),
        gain_grad([(w_mlp_in, grad_inner)], gain_mlp),
    )


def plain(*, n_dp, n_f, place, own, bytes_flat, message_one, message_two, latent_message,
          sizes_one, sizes_two, spans_two, cot_flat, held_one, key_value, attend, feed,
          feed_grads, attend_back, weight_grads, byte_grad, **_):
    def gather(message, sizes):
        parts = [message, *swap_all([message] * n_f, n_f)]
        block = build_block(place, own, parts, sizes, n_f)
        flat = [block] + [swap(block, "dp", n_dp, d) for d in range(1, n_dp)]
        return [(d, [(0, block.shape[0])]) for d in range(n_dp)], flat

    def scatter(parts, sizes):
        terms = [parts[0]] + [swap(parts[d], "dp", n_dp, d) for d in range(1, n_dp)]
        cut = cut_terms(place, own, terms, sizes, n_f)
        return total(cut[0], swap_all(cut, n_f))

    one = held_one(*gather(message_one, (*sizes_one, 1)))
    two = Held(*gather(message_two, sizes_two), spans_two)
    byte_t, keys, values = key_value(one, bytes_flat)
    latent_parts = [latent_message, *swap_all([latent_message] * n_f, n_f)]
    latent_t, queries, found = zip(*[attend(i, one, latent_parts, keys, values) for i in range(2)])
    attended = list(zip(*[[f[0], *swap_all(f, n_f)] for f in found]))
    new, grad_mixed, *messages, attended_t, branch, normed_t, inner, act_t = feed(
        one, two, attended
    )
    each = [(d,) for d in range(n_dp)]
    grads = feed_grads((attended_t, normed_t, act_t), (branch, inner, cot_flat), each)
    grad_two = scatter(grads, sizes_two)
    parts = [[m, *swap_all([m] * n_f, n_f)] for m in messages]
    first, last = [attend_back(i, one, parts[i], (queries[i], keys, values)) for i in range(2)]
    grad_bytes = byte_grad(one, (first[:2], last[:2]))
    grad_one = scatter(
        weight_grads(((byte_t,), latent_t), first[:3], last[:3], each), sizes_one
    )
    ups = [[ups[0], *swap_all(ups, n_f)] for ups in (first[3:], last[3:])]
    grad_latents = latent_grad_call(place, latent_message, grad_mixed, ups, one)
    return new, grad_latents, grad_bytes, grad_one, grad_two


def square(*, n_dp, n_f, place, own, bytes_flat, message_one, message_two, latent_message,
           sizes_one, sizes_two, spans_two, half_one, half_two, cot_flat, held_one, key_value,
           attend, feed, feed_grads, attend_back, weight_grads, byte_grad, **_):
    plan = Plan(n_dp, n_f)
    send, pass_on = plan.send, plan.pass_on

    near = [pass_on(message_one, 2), pass_on(message_one, 1)]
    plan.gate = near
    parts = [message_one, near[1], near[0], *plan.relay(message_one, near[0])]
    block = build_block(place, own, parts, (*sizes_one, 1), n_f)
    plan.gate = [block]
    x, y, other = send(block, 2), send(block, 4), send(block, 1)
    latent_two, latent_one = pass_on(latent_message, 2), pass_on(latent_message, 1)
    plan.gate = [x, y]
    low, high = send(x[:half_one], 4), send(y[half_one:], 2)
    latent_two = passed(latent_two, latent_one, cost=12)
    plan.gate = [x, y, latent_two]
    latent_parts = [
        latent_message, latent_one, latent_two, *plan.relay(latent_message, latent_two)
    ]
    plan.gate = [low, high, other]
    others = [send(v, 1) for v in (x, y, low, high)]
    pairs = list(zip((block, x, y, low, high), (other, *others)))
    one = held_one(*square_pieces(block, pairs, half_one))
    plan.gate = [low, high, latent_two]
    two_two, two_one = pass_on(message_two, 2), pass_on(message_two, 1)
    plan.gate = others
    byte_t, keys, values = key_value(one, tie(bytes_flat, *plan.gate))
    plan.gate = [two_two, two_one, keys]
    parts = [message_two, two_one, two_two, *plan.relay(message_two, two_two)]
    latent_t_first, queries_first, found = attend(0, one, plan.tied(latent_parts), keys, values)
    plan.gate = [queries_first, *parts[3:]]
    block = build_block(place, own, plan.tied(parts), sizes_two, n_f)
    x, y = send(block, 2), send(block, 4)
    attended_first = [found[0], *[pass_on(found[j], j) for j in range(1, n_f)]]
    plan.gate = [block]
    latent_t_last, queries_last, found = attend(1, one, plan.tied(latent_parts), keys, values)
    plan.gate = attended_first[1:]
    attended_last = [found[0], *[pass_on(found[j], j) for j in range(1, n_f)]]
    plan.gate = [x, y, queries_last, *attended_first[1:]]
    low, high = send(x[:half_two], 4), send(y[half_two:], 2)
    attended_last[1] = passed(attended_last[1], *attended_last[2:], cost=4)
    plan.gate = [low, high, *attended_last[1:]]
    pairs = [(v, send(v, 1)) for v in (block, x, y, low, high)]
    two = Held(*square_pieces(block, pairs, half_two), spans_two)
    new, grad_mixed, first, last, attended_t, branch, normed_t, inner, act_t = feed(
        one, two, list(zip(attended_first, attended_last))
    )
    groups = [(0,), (2,), (4,), (6,), (7,), (5, 3, 1)]
    plan.gate = []
    near = [pass_on(first, 2), pass_on(first, 1)]
    grads = feed_grads((attended_t, normed_t, act_t), (branch, inner, cot_flat), groups)
    plan.gate = near
    first_parts = [first, near[1], near[0], *plan.relay(first, near[0])]
    near = [pass_on(last, 2), pass_on(last, 1)]
    crossing = send(grads[4], 1)
    low = add(grads[3][:half_two], crossing[:half_two])
    high = add(grads[3][half_two:], crossing[half_two:])
    plan.gate = [crossing, *first_parts[3:]]
    low, high = send(low, 2), send(high, 4)
    others = send(grads[5], 1)
    back_first = attend_back(0, one, plan.tied(first_parts), (queries_first, keys, values))
    near[0] = passed(near[0], near[1], back_first[0], cost=5)
    plan.gate = [low, high, others, *near, back_first[0]]
    last_parts = [last, near[1], near[0], *plan.relay(last, near[0])]
    x, y = meet_call(grads[1], tie(high, *plan.gate), grads[2], low, others, half_two)
    plan.gate = [x, y, *last_parts[3:]]
    terms_two = [grads[0], others, send(x, 2), send(y, 4)]
    ups_first = back_first[3:]
    ups_first = [ups_first[0], *[pass_on(ups_first[j], j) for j in range(1, n_f)]]
    back_last = attend_back(1, one, plan.tied(last_parts), (queries_last, keys, values))
    plan.gate = [back_last[0], *ups_first[1:]]
    ups = back_last[3:]
    near = [pass_on(ups[1], 1), *plan.spread(ups[3])]
    grads = weight_grads(
        ((byte_t,), (latent_t_first, latent_t_last)),
        back_first[:3],
        [tie(back_last[0], *plan.gate), *back_last[1:3]],
        groups,
    )
    plan.gate = [*near, grads[0], *terms_two[2:]]
    crossing = send(grads[4], 1)
    others = send(tie(grads[5], crossing), 1)
    low = add(grads[3][:half_one], crossing[:half_one])
    high = add(grads[3][half_one:], crossing[half_one:])
    merged = add(tie(ups[2], *plan.gate), near[2])
    plan.gate = [low, high, merged]
    low, high = send(low, 2), send(high, 4)
    ups_last = [ups[0], *near[:2], pass_on(merged, 2)]
    cut_two = cut_terms(place, own, plan.tied(terms_two), sizes_two, n_f)
    plan.gate = [low, high, cut_two[0], others]
    x, y = meet_call(grads[1], tie(high, *plan.gate), grads[2], low, others, half_one)
    plan.gate = [x, y, ups_last[-1]]
    arrived_two = [pass_on(cut_two[j], j) for j in range(1, n_f)]
    plan.gate = [x, y]
    terms_one = [grads[0], others, send(x, 2), send(y, 4)]
    grad_bytes = byte_grad(one, (plan.tied(back_first[:2]), back_last[:2]))
    plan.gate = [*terms_one[2:], grad_bytes]
    cut_one = cut_terms(place, own, plan.tied(terms_one), sizes_one, n_f)
    plan.gate = [cut_one[0]]
    grad_one = total(cut_one[0], [pass_on(cut_one[j], j) for j in range(1, n_f)])
    grad_two = total(cut_two[0], arrived_two)
    grad_latents = latent_grad_call(
        place, latent_message, tie(grad_mixed, *plan.gate), [ups_first, ups_last], one
    )
    return new, grad_latents, grad_bytes, grad_one, grad_two


def solution(mesh):
    rows3 = P("dp", "fsdp", None)
    split2 = P(("dp", "fsdp"), None)
    split1 = P(("dp", "fsdp"))
    in_specs = (rows3,) * 3 + (P("dp", None), P("dp", "fsdp")) + (split2,) * 6 + (split1,) * 3
    out_specs = (rows3,) * 3 + (split2,) * 6 + (split1,) * 3
    body = functools.partial(local, mesh.shape["dp"], mesh.shape["fsdp"])
    return jax.shard_map(
        body, mesh=mesh, in_specs=in_specs, out_specs=out_specs, check_vma=False
    )
```
